32 devices in a mesh: kern: 4 (over x, core), slab: 8 (over z, y).
Axes of the slice: x: 2, y: 2, z: 4, core: 2. Of those that a mesh axis runs over, the one named last changes fastest.
Arguments:
- mask_params: float32 [2048, 2048], P('slab', 'kern'), may hold values from -6 to 6
- target_bits: int32 [2048, 2048], P('slab'), may hold values 0 or 1
- kernels: float32 [4, 2, 512, 512], P('kern', None, None, 'slab'), may hold values from -38.183765 to 38.183765
- weights: float32 [4], P('kern'), may hold values from 0.1 to 0.5
- dose_factors: float32 [2], replicated, may hold values from 0.25 to 1.75
Outputs:
- new_params: float32 [2048, 2048], P('slab', 'kern')
- resist_image: float32 [2, 2, 2048, 2048], P(None, None, 'slab', 'kern')
The draws below stay inside these ranges and needn't reach their ends.
All inputs are finite; a program needn't handle non-finite values. No bound on the sum of `target_bits` on one device may be relied on, other than what follows from the above.
Results may differ from the reference program's by a relative error of at most 0.035.
Values may be sent and summed in bfloat16 or wider, within the bound.
No kernel may reach another device: no remote copies, remote signals or barrier semaphores. Data moves between devices by JAX's collectives and lax.ppermute only.
A program may use at most 128 MiB of HBM per device.

```python
import math
import jax
import jax.numpy as jnp
from jax import lax

N = 2048
F = 512
FOCI = 2
DOSES = 2
STEPS = 2
KERNELS = 4


def with_ends(result, stream_key, smallest, top_value):
    dims = result.shape
    spot = [jax.random.randint(jax.random.fold_in(stream_key, axis), (), 0, dims[axis]) for axis in range(len(dims))]
    result = result.at[tuple(spot)].set(smallest)
    longest = dims.index(max(dims))
    spot[longest] = (spot[longest] + 1) % dims[longest]
    return result.at[tuple(spot)].set(top_value)


def level_of(own_key, shape, pieces, smallest, high):
    def one(axis_at, parts):
        draws = jax.random.uniform(jax.random.fold_in(jax.random.fold_in(own_key, 6), axis_at), (parts,), jnp.float32, smallest / len(pieces), high / len(pieces))
        return jnp.repeat(jnp.exp(draws), shape[axis_at] // parts).reshape((-1,) + (1,) * (len(shape) - axis_at - 1))

    loudness = one(*pieces[0])
    for cut in pieces[1:]:
        loudness = loudness * one(*cut)
    return loudness


def centred(key, extent, deviation, limit, shards=(), kind=jnp.bfloat16):
    loudness = level_of(key, extent, shards, -0.22, 0.18) if shards else 1.0
    result = jax.random.normal(key, extent, jnp.float32) * deviation * loudness
    return jnp.minimum(jnp.maximum(result, -limit), limit).astype(kind)


def setup_inputs(seed: int = 0) -> dict:
    keys = jax.random.split(jax.random.key(seed), 6)
    return {
        "mask_params": centred(keys[0], (N, N), 1.0, 6.0, ((0, 8), (1, 4)), jnp.float32),
        "target_bits": with_ends((jax.random.randint(keys[1], (N, N), 0, 2) < 1).astype(jnp.int32), jax.random.fold_in(keys[1], 1), 0, 1),
        "kernels": centred(keys[2], (KERNELS, 2, F, F), (2.25 * (N // F) * (KERNELS // FOCI) ** -0.5), 38.183765, ((0, 4), (3, 8)), jnp.float32),
        "weights": jnp.clip(jnp.exp(math.log(0.5) - 1.609438 * jax.random.uniform(keys[3], (KERNELS,), jnp.float32) ** level_of(keys[3], (KERNELS,), ((0, 4),), -0.2, 0.2)), 0.1, 0.5),
        "dose_factors": jnp.clip(1.0 + 0.15 * jax.random.normal(keys[4], (DOSES,), jnp.float32), 0.25, 1.75),
    }


steepness = 3.0
threshold = 1.0
step_rate = 0.4

def times_transposed(left, right):
    return lax.dot_general(left, right, (((1,), (1,)), ((), ())), preferred_element_type=jnp.float32)

def transposed_times(left, right):
    return lax.dot_general(left, right, (((0,), (0,)), ((), ())), preferred_element_type=jnp.float32)

def plain_product(left, right):
    return jnp.dot(left, right, preferred_element_type=jnp.float32)

def tables():
    freqs = jnp.arange(F, dtype=jnp.int32) - F // 2
    pixels = jnp.arange(N, dtype=jnp.int32)
    phases = freqs[:, None] * pixels[None, :] % N
    angles = phases.astype(jnp.float32) * (2.0 * math.pi / N)
    scale = 1.0 / math.sqrt(N)
    return ((jnp.cos(angles) * scale).astype(jnp.bfloat16), (jnp.sin(angles) * scale).astype(jnp.bfloat16))

def resist(intensity, dose_factors, target_float):
    dose_grid = dose_factors[None, :, None, None]
    printed = jax.nn.sigmoid(steepness * (dose_grid * intensity[:, None] - threshold))
    errors = (printed - target_float) * printed * (1.0 - printed) * steepness * dose_grid
    return (printed, lax.optimization_barrier(jnp.sum(errors, axis=1)))

def reference(mask_params, target_bits, kernels, weights, dose_factors):
    cosine_table, sine_table = tables()
    stacked_table = jnp.concatenate([cosine_table, sine_table], axis=0)
    target_float = target_bits.astype(jnp.float32)
    foci_ids = jnp.arange(FOCI, dtype=jnp.int32)
    focus_index = jnp.arange(KERNELS, dtype=jnp.int32) % FOCI
    params = mask_params
    printed = None
    for iteration in range(STEPS):
        mask_values = jnp.tanh(params)
        mask_low = mask_values.astype(jnp.bfloat16)
        column_spec = times_transposed(mask_low, stacked_table)
        spec_in_real = column_spec[:, :F].astype(jnp.bfloat16)
        spec_in_imag = (-column_spec[:, F:]).astype(jnp.bfloat16)
        spec_real = plain_product(cosine_table, spec_in_real) + plain_product(sine_table, spec_in_imag)
        spec_imag = plain_product(cosine_table, spec_in_imag) - plain_product(sine_table, spec_in_real)

        def make_field(kernel_pair):
            filt_real = (kernel_pair[0] * spec_real - kernel_pair[1] * spec_imag).astype(jnp.bfloat16)
            filt_imag = (kernel_pair[0] * spec_imag + kernel_pair[1] * spec_real).astype(jnp.bfloat16)
            inv_real = (transposed_times(cosine_table, filt_real) - transposed_times(sine_table, filt_imag)).astype(jnp.bfloat16)
            inv_imag = (transposed_times(cosine_table, filt_imag) + transposed_times(sine_table, filt_real)).astype(jnp.bfloat16)
            field_real = plain_product(inv_real, cosine_table) - plain_product(inv_imag, sine_table)
            field_imag = plain_product(inv_real, sine_table) + plain_product(inv_imag, cosine_table)
            return (field_real, field_imag)

        def add_light(total, inputs):
            kernel_pair, kernel_weight, kernel_focus = inputs
            field_real, field_imag = make_field(kernel_pair)
            selector = (foci_ids == kernel_focus).astype(jnp.float32)
            power = kernel_weight * (field_real * field_real + field_imag * field_imag)
            return (total + selector[:, None, None] * power[None], None)
        intensity, unused = lax.scan(add_light, jnp.zeros((FOCI, N, N), jnp.float32), (kernels, weights, focus_index))
        printed, sens = resist(intensity, dose_factors, target_float)

        def add_grad(total, inputs):
            kernel_pair, kernel_weight, kernel_focus = inputs
            field_real, field_imag = make_field(kernel_pair)
            selector = (foci_ids == kernel_focus).astype(jnp.float32)
            kernel_sens = lax.optimization_barrier(jnp.sum(selector[:, None, None] * sens, axis=0))
            cot_real = (2.0 * kernel_weight * kernel_sens * field_real).astype(jnp.bfloat16)
            cot_imag = (2.0 * kernel_weight * kernel_sens * field_imag).astype(jnp.bfloat16)
            back_real = (times_transposed(cot_real, cosine_table) + times_transposed(cot_imag, sine_table)).astype(jnp.bfloat16)
            back_imag = (times_transposed(cot_imag, cosine_table) - times_transposed(cot_real, sine_table)).astype(jnp.bfloat16)
            grad_real = plain_product(cosine_table, back_real) + plain_product(sine_table, back_imag)
            grad_imag = plain_product(cosine_table, back_imag) - plain_product(sine_table, back_real)
            dspec_real = (kernel_pair[0] * grad_real + kernel_pair[1] * grad_imag).astype(jnp.bfloat16)
            dspec_imag = (kernel_pair[0] * grad_imag - kernel_pair[1] * grad_real).astype(jnp.bfloat16)
            adj_real = (transposed_times(cosine_table, dspec_real) - transposed_times(sine_table, dspec_imag)).astype(jnp.bfloat16)
            adj_imag = (transposed_times(sine_table, dspec_real) + transposed_times(cosine_table, dspec_imag)).astype(jnp.bfloat16)
            return (total + plain_product(adj_real, cosine_table) - plain_product(adj_imag, sine_table), None)
        mask_grad, unused = lax.scan(add_grad, jnp.zeros((N, N), jnp.float32), (kernels, weights, focus_index))
        params = params - step_rate * mask_grad * (1.0 - mask_values * mask_values)
    return (params, printed)
```

```python
import functools

import jax
import jax.numpy as jnp
import numpy as np
from jax import lax
from jax.experimental import pallas as pl
from jax.experimental.pallas import tpu as pltpu
from jax.sharding import PartitionSpec as P

FOCI = 2
STEPS = 2
STEEPNESS = 3.0
THRESHOLD = 1.0
STEP_RATE = 0.4
BLOCK = 16
EXTRA = 128
SPREAD = 64
VMEM_LIMIT = 50 * 1024 * 1024
FLOAT = jnp.float32
HALF = jnp.bfloat16
AXES = ("kern", "slab")


def plain(left, right):
    return jnp.dot(left, right, preferred_element_type=FLOAT)


def trig_tables(pixels, freqs):
    phases = ((np.arange(freqs) - freqs // 2)[:, None] * np.arange(pixels)[None, :]) % pixels
    angles = phases.astype(np.float32) * np.float32(2.0 * np.pi / pixels)
    scale = np.float32(1.0 / np.sqrt(pixels))
    cosine = (np.cos(angles.astype(np.float64)).astype(np.float32) * scale).astype(HALF)
    sine = (np.sin(angles.astype(np.float64)).astype(np.float32) * scale).astype(HALF)
    return np.stack([cosine.astype(np.float32), sine.astype(np.float32)])


def row_blocks(tables, parts):
    _, freqs, pixels = tables.shape
    split = tables.transpose(0, 2, 1).reshape(2, parts, pixels // parts, freqs)
    return np.ascontiguousarray(split.transpose(1, 0, 2, 3))


def col_blocks(tables, parts):
    _, freqs, pixels = tables.shape
    split = tables.reshape(2, freqs, parts, pixels // parts)
    return np.ascontiguousarray(split.transpose(2, 0, 1, 3))


def flat_index(kern, slab, sizes):
    return kern * sizes["slab"] + slab


def plan_rounds(sizes):
    kern_bits = [("kern", bit) for bit in range(1, sizes["kern"].bit_length() - 1)]
    slab_bits = [("slab", bit) for bit in range(sizes["slab"].bit_length() - 1)]
    rounds = [kern_bits[:1] + slab_bits[:1], slab_bits[1:3], kern_bits[1:3], slab_bits[3:]]
    return [bits for bits in rounds if bits]


def partner(values, bits, place, sizes):
    shift = {"kern": 0, "slab": 0}
    for i, (axis, bit) in enumerate(bits):
        if (place >> (len(bits) - 1 - i)) & 1:
            shift[axis] |= 1 << bit
    mask = flat_index(shift["kern"], shift["slab"], sizes)
    total = sizes["kern"] * sizes["slab"]
    return lax.ppermute(values, AXES, [(i, i ^ mask) for i in range(total)])


def add_all(pieces):
    total = pieces[0].astype(FLOAT)
    for piece in pieces[1:]:
        total = total + piece.astype(FLOAT)
    return total.astype(HALF)


def tied(values, others):
    return lax.optimization_barrier((values, others))


def reduce_all(parts, rounds, sizes, early=None, late=None):
    core = [("kern", 0)]
    count = len(parts) // 2
    parts = [add_all([mine, partner(other, core, 1, sizes)]) for mine, other in zip(parts[:count], parts[count:])]
    others = [partner(parts[p], rounds[0], p, sizes) for p in range(1, count)]
    if early is not None:
        others, early = tied(others, early)
    total = add_all([parts[0]] + others)
    for bits in rounds[1:]:
        others = [partner(total, bits, p, sizes) for p in range(1, 1 << len(bits))]
        if late is not None and bits is rounds[1]:
            others, late = tied(others, late)
        total = add_all([total] + others)
    pieces = [total] + [partner(total, rounds[0], p, sizes) for p in range(1, count)]
    return pieces + [partner(piece, core, 1, sizes) for piece in pieces], early, late


def start_all(copies, sems):
    started = [pltpu.make_async_copy(source, target, sems.at[i]) for i, (source, target) in enumerate(copies)]
    for copy in started:
        copy.start()
    return started


def piece_copies(pieces, spec, me):
    size = pieces[0].shape[0]
    return [
        (piece, spec.at[pl.ds(pl.multiple_of((place ^ me) * size, size), size)]) for place, piece in enumerate(pieces)
    ]


def iotas(rows, cols):
    shape = (rows, cols)
    return lax.broadcasted_iota(jnp.int32, shape, 0), lax.broadcasted_iota(jnp.int32, shape, 1)


def ones_where(condition):
    return jnp.where(condition, 1.0, 0.0).astype(HALF)


def anti_diagonal(size, total):
    row, lane = iotas(size, size)
    return ones_where(row + lane == total)


def spread_row(line):
    width = line.shape[1]
    row, lane = iotas(width // SPREAD, width)
    masked = jnp.where(lane // SPREAD == row, line, 0.0).astype(HALF)
    row, lane = iotas(width, EXTRA)
    return plain(masked, ones_where(lane == row % SPREAD + SPREAD))


def collect_rows(extra, width):
    row, lane = iotas(EXTRA, width)
    wide = plain(extra, ones_where(row == lane % SPREAD + SPREAD))
    row, lane = iotas(extra.shape[0], width)
    return jnp.where(lane // SPREAD == row, wide, 0.0)


def write_blocks(source, outs, me):
    for place, out in enumerate(outs):
        size = out.shape[0]
        out[...] = source[pl.ds(pl.multiple_of((place ^ me) * size, size), size)].astype(HALF)


def spectrum_of(mask_low, rows_t, cols_ref, col_spec, total):
    cols, rows = mask_low.shape
    half = total.shape[0]
    width = 4 * half
    col_spec[:, :rows] = plain(cols_ref[half:, :cols], mask_low).astype(HALF)
    col_spec[:, rows:] = (-plain(cols_ref[half:, cols:], mask_low)).astype(HALF)
    edge_re = plain(cols_ref[:BLOCK, :cols], mask_low).astype(HALF)
    edge_im = (-plain(cols_ref[:BLOCK, cols:], mask_low)).astype(HALF)
    edge = plain(edge_re, rows_t[:rows, :width]) + plain(edge_im, rows_t[rows:, :width])
    total[:, :width] = plain(col_spec[...], rows_t[:, :width]).astype(HALF)
    extra = plain(col_spec[...], rows_t[:, width:])
    spread = spread_row(edge[:1])
    count = spread.shape[0]
    total[:count, width:] = (extra[:count] + spread).astype(HALF)
    total[count:, width:] = extra[count:].astype(HALF)


def fill_rows_t(raw, rows_t):
    rows, freqs = raw.shape[1:]
    rows_t[:rows, :freqs] = raw[0].astype(HALF)
    rows_t[:rows, freqs : 2 * freqs] = (-raw[1]).astype(HALF)
    rows_t[rows:, :freqs] = raw[1].astype(HALF)
    rows_t[rows:, freqs : 2 * freqs] = raw[0].astype(HALF)
    lane = iotas(rows, EXTRA)[1]
    cosine, sine = raw[0, :, :1], -raw[1, :, :1]
    zero = jnp.zeros((rows, EXTRA), FLOAT)
    rows_t[:rows, 2 * freqs :] = jnp.where(lane == 0, cosine, jnp.where(lane == 1, -sine, zero)).astype(HALF)
    rows_t[rows:, 2 * freqs :] = jnp.where(lane == 0, sine, jnp.where(lane == 1, cosine, zero)).astype(HALF)


def first_kernel(index_ref, params_ref, rows_all, cols_all, *rest):
    outs, scratch = rest[:-7], rest[-7:]
    raw_rows, raw_cols, rows_t, cols_ref, col_spec, total, sems = scratch
    slab, pair, core, me = (index_ref[i] for i in range(4))
    cols = params_ref.shape[1]
    own = pl.ds(pl.multiple_of(core * cols, cols), cols)
    waits = start_all([(cols_all.at[pair, :, :, own], raw_cols), (rows_all.at[slab], raw_rows)], sems)
    mask_low = jnp.tanh(params_ref[...]).T.astype(HALF)
    waits[0].wait()
    cols_ref[:, :cols] = raw_cols[0].astype(HALF)
    cols_ref[:, cols:] = raw_cols[1].astype(HALF)
    waits[1].wait()
    fill_rows_t(raw_rows, rows_t)
    spectrum_of(mask_low, rows_t, cols_ref, col_spec, total)
    write_blocks(total, outs, me)


def table_kernel(index_ref, rows_all, cols_all, target_all, *rest):
    rows_n, rows_t, cols_n, cols_t, target_ref, raw_rows, raw_cols, raw_target, sems = rest
    slab, pair = index_ref[0], index_ref[1]
    rows, freqs = raw_rows.shape[1:]
    wide = raw_cols.shape[2]
    here = pl.ds(pl.multiple_of(pair * wide, wide), wide)
    waits = start_all(
        [(rows_all.at[slab], raw_rows), (cols_all.at[pair], raw_cols), (target_all.at[:, here], raw_target)], sems
    )
    waits[0].wait()
    fill_rows_t(raw_rows, rows_t)
    cosine, sine = raw_rows[0].T, raw_rows[1].T
    rows_n[:freqs, :rows] = cosine.astype(HALF)
    rows_n[:freqs, rows:] = sine.astype(HALF)
    rows_n[freqs : 2 * freqs, :rows] = (-sine).astype(HALF)
    rows_n[freqs : 2 * freqs, rows:] = cosine.astype(HALF)
    line = iotas(EXTRA, rows)[0]
    first, second = cosine[:1], -sine[:1]
    zero = jnp.zeros((EXTRA, rows), FLOAT)
    rows_n[2 * freqs :, :rows] = jnp.where(line == 0, first, jnp.where(line == 1, -second, zero)).astype(HALF)
    rows_n[2 * freqs :, rows:] = jnp.where(line == 0, second, jnp.where(line == 1, first, zero)).astype(HALF)
    waits[1].wait()
    for part in range(2):
        cols_n[:, part * wide : (part + 1) * wide] = raw_cols[part].astype(HALF)
        for start in range(0, wide, 128):
            some = raw_cols[part, :, start : start + 128].T
            cols_t[start : start + 128, part * freqs : (part + 1) * freqs] = some.astype(HALF)
    waits[2].wait()
    for start in range(0, wide, 128):
        target_ref[start : start + 128] = (2 * raw_target[:, start : start + 128] - 1).astype(FLOAT).T


def update_kernel(first, last, count, index_ref, params_ref, rows_n, rows_t, cols_n, cols_t, *rest):
    pieces, rest = rest[:count], rest[count:]
    if last:
        new_ref, rows_v, cols_v, spec, back, sems = rest
    else:
        new_ref, outs, scratch = rest[0], rest[1 : 1 + count], rest[1 + count :]
        rows_v, rows_t_v, cols_v, cols_n_v, spec, back, col_spec, sems = scratch
    core, me = index_ref[2], index_ref[3]
    params = params_ref[...].T if first else params_ref[...]
    cols, rows = params.shape
    half = spec.shape[0]
    freqs = 2 * half
    here = pl.ds(pl.multiple_of(core * cols, cols), cols)
    copies = piece_copies(pieces, spec, me) + [(rows_n, rows_v), (cols_t.at[here], cols_v)]
    if not last:
        wide = cols_n.shape[1] // 2
        copies += [
            (rows_t, rows_t_v),
            (cols_n.at[:, here], cols_n_v.at[:, :cols]),
            (cols_n.at[:, pl.ds(pl.multiple_of(wide + core * cols, cols), cols)], cols_n_v.at[:, cols:]),
        ]
    waits = start_all(copies, sems)
    back[...] = jnp.zeros_like(back)
    for i in range(count + 1):
        waits[i].wait()
    result = plain(spec[...], rows_v[...])
    back[half:freqs] = result[:, :rows].astype(HALF)
    back[freqs + half :] = (-result[:, rows:]).astype(HALF)
    edge = collect_rows(spec[: 2 * freqs // SPREAD, 2 * freqs :], 2 * freqs).astype(HALF)
    edge = jnp.sum(plain(edge, rows_v[: 2 * freqs]), axis=0, keepdims=True)
    line = iotas(BLOCK, rows)[0]
    back[:BLOCK] = jnp.where(line == 0, edge[:, :rows], 0.0).astype(HALF)
    back[freqs : freqs + BLOCK] = jnp.where(line == 0, -edge[:, rows:], 0.0).astype(HALF)
    waits[count + 1].wait()
    gradient = plain(cols_v[...], back[...])
    mask = jnp.tanh(params)
    params = params - STEP_RATE * gradient * (1.0 - mask * mask)
    if last:
        new_ref[...] = params.T
    else:
        new_ref[...] = params
        for i in range(count + 2, len(waits)):
            waits[i].wait()
        spectrum_of(jnp.tanh(params).astype(HALF), rows_t_v, cols_n_v, col_spec, spec)
        write_blocks(spec, outs, me)


def loop(count, step):
    if count <= 2:
        for i in range(count):
            step(i)
    else:
        pl.loop(0, count)(step)


def image_kernel(last, parts, order, index_ref, dose_ref, rows_n, rows_t, cols_n, cols_t, target_all, *rest):
    spec_pieces, rest = rest[:parts], rest[parts:]
    outs = rest[-16 - parts - (2 if last else 0) : -16]
    spectra = rest[: -16 - len(outs)]
    scratch = rest[-16:]
    rows_v, rows_t_v, cols_v, cols_t_v, target_ref, kern_ref, spec = scratch[:7]
    filtered, sides, fields, cotangent, back, total, half_spec, turned, sems = scratch[7:]
    if last:
        own_light, other_light, outs = outs[0], outs[1], outs[2:]
    slab, core, me = index_ref[0], index_ref[2], index_ref[3]
    wide, rows = target_ref.shape
    count, freqs = fields.shape[0], spec.shape[0]
    width = kern_ref.shape[2]

    def kernel_rows(k, start):
        part = slab ^ (start // width)
        place = 0
        for axis, bit in order:
            place = 2 * place + (((k >> (bit - 1)) & 1) if axis == "kern" else ((part >> bit) & 1))
        here = pl.ds(start % width, BLOCK)
        return kern_ref[place, 0, here].astype(FLOAT), kern_ref[place, 1, here].astype(FLOAT)

    copies = piece_copies(spec_pieces, half_spec, me) + [(rows_n.at[: 2 * freqs], rows_v)]
    size = spectra[0].shape[0]
    copies += [(piece, kern_ref.at[i * size : (i + 1) * size]) for i, piece in enumerate(spectra)]
    needed = len(copies)
    copies += [(cols_t, cols_t_v), (target_all, target_ref), (cols_n, cols_v), (rows_t.at[:, : 2 * freqs], rows_t_v)]
    waits = start_all(copies, sems)
    total[...] = jnp.zeros_like(total)
    for wait in waits[: len(spec_pieces)]:
        wait.wait()

    half = freqs // 2
    mirror = anti_diagonal(freqs, freqs)
    flip = anti_diagonal(half, half)
    spec[half:] = half_spec[:, : 2 * freqs]
    lane = iotas(half, freqs)[1]
    past_re = half_spec[:, 2 * freqs : 2 * freqs + EXTRA][:, :1].astype(FLOAT)
    past_im = half_spec[:, 2 * freqs : 2 * freqs + EXTRA][:, 1:2].astype(FLOAT)
    turned[:, :freqs] = jnp.where(lane == 0, past_re, plain(half_spec[:, :freqs], mirror)).astype(HALF)
    turned[:, freqs:] = jnp.where(lane == 0, -past_im, -plain(half_spec[:, freqs : 2 * freqs], mirror)).astype(HALF)
    edge = collect_rows(half_spec[: 2 * freqs // SPREAD, 2 * freqs :], 2 * freqs)
    edge = jnp.sum(edge, axis=0, keepdims=True)
    line = iotas(half, 2 * freqs)[0]
    spec[:half] = jnp.where(line == 0, edge, plain(flip, turned[...])).astype(HALF)
    for wait in waits[len(spec_pieces) : needed]:
        wait.wait()

    def make_rows(k):
        for start in range(0, freqs, BLOCK):
            here = pl.ds(start, BLOCK)
            spec_re, spec_im = spec[here, :freqs].astype(FLOAT), spec[here, freqs:].astype(FLOAT)
            real, imag = kernel_rows(k, start)
            filtered[here, :freqs] = (real * spec_re - imag * spec_im).astype(HALF)
            filtered[here, freqs:] = (real * spec_im + imag * spec_re).astype(HALF)
        result = plain(filtered[...], rows_v[...])
        sides[k, :freqs] = result.astype(HALF)
        sides[k, freqs:, :rows] = (-result[:, rows:]).astype(HALF)
        sides[k, freqs:, rows:] = result[:, :rows].astype(HALF)

    loop(count, make_rows)

    waits[needed].wait()

    def make_fields(k):
        fields[k] = plain(cols_t_v[...], sides[k])

    loop(count, make_fields)

    waits[needed + 1].wait()
    chunk = 32

    @pl.loop(0, wide // chunk)
    def make_sens(i):
        here = pl.ds(pl.multiple_of(i * chunk, chunk), chunk)
        low = pl.ds(pl.multiple_of(wide + i * chunk, chunk), chunk)
        target = target_ref[here]
        light = None
        for k in range(count):
            real, imag = fields[k, here, :rows], fields[k, here, rows:]
            power = real * real + imag * imag
            light = power if light is None else light + power
        if last:
            side = (i * chunk) // (wide // 2)
            place = pl.ds(pl.multiple_of(i * chunk - side * (wide // 2), chunk), chunk)

            @pl.when(side == core)
            def _():
                own_light[place] = light

            @pl.when(side != core)
            def _():
                other_light[place] = light.astype(HALF)

        sens = None
        for dose in range(dose_ref.shape[0]):
            factor = dose_ref[dose]
            level = jnp.tanh((0.5 * STEEPNESS * factor) * light - 0.5 * STEEPNESS * THRESHOLD)
            slope = (level - target) * (1.0 - level * level) * (0.25 * STEEPNESS * factor)
            sens = slope if sens is None else sens + slope
        for k in range(count):
            real = sens * fields[k, here, :rows]
            imag = sens * fields[k, here, rows:]
            cotangent[k, here, :rows] = real.astype(HALF)
            cotangent[k, here, rows:] = imag.astype(HALF)
            cotangent[k, low, :rows] = imag.astype(HALF)
            cotangent[k, low, rows:] = (-real).astype(HALF)

    waits[needed + 2].wait()
    waits[needed + 3].wait()

    def go_back(k):
        back[...] = plain(cols_v[...], cotangent[k]).astype(HALF)
        slopes = filtered_slopes(back, rows_t_v)
        for start in range(0, freqs, BLOCK):
            here = pl.ds(start, BLOCK)
            real, imag = kernel_rows(k, start)
            slope_re, slope_im = slopes(start)
            total[here, :freqs] += real * slope_re + imag * slope_im
            total[here, freqs:] += real * slope_im - imag * slope_re

    def filtered_slopes(back, table):
        step = min(256, freqs)
        made = {}

        def at(start):
            first = start // step * step
            if first not in made:
                made.clear()
                made[first] = plain(back[first : first + step], table[...])
            part = made[first][start - first : start - first + BLOCK]
            return part[:, :freqs], part[:, freqs:]

        return at

    loop(count, go_back)

    turned[...] = plain(flip, total[:half].astype(HALF)).astype(HALF)
    half_spec[:, :freqs] = (total[half:, :freqs] + plain(turned[:, :freqs], mirror)).astype(HALF)
    half_spec[:, freqs : 2 * freqs] = (total[half:, freqs:] - plain(turned[:, freqs:], mirror)).astype(HALF)
    past_re = turned[:, :EXTRA][:, :1].astype(FLOAT)
    past_im = turned[:, freqs : freqs + EXTRA][:, :1].astype(FLOAT)
    lane = iotas(half, EXTRA)[1]
    extra = jnp.where(lane == 0, past_re, jnp.where(lane == 1, -past_im, 0.0))
    spread = spread_row(total[:1])
    lines = spread.shape[0]
    half_spec[:lines, 2 * freqs :] = (extra[:lines] + spread).astype(HALF)
    half_spec[lines:, 2 * freqs :] = extra[lines:].astype(HALF)
    write_blocks(half_spec, outs, me)


def print_kernel(index_ref, dose_ref, own_ref, other_ref, printed_ref):
    core = index_ref[2]
    cols = own_ref.shape[0]
    for focus, light_ref in ((core, own_ref), (1 - core, other_ref)):
        for start in range(0, cols, 128):
            light = light_ref[start : start + 128].astype(FLOAT).T
            for dose in range(dose_ref.shape[0]):
                level = jnp.tanh(0.5 * STEEPNESS * (dose_ref[dose] * light - THRESHOLD))
                printed_ref[focus, dose, :, start : start + 128] = 0.5 * level + 0.5


def body(kern_size, slab_size, mask_params, target_bits, kernels, weights, dose_factors):
    rows, cols = mask_params.shape
    freqs = kernels.shape[2]
    assert kernels.shape[0] == 1 and kern_size % FOCI == 0
    count = kern_size // FOCI
    wide = FOCI * cols
    sizes = {"kern": kern_size, "slab": slab_size}
    slab, kern = lax.axis_index("slab"), lax.axis_index("kern")
    rounds = plan_rounds(sizes)
    me = jnp.int32(0)
    for axis, bit in [("kern", 0)] + rounds[0]:
        me = 2 * me + (((kern if axis == "kern" else slab) >> bit) & 1)
    index = jnp.stack([slab, kern // FOCI, kern % FOCI, me]).astype(jnp.int32)
    tables = trig_tables(rows * slab_size, freqs)
    rows_all = jnp.asarray(row_blocks(tables, slab_size))
    cols_all = jnp.asarray(col_blocks(tables, count))

    smem = pl.BlockSpec(memory_space=pltpu.SMEM)
    vmem = pl.BlockSpec(memory_space=pltpu.VMEM)
    anywhere = pl.BlockSpec(memory_space=pl.ANY)
    hbm = pl.BlockSpec(memory_space=pltpu.HBM)
    compiler_params = pltpu.CompilerParams(vmem_limit_bytes=VMEM_LIMIT)
    members = 1 << len(rounds[0])
    parts_out = [jax.ShapeDtypeStruct((freqs // 4 // members, 2 * freqs + EXTRA), HALF)] * (2 * members)
    rows_n_like = ((2 * freqs + EXTRA, 2 * rows), HALF)
    rows_t_like = ((2 * rows, 2 * freqs + EXTRA), HALF)
    cols_n_like = ((freqs, 2 * wide), HALF)
    cols_t_like = ((wide, 2 * freqs), HALF)
    spec_like = ((freqs, 2 * freqs), HALF)
    half_like = ((freqs // 2, 2 * freqs + EXTRA), HALF)
    raw_rows_like = ((2, rows, freqs), FLOAT)
    dma = pltpu.SemaphoreType.DMA

    table_likes = [rows_n_like, rows_t_like, cols_n_like, cols_t_like, ((wide, rows), FLOAT)]
    rows_n, rows_t, cols_n, cols_t, target = pl.pallas_call(
        table_kernel,
        out_shape=[jax.ShapeDtypeStruct(*like) for like in table_likes],
        in_specs=[smem, hbm, hbm, anywhere],
        out_specs=[vmem] * 5,
        scratch_shapes=[
            pltpu.VMEM(*raw_rows_like),
            pltpu.VMEM((2, freqs, wide), FLOAT),
            pltpu.VMEM((rows, wide), jnp.int32),
            dma((3,)),
        ],
        compiler_params=pltpu.CompilerParams(vmem_limit_bytes=60 * 1024 * 1024),
        name="make_tables",
    )(index, rows_all, cols_all, target_bits)
    made = (rows_n, rows_t, cols_n, cols_t)

    begun = [jnp.swapaxes(kernels * jnp.sqrt(weights)[:, None, None, None], 2, 3).astype(HALF)]
    for bits in reversed(rounds[1:]):
        value = begun[0] if len(begun) == 1 else jnp.concatenate(begun, axis=0)
        begun = [value] + [partner(value, bits, p, sizes) for p in range(1, 1 << len(bits))]
    spectra = None
    order = [pair for bits in rounds for pair in bits]

    parts = pl.pallas_call(
        first_kernel,
        out_shape=parts_out,
        in_specs=[smem, vmem, hbm, hbm],
        out_specs=[vmem] * len(parts_out),
        scratch_shapes=[
            pltpu.VMEM(*raw_rows_like),
            pltpu.VMEM((2, freqs, cols), FLOAT),
            pltpu.VMEM(*rows_t_like),
            pltpu.VMEM((freqs, 2 * cols), HALF),
            pltpu.VMEM((freqs // 2, 2 * rows), HALF),
            pltpu.VMEM(*half_like),
            dma((2,)),
        ],
        compiler_params=compiler_params,
        name="first_spectrum",
    )(index, mask_params, rows_all, cols_all)

    params, printed = mask_params, None
    for step in range(STEPS):
        first, last = step == 0, step == STEPS - 1
        if first:
            parts, (begun, made, target), _ = reduce_all(parts, rounds, sizes, (begun, made, target))
            value = jnp.concatenate(begun, axis=0)
            spectra = [value] + [partner(value, rounds[0], p, sizes) for p in range(1, members)]
        else:
            parts, _, _ = reduce_all(parts, rounds, sizes)
        out_shape = list(parts_out)
        if last:
            lights = [jax.ShapeDtypeStruct((cols, rows), FLOAT), jax.ShapeDtypeStruct((cols, rows), HALF)]
            out_shape = lights + out_shape
        outs = pl.pallas_call(
            functools.partial(image_kernel, last, len(parts), order),
            out_shape=out_shape,
            in_specs=[smem, smem] + [hbm] * 5 + [anywhere] * (len(parts) + len(spectra)),
            out_specs=[vmem] * len(out_shape),
            scratch_shapes=[
                pltpu.VMEM((2 * freqs, 2 * rows), HALF),
                pltpu.VMEM((2 * rows, 2 * freqs), HALF),
                pltpu.VMEM(*cols_n_like),
                pltpu.VMEM(*cols_t_like),
                pltpu.VMEM((wide, rows), FLOAT),
                pltpu.VMEM((count * slab_size,) + kernels.shape[1:2] + (kernels.shape[3], freqs), HALF),
                pltpu.VMEM(*spec_like),
                pltpu.VMEM(*spec_like),
                pltpu.VMEM((count, 2 * freqs, 2 * rows), HALF),
                pltpu.VMEM((count, wide, 2 * rows), FLOAT),
                pltpu.VMEM((count, 2 * wide, 2 * rows), HALF),
                pltpu.VMEM((freqs, 2 * rows), HALF),
                pltpu.VMEM((freqs, 2 * freqs), FLOAT),
                pltpu.VMEM(*half_like),
                pltpu.VMEM((freqs // 2, 2 * freqs), HALF),
                dma((len(parts) + 5 + len(spectra),)),
            ],
            compiler_params=compiler_params,
            name="image_and_back",
        )(
            index,
            dose_factors,
            *made,
            target,
            *parts,
            *spectra,
        )
        parts = outs[-len(parts) :]
        if last:
            printed = pl.pallas_call(
                print_kernel,
                out_shape=jax.ShapeDtypeStruct((FOCI, dose_factors.shape[0], rows, cols), FLOAT),
                in_specs=[smem, smem, vmem, vmem],
                out_specs=vmem,
                compiler_params=compiler_params,
                name="print_resist",
            )(index, dose_factors, outs[0], partner(outs[1], [("kern", 0)], 1, sizes))
        parts, _, printed = reduce_all(parts, rounds, sizes, None, printed)
        tile = jax.ShapeDtypeStruct((rows, cols) if last else (cols, rows), FLOAT)
        common = [pltpu.VMEM(*rows_n_like), pltpu.VMEM((cols, 2 * freqs), HALF)]
        work = [pltpu.VMEM(*half_like), pltpu.VMEM((2 * freqs, rows), HALF)]
        if last:
            scratch = common + work + [dma((len(parts) + 2,))]
        else:
            scratch = common[:1] + [pltpu.VMEM(*rows_t_like)] + common[1:]
            scratch += [pltpu.VMEM((freqs, 2 * cols), HALF)] + work
            scratch += [pltpu.VMEM((freqs // 2, 2 * rows), HALF), dma((len(parts) + 5,))]
        outs = pl.pallas_call(
            functools.partial(update_kernel, first, last, len(parts)),
            out_shape=[tile] if last else [tile] + parts_out,
            in_specs=[smem, vmem] + [hbm] * 4 + [anywhere] * len(parts),
            out_specs=[vmem] * (1 if last else 1 + len(parts)),
            scratch_shapes=scratch,
            compiler_params=compiler_params,
            name="update",
        )(index, params, *made, *parts)
        params = outs[0]
        if not last:
            parts = outs[1:]
    return (params, printed)


def solution(mesh):
    sizes = dict(mesh.shape)
    in_specs = (P("slab", "kern"), P("slab", None), P("kern", None, None, "slab"), P("kern"), P())
    out_specs = (P("slab", "kern"), P(None, None, "slab", "kern"))
    return jax.shard_map(
        functools.partial(body, sizes["kern"], sizes["slab"]),
        mesh=mesh,
        in_specs=in_specs,
        out_specs=out_specs,
        check_vma=False,
    )
```

```python
import functools

import jax
import jax.numpy as jnp
import numpy as np
from jax import lax
from jax.experimental import pallas as pl
from jax.experimental.pallas import tpu as pltpu
from jax.sharding import PartitionSpec as P

FOCI = 2
STEPS = 2
STEEPNESS = 3.0
THRESHOLD = 1.0
STEP_RATE = 0.4
BLOCK = 16
EXTRA = 128
SPREAD = 64
VMEM_LIMIT = 50 * 1024 * 1024
FLOAT = jnp.float32
HALF = jnp.bfloat16
AXES = ("kern", "slab")


def plain(left, right):
    return jnp.dot(left, right, preferred_element_type=FLOAT)


def trig_tables(pixels, freqs):
    phases = ((np.arange(freqs) - freqs // 2)[:, None] * np.arange(pixels)[None, :]) % pixels
    angles = phases.astype(np.float32) * np.float32(2.0 * np.pi / pixels)
    scale = np.float32(1.0 / np.sqrt(pixels))
    cosine = (np.cos(angles.astype(np.float64)).astype(np.float32) * scale).astype(HALF)
    sine = (np.sin(angles.astype(np.float64)).astype(np.float32) * scale).astype(HALF)
    return np.stack([cosine.astype(np.float32), sine.astype(np.float32)])


def row_blocks(tables, parts):
    _, freqs, pixels = tables.shape
    split = tables.transpose(0, 2, 1).reshape(2, parts, pixels // parts, freqs)
    return np.ascontiguousarray(split.transpose(1, 0, 2, 3))


def col_blocks(tables, parts):
    _, freqs, pixels = tables.shape
    split = tables.reshape(2, freqs, parts, pixels // parts)
    return np.ascontiguousarray(split.transpose(2, 0, 1, 3))


def flat_index(kern, slab, sizes):
    return kern * sizes["slab"] + slab


def plan_rounds(sizes):
    kern_bits = [("kern", bit) for bit in range(1, sizes["kern"].bit_length() - 1)]
    slab_bits = [("slab", bit) for bit in range(sizes["slab"].bit_length() - 1)]
    rounds = [kern_bits[:1] + slab_bits[:1], slab_bits[1:3], kern_bits[1:3], slab_bits[3:]]
    return [bits for bits in rounds if bits]


def partner(values, bits, place, sizes):
    shift = {"kern": 0, "slab": 0}
    for i, (axis, bit) in enumerate(bits):
        if (place >> (len(bits) - 1 - i)) & 1:
            shift[axis] |= 1 << bit
    mask = flat_index(shift["kern"], shift["slab"], sizes)
    total = sizes["kern"] * sizes["slab"]
    return lax.ppermute(values, AXES, [(i, i ^ mask) for i in range(total)])


def add_all(pieces):
    total = pieces[0].astype(FLOAT)
    for piece in pieces[1:]:
        total = total + piece.astype(FLOAT)
    return total.astype(HALF)


def tied(values, others):
    return lax.optimization_barrier((values, others))


def reduce_all(parts, rounds, sizes, late=None):
    core = [("kern", 0)]
    count = len(parts) // 2
    parts = [add_all([mine, partner(other, core, 1, sizes)]) for mine, other in zip(parts[:count], parts[count:])]
    total = add_all([parts[0]] + [partner(parts[p], rounds[0], p, sizes) for p in range(1, count)])
    for bits in rounds[1:]:
        others = [partner(total, bits, p, sizes) for p in range(1, 1 << len(bits))]
        if late is not None and bits is rounds[1]:
            others, late = tied(others, late)
        total = add_all([total] + others)
    pieces = [total] + [partner(total, rounds[0], p, sizes) for p in range(1, count)]
    return pieces + [partner(piece, core, 1, sizes) for piece in pieces], late


def start_all(copies, sems):
    started = [pltpu.make_async_copy(source, target, sems.at[i]) for i, (source, target) in enumerate(copies)]
    for copy in started:
        copy.start()
    return started


def piece_copies(pieces, spec, me):
    size = pieces[0].shape[0]
    return [
        (piece, spec.at[pl.ds(pl.multiple_of((place ^ me) * size, size), size)]) for place, piece in enumerate(pieces)
    ]


def iotas(rows, cols):
    shape = (rows, cols)
    return lax.broadcasted_iota(jnp.int32, shape, 0), lax.broadcasted_iota(jnp.int32, shape, 1)


def ones_where(condition):
    return jnp.where(condition, 1.0, 0.0).astype(HALF)


def anti_diagonal(size, total):
    row, lane = iotas(size, size)
    return ones_where(row + lane == total)


def spread_row(line):
    width = line.shape[1]
    row, lane = iotas(width // SPREAD, width)
    masked = jnp.where(lane // SPREAD == row, line, 0.0).astype(HALF)
    row, lane = iotas(width, EXTRA)
    return plain(masked, ones_where(lane == row % SPREAD + SPREAD))


def collect_rows(extra, width):
    row, lane = iotas(EXTRA, width)
    wide = plain(extra, ones_where(row == lane % SPREAD + SPREAD))
    row, lane = iotas(extra.shape[0], width)
    return jnp.where(lane // SPREAD == row, wide, 0.0)


def write_blocks(source, outs, me):
    for place, out in enumerate(outs):
        size = out.shape[0]
        out[...] = source[pl.ds(pl.multiple_of((place ^ me) * size, size), size)].astype(HALF)


def spectrum_of(mask_low, rows_t, cols_ref, col_spec, total):
    cols, rows = mask_low.shape
    half = total.shape[0]
    width = 4 * half
    col_spec[:, :rows] = plain(cols_ref[half:, :cols], mask_low).astype(HALF)
    col_spec[:, rows:] = (-plain(cols_ref[half:, cols:], mask_low)).astype(HALF)
    edge_re = plain(cols_ref[:BLOCK, :cols], mask_low).astype(HALF)
    edge_im = (-plain(cols_ref[:BLOCK, cols:], mask_low)).astype(HALF)
    edge = plain(edge_re, rows_t[:rows, :width]) + plain(edge_im, rows_t[rows:, :width])
    total[:, :width] = plain(col_spec[...], rows_t[:, :width]).astype(HALF)
    extra = plain(col_spec[...], rows_t[:, width:])
    spread = spread_row(edge[:1])
    count = spread.shape[0]
    total[:count, width:] = (extra[:count] + spread).astype(HALF)
    total[count:, width:] = extra[count:].astype(HALF)


def fill_rows_t(raw, rows_t):
    rows, freqs = raw.shape[1:]
    rows_t[:rows, :freqs] = raw[0].astype(HALF)
    rows_t[:rows, freqs : 2 * freqs] = (-raw[1]).astype(HALF)
    rows_t[rows:, :freqs] = raw[1].astype(HALF)
    rows_t[rows:, freqs : 2 * freqs] = raw[0].astype(HALF)
    lane = iotas(rows, EXTRA)[1]
    cosine, sine = raw[0, :, :1], -raw[1, :, :1]
    zero = jnp.zeros((rows, EXTRA), FLOAT)
    rows_t[:rows, 2 * freqs :] = jnp.where(lane == 0, cosine, jnp.where(lane == 1, -sine, zero)).astype(HALF)
    rows_t[rows:, 2 * freqs :] = jnp.where(lane == 0, sine, jnp.where(lane == 1, cosine, zero)).astype(HALF)


def first_kernel(index_ref, params_ref, rows_all, cols_all, *rest):
    outs, scratch = rest[:-7], rest[-7:]
    raw_rows, raw_cols, rows_t, cols_ref, col_spec, total, sems = scratch
    slab, pair, core, me = (index_ref[i] for i in range(4))
    cols = params_ref.shape[1]
    own = pl.ds(pl.multiple_of(core * cols, cols), cols)
    waits = start_all([(cols_all.at[pair, :, :, own], raw_cols), (rows_all.at[slab], raw_rows)], sems)
    mask_low = jnp.tanh(params_ref[...]).T.astype(HALF)
    waits[0].wait()
    cols_ref[:, :cols] = raw_cols[0].astype(HALF)
    cols_ref[:, cols:] = raw_cols[1].astype(HALF)
    waits[1].wait()
    fill_rows_t(raw_rows, rows_t)
    spectrum_of(mask_low, rows_t, cols_ref, col_spec, total)
    write_blocks(total, outs, me)


def table_kernel(index_ref, rows_all, cols_all, target_all, *rest):
    rows_n, rows_t, cols_n, cols_t, target_ref, raw_rows, raw_cols, raw_target, sems = rest
    slab, pair = index_ref[0], index_ref[1]
    rows, freqs = raw_rows.shape[1:]
    wide = raw_cols.shape[2]
    here = pl.ds(pl.multiple_of(pair * wide, wide), wide)
    waits = start_all(
        [(rows_all.at[slab], raw_rows), (cols_all.at[pair], raw_cols), (target_all.at[:, here], raw_target)], sems
    )
    waits[0].wait()
    fill_rows_t(raw_rows, rows_t)
    cosine, sine = raw_rows[0].T, raw_rows[1].T
    rows_n[:freqs, :rows] = cosine.astype(HALF)
    rows_n[:freqs, rows:] = sine.astype(HALF)
    rows_n[freqs : 2 * freqs, :rows] = (-sine).astype(HALF)
    rows_n[freqs : 2 * freqs, rows:] = cosine.astype(HALF)
    line = iotas(EXTRA, rows)[0]
    first, second = cosine[:1], -sine[:1]
    zero = jnp.zeros((EXTRA, rows), FLOAT)
    rows_n[2 * freqs :, :rows] = jnp.where(line == 0, first, jnp.where(line == 1, -second, zero)).astype(HALF)
    rows_n[2 * freqs :, rows:] = jnp.where(line == 0, second, jnp.where(line == 1, first, zero)).astype(HALF)
    waits[1].wait()
    for part in range(2):
        cols_n[:, part * wide : (part + 1) * wide] = raw_cols[part].astype(HALF)
        for start in range(0, wide, 128):
            some = raw_cols[part, :, start : start + 128].T
            cols_t[start : start + 128, part * freqs : (part + 1) * freqs] = some.astype(HALF)
    waits[2].wait()
    for start in range(0, wide, 128):
        target_ref[start : start + 128] = (2 * raw_target[:, start : start + 128] - 1).astype(FLOAT).T


def update_kernel(first, last, count, index_ref, params_ref, rows_n, rows_t, cols_n, cols_t, *rest):
    pieces, rest = rest[:count], rest[count:]
    if last:
        new_ref, rows_v, cols_v, spec, back, sems = rest
    else:
        new_ref, outs, scratch = rest[0], rest[1 : 1 + count], rest[1 + count :]
        rows_v, rows_t_v, cols_v, cols_n_v, spec, back, col_spec, sems = scratch
    core, me = index_ref[2], index_ref[3]
    params = params_ref[...].T if first else params_ref[...]
    cols, rows = params.shape
    half = spec.shape[0]
    freqs = 2 * half
    here = pl.ds(pl.multiple_of(core * cols, cols), cols)
    copies = piece_copies(pieces, spec, me) + [(rows_n, rows_v), (cols_t.at[here], cols_v)]
    if not last:
        wide = cols_n.shape[1] // 2
        copies += [
            (rows_t, rows_t_v),
            (cols_n.at[:, here], cols_n_v.at[:, :cols]),
            (cols_n.at[:, pl.ds(pl.multiple_of(wide + core * cols, cols), cols)], cols_n_v.at[:, cols:]),
        ]
    waits = start_all(copies, sems)
    back[...] = jnp.zeros_like(back)
    for i in range(count + 1):
        waits[i].wait()
    result = plain(spec[...], rows_v[...])
    back[half:freqs] = result[:, :rows].astype(HALF)
    back[freqs + half :] = (-result[:, rows:]).astype(HALF)
    edge = collect_rows(spec[: 2 * freqs // SPREAD, 2 * freqs :], 2 * freqs).astype(HALF)
    edge = jnp.sum(plain(edge, rows_v[: 2 * freqs]), axis=0, keepdims=True)
    line = iotas(BLOCK, rows)[0]
    back[:BLOCK] = jnp.where(line == 0, edge[:, :rows], 0.0).astype(HALF)
    back[freqs : freqs + BLOCK] = jnp.where(line == 0, -edge[:, rows:], 0.0).astype(HALF)
    waits[count + 1].wait()
    gradient = plain(cols_v[...], back[...])
    mask = jnp.tanh(params)
    params = params - STEP_RATE * gradient * (1.0 - mask * mask)
    if last:
        new_ref[...] = params.T
    else:
        new_ref[...] = params
        for i in range(count + 2, len(waits)):
            waits[i].wait()
        spectrum_of(jnp.tanh(params).astype(HALF), rows_t_v, cols_n_v, col_spec, spec)
        write_blocks(spec, outs, me)


def loop(count, step):
    if count <= 2:
        for i in range(count):
            step(i)
    else:
        pl.loop(0, count)(step)


def image_kernel(last, parts, order, index_ref, dose_ref, rows_n, rows_t, cols_n, cols_t, target_all, *rest):
    spec_pieces, rest = rest[:parts], rest[parts:]
    outs = rest[-16 - parts - (2 if last else 0) : -16]
    spectra = rest[: -16 - len(outs)]
    scratch = rest[-16:]
    rows_v, rows_t_v, cols_v, cols_t_v, target_ref, kern_ref, spec = scratch[:7]
    filtered, sides, fields, cotangent, back, total, half_spec, turned, sems = scratch[7:]
    if last:
        own_light, other_light, outs = outs[0], outs[1], outs[2:]
    slab, core, me = index_ref[0], index_ref[2], index_ref[3]
    wide, rows = target_ref.shape
    count, freqs = fields.shape[0], spec.shape[0]
    width = kern_ref.shape[2]

    def kernel_rows(k, start):
        part = slab ^ (start // width)
        place = 0
        for axis, bit in order:
            place = 2 * place + (((k >> (bit - 1)) & 1) if axis == "kern" else ((part >> bit) & 1))
        here = pl.ds(start % width, BLOCK)
        return kern_ref[place, 0, here].astype(FLOAT), kern_ref[place, 1, here].astype(FLOAT)

    copies = piece_copies(spec_pieces, half_spec, me) + [(rows_n.at[: 2 * freqs], rows_v)]
    filled = 0
    for piece in spectra:
        copies.append((piece, kern_ref.at[filled : filled + piece.shape[0]]))
        filled += piece.shape[0]
    needed = len(copies)
    copies += [(cols_t, cols_t_v), (target_all, target_ref), (cols_n, cols_v), (rows_t.at[:, : 2 * freqs], rows_t_v)]
    waits = start_all(copies, sems)
    if count > 2:
        total[...] = jnp.zeros_like(total)
    for wait in waits[: len(spec_pieces)]:
        wait.wait()

    half = freqs // 2
    mirror = anti_diagonal(freqs, freqs)
    flip = anti_diagonal(half, half)
    spec[half:] = half_spec[:, : 2 * freqs]
    lane = iotas(half, freqs)[1]
    past_re = half_spec[:, 2 * freqs : 2 * freqs + EXTRA][:, :1].astype(FLOAT)
    past_im = half_spec[:, 2 * freqs : 2 * freqs + EXTRA][:, 1:2].astype(FLOAT)
    turned[:, :freqs] = jnp.where(lane == 0, past_re, plain(half_spec[:, :freqs], mirror)).astype(HALF)
    turned[:, freqs:] = jnp.where(lane == 0, -past_im, -plain(half_spec[:, freqs : 2 * freqs], mirror)).astype(HALF)
    edge = collect_rows(half_spec[: 2 * freqs // SPREAD, 2 * freqs :], 2 * freqs)
    edge = jnp.sum(edge, axis=0, keepdims=True)
    line = iotas(half, 2 * freqs)[0]
    spec[:half] = jnp.where(line == 0, edge, plain(flip, turned[...])).astype(HALF)
    for wait in waits[len(spec_pieces) : needed]:
        wait.wait()

    def make_rows(k):
        for start in range(0, freqs, BLOCK):
            here = pl.ds(start, BLOCK)
            spec_re, spec_im = spec[here, :freqs].astype(FLOAT), spec[here, freqs:].astype(FLOAT)
            real, imag = kernel_rows(k, start)
            filtered[here, :freqs] = (real * spec_re - imag * spec_im).astype(HALF)
            filtered[here, freqs:] = (real * spec_im + imag * spec_re).astype(HALF)
        result = plain(filtered[...], rows_v[...])
        sides[k, :freqs] = result.astype(HALF)
        sides[k, freqs:, :rows] = (-result[:, rows:]).astype(HALF)
        sides[k, freqs:, rows:] = result[:, :rows].astype(HALF)

    loop(count, make_rows)

    waits[needed].wait()

    def make_fields(k):
        fields[k] = plain(cols_t_v[...], sides[k])

    loop(count, make_fields)

    waits[needed + 1].wait()
    chunk = 32

    @pl.loop(0, wide // chunk, unroll=4)
    def make_sens(i):
        here = pl.ds(pl.multiple_of(i * chunk, chunk), chunk)
        low = pl.ds(pl.multiple_of(wide + i * chunk, chunk), chunk)
        target = target_ref[here]
        light = None
        for k in range(count):
            real, imag = fields[k, here, :rows], fields[k, here, rows:]
            power = real * real + imag * imag
            light = power if light is None else light + power
        if last:
            side = (i * chunk) // (wide // 2)
            place = pl.ds(pl.multiple_of(i * chunk - side * (wide // 2), chunk), chunk)

            @pl.when(side == core)
            def _():
                own_light[place] = light

            @pl.when(side != core)
            def _():
                other_light[place] = light.astype(HALF)

        sens = None
        for dose in range(dose_ref.shape[0]):
            factor = dose_ref[dose]
            level = jnp.tanh((0.5 * STEEPNESS * factor) * light - 0.5 * STEEPNESS * THRESHOLD)
            slope = (level - target) * (1.0 - level * level) * (0.25 * STEEPNESS * factor)
            sens = slope if sens is None else sens + slope
        for k in range(count):
            real = sens * fields[k, here, :rows]
            imag = sens * fields[k, here, rows:]
            cotangent[k, here, :rows] = real.astype(HALF)
            cotangent[k, here, rows:] = imag.astype(HALF)
            cotangent[k, low, :rows] = imag.astype(HALF)
            cotangent[k, low, rows:] = (-real).astype(HALF)

    waits[needed + 2].wait()
    waits[needed + 3].wait()

    def go_back(k):
        back[...] = plain(cols_v[...], cotangent[k]).astype(HALF)
        slopes = filtered_slopes(back, rows_t_v)
        for start in range(0, freqs, BLOCK):
            here = pl.ds(start, BLOCK)
            real, imag = kernel_rows(k, start)
            slope_re, slope_im = slopes(start)
            total_re = real * slope_re + imag * slope_im
            total_im = real * slope_im - imag * slope_re
            if count > 2 or k > 0:
                total_re += total[here, :freqs]
                total_im += total[here, freqs:]
            total[here, :freqs] = total_re
            total[here, freqs:] = total_im

    def filtered_slopes(back, table):
        step = min(256, freqs)
        made = {}

        def at(start):
            first = start // step * step
            if first not in made:
                made.clear()
                made[first] = plain(back[first : first + step], table[...])
            part = made[first][start - first : start - first + BLOCK]
            return part[:, :freqs], part[:, freqs:]

        return at

    loop(count, go_back)

    turned[...] = plain(flip, total[:half].astype(HALF)).astype(HALF)
    half_spec[:, :freqs] = (total[half:, :freqs] + plain(turned[:, :freqs], mirror)).astype(HALF)
    half_spec[:, freqs : 2 * freqs] = (total[half:, freqs:] - plain(turned[:, freqs:], mirror)).astype(HALF)
    past_re = turned[:, :EXTRA][:, :1].astype(FLOAT)
    past_im = turned[:, freqs : freqs + EXTRA][:, :1].astype(FLOAT)
    lane = iotas(half, EXTRA)[1]
    extra = jnp.where(lane == 0, past_re, jnp.where(lane == 1, -past_im, 0.0))
    spread = spread_row(total[:1])
    lines = spread.shape[0]
    half_spec[:lines, 2 * freqs :] = (extra[:lines] + spread).astype(HALF)
    half_spec[lines:, 2 * freqs :] = extra[lines:].astype(HALF)
    write_blocks(half_spec, outs, me)


def print_kernel(index_ref, dose_ref, own_ref, other_ref, printed_ref):
    core = index_ref[2]
    cols = own_ref.shape[0]
    for focus, light_ref in ((core, own_ref), (1 - core, other_ref)):
        for start in range(0, cols, 128):
            light = light_ref[start : start + 128].astype(FLOAT).T
            for dose in range(dose_ref.shape[0]):
                level = jnp.tanh(0.5 * STEEPNESS * (dose_ref[dose] * light - THRESHOLD))
                printed_ref[focus, dose, :, start : start + 128] = 0.5 * level + 0.5


def body(kern_size, slab_size, mask_params, target_bits, kernels, weights, dose_factors):
    rows, cols = mask_params.shape
    freqs = kernels.shape[2]
    assert kernels.shape[0] == 1 and kern_size % FOCI == 0
    count = kern_size // FOCI
    wide = FOCI * cols
    sizes = {"kern": kern_size, "slab": slab_size}
    slab, kern = lax.axis_index("slab"), lax.axis_index("kern")
    rounds = plan_rounds(sizes)
    me = jnp.int32(0)
    for axis, bit in [("kern", 0)] + rounds[0]:
        me = 2 * me + (((kern if axis == "kern" else slab) >> bit) & 1)
    index = jnp.stack([slab, kern // FOCI, kern % FOCI, me]).astype(jnp.int32)
    tables = trig_tables(rows * slab_size, freqs)
    rows_all = jnp.asarray(row_blocks(tables, slab_size))
    cols_all = jnp.asarray(col_blocks(tables, count))

    smem = pl.BlockSpec(memory_space=pltpu.SMEM)
    vmem = pl.BlockSpec(memory_space=pltpu.VMEM)
    anywhere = pl.BlockSpec(memory_space=pl.ANY)
    hbm = pl.BlockSpec(memory_space=pltpu.HBM)
    compiler_params = pltpu.CompilerParams(vmem_limit_bytes=VMEM_LIMIT)
    members = 1 << len(rounds[0])
    parts_out = [jax.ShapeDtypeStruct((freqs // 4 // members, 2 * freqs + EXTRA), HALF)] * (2 * members)
    rows_n_like = ((2 * freqs + EXTRA, 2 * rows), HALF)
    rows_t_like = ((2 * rows, 2 * freqs + EXTRA), HALF)
    cols_n_like = ((freqs, 2 * wide), HALF)
    cols_t_like = ((wide, 2 * freqs), HALF)
    spec_like = ((freqs, 2 * freqs), HALF)
    half_like = ((freqs // 2, 2 * freqs + EXTRA), HALF)
    raw_rows_like = ((2, rows, freqs), FLOAT)
    dma = pltpu.SemaphoreType.DMA

    table_likes = [rows_n_like, rows_t_like, cols_n_like, cols_t_like, ((wide, rows), FLOAT)]
    rows_n, rows_t, cols_n, cols_t, target = pl.pallas_call(
        table_kernel,
        out_shape=[jax.ShapeDtypeStruct(*like) for like in table_likes],
        in_specs=[smem, hbm, hbm, anywhere],
        out_specs=[vmem] * 5,
        scratch_shapes=[
            pltpu.VMEM(*raw_rows_like),
            pltpu.VMEM((2, freqs, wide), FLOAT),
            pltpu.VMEM((rows, wide), jnp.int32),
            dma((3,)),
        ],
        compiler_params=pltpu.CompilerParams(vmem_limit_bytes=60 * 1024 * 1024),
        name="make_tables",
    )(index, rows_all, cols_all, target_bits)
    made = (rows_n, rows_t, cols_n, cols_t)

    begun = [jnp.swapaxes(kernels * jnp.sqrt(weights)[:, None, None, None], 2, 3).astype(HALF)]
    for bits in reversed(rounds[1:]):
        value = begun[0] if len(begun) == 1 else jnp.concatenate(begun, axis=0)
        begun = [value] + [partner(value, bits, p, sizes) for p in range(1, 1 << len(bits))]
    spectra = None
    order = [pair for bits in rounds for pair in bits]

    parts = pl.pallas_call(
        first_kernel,
        out_shape=parts_out,
        in_specs=[smem, vmem, hbm, hbm],
        out_specs=[vmem] * len(parts_out),
        scratch_shapes=[
            pltpu.VMEM(*raw_rows_like),
            pltpu.VMEM((2, freqs, cols), FLOAT),
            pltpu.VMEM(*rows_t_like),
            pltpu.VMEM((freqs, 2 * cols), HALF),
            pltpu.VMEM((freqs // 2, 2 * rows), HALF),
            pltpu.VMEM(*half_like),
            dma((2,)),
        ],
        compiler_params=compiler_params,
        name="first_spectrum",
    )(index, mask_params, rows_all, cols_all)

    parts, (begun, made, target) = tied(parts, (begun, made, target))
    params, printed = mask_params, None
    for step in range(STEPS):
        first, last = step == 0, step == STEPS - 1
        if first:
            value = jnp.concatenate(begun, axis=0)
            spectra = [value] + [partner(value, rounds[0], p, sizes) for p in (1, 2)]
            parts, spectra = reduce_all(parts, rounds, sizes, spectra)
            cut = spectra[0].shape[0] // 2
            spectra = spectra + [
                partner(spectra[2][:cut], rounds[0], 1, sizes),
                partner(spectra[1][cut:], rounds[0], 2, sizes),
            ]
        else:
            parts, _ = reduce_all(parts, rounds, sizes)
        out_shape = list(parts_out)
        if last:
            lights = [jax.ShapeDtypeStruct((cols, rows), FLOAT), jax.ShapeDtypeStruct((cols, rows), HALF)]
            out_shape = lights + out_shape
        outs = pl.pallas_call(
            functools.partial(image_kernel, last, len(parts), order),
            out_shape=out_shape,
            in_specs=[smem, smem] + [hbm] * 5 + [anywhere] * (len(parts) + len(spectra)),
            out_specs=[vmem] * len(out_shape),
            scratch_shapes=[
                pltpu.VMEM((2 * freqs, 2 * rows), HALF),
                pltpu.VMEM((2 * rows, 2 * freqs), HALF),
                pltpu.VMEM(*cols_n_like),
                pltpu.VMEM(*cols_t_like),
                pltpu.VMEM((wide, rows), FLOAT),
                pltpu.VMEM((count * slab_size,) + kernels.shape[1:2] + (kernels.shape[3], freqs), HALF),
                pltpu.VMEM(*spec_like),
                pltpu.VMEM(*spec_like),
                pltpu.VMEM((count, 2 * freqs, 2 * rows), HALF),
                pltpu.VMEM((count, wide, 2 * rows), FLOAT),
                pltpu.VMEM((count, 2 * wide, 2 * rows), HALF),
                pltpu.VMEM((freqs, 2 * rows), HALF),
                pltpu.VMEM((freqs, 2 * freqs), FLOAT),
                pltpu.VMEM(*half_like),
                pltpu.VMEM((freqs // 2, 2 * freqs), HALF),
                dma((len(parts) + 5 + len(spectra),)),
            ],
            compiler_params=compiler_params,
            name="image_and_back",
        )(
            index,
            dose_factors,
            *made,
            target,
            *parts,
            *spectra,
        )
        parts = outs[-len(parts) :]
        if last:
            printed = pl.pallas_call(
                print_kernel,
                out_shape=jax.ShapeDtypeStruct((FOCI, dose_factors.shape[0], rows, cols), FLOAT),
                in_specs=[smem, smem, vmem, vmem],
                out_specs=vmem,
                compiler_params=compiler_params,
                name="print_resist",
            )(index, dose_factors, outs[0], partner(outs[1], [("kern", 0)], 1, sizes))
        parts, printed = reduce_all(parts, rounds, sizes, printed)
        tile = jax.ShapeDtypeStruct((rows, cols) if last else (cols, rows), FLOAT)
        common = [pltpu.VMEM(*rows_n_like), pltpu.VMEM((cols, 2 * freqs), HALF)]
        work = [pltpu.VMEM(*half_like), pltpu.VMEM((2 * freqs, rows), HALF)]
        if last:
            scratch = common + work + [dma((len(parts) + 2,))]
        else:
            scratch = common[:1] + [pltpu.VMEM(*rows_t_like)] + common[1:]
            scratch += [pltpu.VMEM((freqs, 2 * cols), HALF)] + work
            scratch += [pltpu.VMEM((freqs // 2, 2 * rows), HALF), dma((len(parts) + 5,))]
        outs = pl.pallas_call(
            functools.partial(update_kernel, first, last, len(parts)),
            out_shape=[tile] if last else [tile] + parts_out,
            in_specs=[smem, vmem] + [hbm] * 4 + [anywhere] * len(parts),
            out_specs=[vmem] * (1 if last else 1 + len(parts)),
            scratch_shapes=scratch,
            compiler_params=compiler_params,
            name="update",
        )(index, params, *made, *parts)
        params = outs[0]
        if not last:
            parts = outs[1:]
    return (params, printed)


def solution(mesh):
    sizes = dict(mesh.shape)
    in_specs = (P("slab", "kern"), P("slab", None), P("kern", None, None, "slab"), P("kern"), P())
    out_specs = (P("slab", "kern"), P(None, None, "slab", "kern"))
    return jax.shard_map(
        functools.partial(body, sizes["kern"], sizes["slab"]),
        mesh=mesh,
        in_specs=in_specs,
        out_specs=out_specs,
        check_vma=False,
    )
```

```python
import functools

import jax
import jax.numpy as jnp
import numpy as np
from jax import lax
from jax.experimental import pallas as pl
from jax.experimental.pallas import tpu as pltpu
from jax.sharding import PartitionSpec as P

FOCI = 2
STEPS = 2
STEEPNESS = 3.0
THRESHOLD = 1.0
STEP_RATE = 0.4
BLOCK = 16
EXTRA = 128
SPREAD = 64
VMEM_LIMIT = 50 * 1024 * 1024
FLOAT = jnp.float32
HALF = jnp.bfloat16
AXES = ("kern", "slab")


def plain(left, right):
    return jnp.dot(left, right, preferred_element_type=FLOAT)


def trig_tables(pixels, freqs):
    phases = ((np.arange(freqs) - freqs // 2)[:, None] * np.arange(pixels)[None, :]) % pixels
    angles = phases.astype(np.float32) * np.float32(2.0 * np.pi / pixels)
    scale = np.float32(1.0 / np.sqrt(pixels))
    cosine = (np.cos(angles.astype(np.float64)).astype(np.float32) * scale).astype(HALF)
    sine = (np.sin(angles.astype(np.float64)).astype(np.float32) * scale).astype(HALF)
    return np.stack([cosine.astype(np.float32), sine.astype(np.float32)])


def row_blocks(tables, parts):
    _, freqs, pixels = tables.shape
    split = tables.transpose(0, 2, 1).reshape(2, parts, pixels // parts, freqs)
    return np.ascontiguousarray(split.transpose(1, 0, 2, 3))


def col_blocks(tables, parts):
    _, freqs, pixels = tables.shape
    split = tables.reshape(2, freqs, parts, pixels // parts)
    return np.ascontiguousarray(split.transpose(2, 0, 1, 3))


def flat_index(kern, slab, sizes):
    return kern * sizes["slab"] + slab


def plan_rounds(sizes):
    kern_bits = [("kern", bit) for bit in range(1, sizes["kern"].bit_length() - 1)]
    slab_bits = [("slab", bit) for bit in range(sizes["slab"].bit_length() - 1)]
    rounds = [kern_bits[:1] + slab_bits[:1], slab_bits[1:3], kern_bits[1:3], slab_bits[3:]]
    return [bits for bits in rounds if bits]


def partner(values, bits, place, sizes):
    shift = {"kern": 0, "slab": 0}
    for i, (axis, bit) in enumerate(bits):
        if (place >> (len(bits) - 1 - i)) & 1:
            shift[axis] |= 1 << bit
    mask = flat_index(shift["kern"], shift["slab"], sizes)
    total = sizes["kern"] * sizes["slab"]
    return lax.ppermute(values, AXES, [(i, i ^ mask) for i in range(total)])


def add_all(pieces):
    total = pieces[0].astype(FLOAT)
    for piece in pieces[1:]:
        total = total + piece.astype(FLOAT)
    return total.astype(HALF)


def tied(values, others):
    return lax.optimization_barrier((values, others))


def reduce_all(parts, rounds, sizes, early=None, late=None):
    core = [("kern", 0)]
    count = len(parts) // 2
    parts = [add_all([mine, partner(other, core, 1, sizes)]) for mine, other in zip(parts[:count], parts[count:])]
    others = [partner(parts[p], rounds[0], p, sizes) for p in range(1, count)]
    if early is not None:
        others, early = tied(others, early)
    total = add_all([parts[0]] + others)
    for bits in rounds[1:]:
        others = [partner(total, bits, p, sizes) for p in range(1, 1 << len(bits))]
        if late is not None and bits is rounds[1]:
            others, late = tied(others, late(early))
        total = add_all([total] + others)
    pieces = [total] + [partner(total, rounds[0], p, sizes) for p in range(1, count)]
    return pieces + [partner(piece, core, 1, sizes) for piece in pieces], late


def start_all(copies, sems):
    started = [pltpu.make_async_copy(source, target, sems.at[i]) for i, (source, target) in enumerate(copies)]
    for copy in started:
        copy.start()
    return started


def piece_copies(pieces, spec, me):
    size = pieces[0].shape[0]
    return [
        (piece, spec.at[pl.ds(pl.multiple_of((place ^ me) * size, size), size)]) for place, piece in enumerate(pieces)
    ]


def iotas(rows, cols):
    shape = (rows, cols)
    return lax.broadcasted_iota(jnp.int32, shape, 0), lax.broadcasted_iota(jnp.int32, shape, 1)


def ones_where(condition):
    return jnp.where(condition, 1.0, 0.0).astype(HALF)


def anti_diagonal(size, total):
    row, lane = iotas(size, size)
    return ones_where(row + lane == total)


def spread_row(line):
    width = line.shape[1]
    row, lane = iotas(width // SPREAD, width)
    masked = jnp.where(lane // SPREAD == row, line, 0.0).astype(HALF)
    row, lane = iotas(width, EXTRA)
    return plain(masked, ones_where(lane == row % SPREAD + SPREAD))


def collect_rows(extra, width):
    row, lane = iotas(EXTRA, width)
    wide = plain(extra, ones_where(row == lane % SPREAD + SPREAD))
    row, lane = iotas(extra.shape[0], width)
    return jnp.where(lane // SPREAD == row, wide, 0.0)


def write_blocks(source, outs, me):
    for place, out in enumerate(outs):
        size = out.shape[0]
        out[...] = source[pl.ds(pl.multiple_of((place ^ me) * size, size), size)].astype(HALF)


def spectrum_of(mask_low, rows_t, cols_ref, col_spec, total):
    cols, rows = mask_low.shape
    half = total.shape[0]
    width = 4 * half
    col_spec[:, :rows] = plain(cols_ref[half:, :cols], mask_low).astype(HALF)
    col_spec[:, rows:] = (-plain(cols_ref[half:, cols:], mask_low)).astype(HALF)
    edge_re = plain(cols_ref[:BLOCK, :cols], mask_low).astype(HALF)
    edge_im = (-plain(cols_ref[:BLOCK, cols:], mask_low)).astype(HALF)
    edge = plain(edge_re, rows_t[:rows, :width]) + plain(edge_im, rows_t[rows:, :width])
    total[:, :width] = plain(col_spec[...], rows_t[:, :width]).astype(HALF)
    extra = plain(col_spec[...], rows_t[:, width:])
    spread = spread_row(edge[:1])
    count = spread.shape[0]
    total[:count, width:] = (extra[:count] + spread).astype(HALF)
    total[count:, width:] = extra[count:].astype(HALF)


def fill_rows_t(raw, rows_t):
    rows, freqs = raw.shape[1:]
    rows_t[:rows, :freqs] = raw[0].astype(HALF)
    rows_t[:rows, freqs : 2 * freqs] = (-raw[1]).astype(HALF)
    rows_t[rows:, :freqs] = raw[1].astype(HALF)
    rows_t[rows:, freqs : 2 * freqs] = raw[0].astype(HALF)
    lane = iotas(rows, EXTRA)[1]
    cosine, sine = raw[0, :, :1], -raw[1, :, :1]
    zero = jnp.zeros((rows, EXTRA), FLOAT)
    rows_t[:rows, 2 * freqs :] = jnp.where(lane == 0, cosine, jnp.where(lane == 1, -sine, zero)).astype(HALF)
    rows_t[rows:, 2 * freqs :] = jnp.where(lane == 0, sine, jnp.where(lane == 1, cosine, zero)).astype(HALF)


def first_kernel(index_ref, params_ref, rows_all, cols_all, *rest):
    outs, scratch = rest[:-7], rest[-7:]
    raw_rows, raw_cols, rows_t, cols_ref, col_spec, total, sems = scratch
    slab, pair, core, me = (index_ref[i] for i in range(4))
    cols = params_ref.shape[1]
    own = pl.ds(pl.multiple_of(core * cols, cols), cols)
    waits = start_all([(cols_all.at[pair, :, :, own], raw_cols), (rows_all.at[slab], raw_rows)], sems)
    mask_low = jnp.tanh(params_ref[...]).T.astype(HALF)
    waits[0].wait()
    cols_ref[:, :cols] = raw_cols[0].astype(HALF)
    cols_ref[:, cols:] = raw_cols[1].astype(HALF)
    waits[1].wait()
    fill_rows_t(raw_rows, rows_t)
    spectrum_of(mask_low, rows_t, cols_ref, col_spec, total)
    write_blocks(total, outs, me)


def table_kernel(index_ref, rows_all, cols_all, target_all, *rest):
    rows_n, rows_t, cols_n, cols_t, target_ref, raw_rows, raw_cols, raw_target, sems = rest
    slab, pair = index_ref[0], index_ref[1]
    rows, freqs = raw_rows.shape[1:]
    wide = raw_cols.shape[2]
    here = pl.ds(pl.multiple_of(pair * wide, wide), wide)
    waits = start_all(
        [(rows_all.at[slab], raw_rows), (cols_all.at[pair], raw_cols), (target_all.at[:, here], raw_target)], sems
    )
    waits[0].wait()
    fill_rows_t(raw_rows, rows_t)
    cosine, sine = raw_rows[0].T, raw_rows[1].T
    rows_n[:freqs, :rows] = cosine.astype(HALF)
    rows_n[:freqs, rows:] = sine.astype(HALF)
    rows_n[freqs : 2 * freqs, :rows] = (-sine).astype(HALF)
    rows_n[freqs : 2 * freqs, rows:] = cosine.astype(HALF)
    line = iotas(EXTRA, rows)[0]
    first, second = cosine[:1], -sine[:1]
    zero = jnp.zeros((EXTRA, rows), FLOAT)
    rows_n[2 * freqs :, :rows] = jnp.where(line == 0, first, jnp.where(line == 1, -second, zero)).astype(HALF)
    rows_n[2 * freqs :, rows:] = jnp.where(line == 0, second, jnp.where(line == 1, first, zero)).astype(HALF)
    waits[1].wait()
    for part in range(2):
        cols_n[:, part * wide : (part + 1) * wide] = raw_cols[part].astype(HALF)
        for start in range(0, wide, 128):
            some = raw_cols[part, :, start : start + 128].T
            cols_t[start : start + 128, part * freqs : (part + 1) * freqs] = some.astype(HALF)
    waits[2].wait()
    for start in range(0, wide, 128):
        target_ref[start : start + 128] = (2 * raw_target[:, start : start + 128] - 1).astype(FLOAT).T


def update_kernel(first, last, count, index_ref, params_ref, rows_n, rows_t, cols_n, cols_t, *rest):
    pieces, rest = rest[:count], rest[count:]
    if last:
        new_ref, rows_v, cols_v, spec, back, sems = rest
    else:
        new_ref, outs, scratch = rest[0], rest[1 : 1 + count], rest[1 + count :]
        rows_v, rows_t_v, cols_v, cols_n_v, spec, back, col_spec, sems = scratch
    core, me = index_ref[2], index_ref[3]
    params = params_ref[...].T if first else params_ref[...]
    cols, rows = params.shape
    half = spec.shape[0]
    freqs = 2 * half
    here = pl.ds(pl.multiple_of(core * cols, cols), cols)
    copies = piece_copies(pieces, spec, me) + [(rows_n, rows_v), (cols_t.at[here], cols_v)]
    if not last:
        wide = cols_n.shape[1] // 2
        copies += [
            (rows_t, rows_t_v),
            (cols_n.at[:, here], cols_n_v.at[:, :cols]),
            (cols_n.at[:, pl.ds(pl.multiple_of(wide + core * cols, cols), cols)], cols_n_v.at[:, cols:]),
        ]
    waits = start_all(copies, sems)
    back[...] = jnp.zeros_like(back)
    for i in range(count + 1):
        waits[i].wait()
    result = plain(spec[...], rows_v[...])
    back[half:freqs] = result[:, :rows].astype(HALF)
    back[freqs + half :] = (-result[:, rows:]).astype(HALF)
    edge = collect_rows(spec[: 2 * freqs // SPREAD, 2 * freqs :], 2 * freqs).astype(HALF)
    edge = jnp.sum(plain(edge, rows_v[: 2 * freqs]), axis=0, keepdims=True)
    line = iotas(BLOCK, rows)[0]
    back[:BLOCK] = jnp.where(line == 0, edge[:, :rows], 0.0).astype(HALF)
    back[freqs : freqs + BLOCK] = jnp.where(line == 0, -edge[:, rows:], 0.0).astype(HALF)
    waits[count + 1].wait()
    gradient = plain(cols_v[...], back[...])
    mask = jnp.tanh(params)
    params = params - STEP_RATE * gradient * (1.0 - mask * mask)
    if last:
        new_ref[...] = params.T
    else:
        new_ref[...] = params
        for i in range(count + 2, len(waits)):
            waits[i].wait()
        spectrum_of(jnp.tanh(params).astype(HALF), rows_t_v, cols_n_v, col_spec, spec)
        write_blocks(spec, outs, me)


def loop(count, step):
    if count <= 2:
        for i in range(count):
            step(i)
    else:
        pl.loop(0, count)(step)


def image_kernel(last, parts, order, index_ref, dose_ref, rows_n, rows_t, cols_n, cols_t, target_all, *rest):
    spec_pieces, rest = rest[:parts], rest[parts:]
    outs = rest[-16 - parts - (2 if last else 0) : -16]
    spectra = rest[: -16 - len(outs)]
    scratch = rest[-16:]
    rows_v, rows_t_v, cols_v, cols_t_v, target_ref, kern_ref, spec = scratch[:7]
    filtered, sides, fields, cotangent, back, total, half_spec, turned, sems = scratch[7:]
    if last:
        own_light, other_light, outs = outs[0], outs[1], outs[2:]
    slab, core, me = index_ref[0], index_ref[2], index_ref[3]
    wide, rows = target_ref.shape
    count, freqs = fields.shape[0], spec.shape[0]
    width = kern_ref.shape[2]

    def kernel_rows(k, start):
        part = slab ^ (start // width)
        place = 0
        for axis, bit in order:
            place = 2 * place + (((k >> (bit - 1)) & 1) if axis == "kern" else ((part >> bit) & 1))
        here = pl.ds(start % width, BLOCK)
        return kern_ref[place, 0, here], kern_ref[place, 1, here]

    copies = piece_copies(spec_pieces, half_spec, me) + [(rows_n.at[: 2 * freqs], rows_v)]
    filled = 0
    for piece in spectra:
        copies.append((piece, kern_ref.at[filled : filled + piece.shape[0]]))
        filled += piece.shape[0]
    needed = len(copies)
    copies += [(cols_t, cols_t_v), (target_all, target_ref), (cols_n, cols_v), (rows_t.at[:, : 2 * freqs], rows_t_v)]
    waits = start_all(copies, sems)
    if count > 2:
        total[...] = jnp.zeros_like(total)
    for wait in waits[: len(spec_pieces)]:
        wait.wait()

    half = freqs // 2
    mirror = anti_diagonal(freqs, freqs)
    flip = anti_diagonal(half, half)
    spec[half:] = half_spec[:, : 2 * freqs]
    lane = iotas(half, freqs)[1]
    past_re = half_spec[:, 2 * freqs : 2 * freqs + EXTRA][:, :1].astype(FLOAT)
    past_im = half_spec[:, 2 * freqs : 2 * freqs + EXTRA][:, 1:2].astype(FLOAT)
    turned[:, :freqs] = jnp.where(lane == 0, past_re, plain(half_spec[:, :freqs], mirror)).astype(HALF)
    turned[:, freqs:] = jnp.where(lane == 0, -past_im, -plain(half_spec[:, freqs : 2 * freqs], mirror)).astype(HALF)
    edge = collect_rows(half_spec[: 2 * freqs // SPREAD, 2 * freqs :], 2 * freqs)
    edge = jnp.sum(edge, axis=0, keepdims=True)
    line = iotas(half, 2 * freqs)[0]
    spec[:half] = jnp.where(line == 0, edge, plain(flip, turned[...])).astype(HALF)
    for wait in waits[len(spec_pieces) : needed]:
        wait.wait()

    def make_rows(k):
        for start in range(0, freqs, BLOCK):
            here = pl.ds(start, BLOCK)
            spec_re, spec_im = spec[here, :freqs], spec[here, freqs:]
            real, imag = kernel_rows(k, start)
            filtered[here, :freqs] = real * spec_re - imag * spec_im
            filtered[here, freqs:] = real * spec_im + imag * spec_re
        result = plain(filtered[...], rows_v[...])
        sides[k, :freqs] = result.astype(HALF)
        sides[k, freqs:, :rows] = (-result[:, rows:]).astype(HALF)
        sides[k, freqs:, rows:] = result[:, :rows].astype(HALF)

    loop(count, make_rows)

    waits[needed].wait()

    def make_fields(k):
        fields[k] = plain(cols_t_v[...], sides[k]).astype(HALF)

    loop(count, make_fields)

    waits[needed + 1].wait()
    chunk = 32

    @pl.loop(0, wide // chunk, unroll=4)
    def make_sens(i):
        here = pl.ds(pl.multiple_of(i * chunk, chunk), chunk)
        low = pl.ds(pl.multiple_of(wide + i * chunk, chunk), chunk)
        target = target_ref[here]
        light = None
        for k in range(count):
            real, imag = fields[k, here, :rows].astype(FLOAT), fields[k, here, rows:].astype(FLOAT)
            power = real * real + imag * imag
            light = power if light is None else light + power
        if last:
            side = (i * chunk) // (wide // 2)
            place = pl.ds(pl.multiple_of(i * chunk - side * (wide // 2), chunk), chunk)

            @pl.when(side == core)
            def _():
                own_light[place] = light

            @pl.when(side != core)
            def _():
                other_light[place] = light.astype(HALF)

        sens = None
        for dose in range(dose_ref.shape[0]):
            factor = dose_ref[dose]
            level = jnp.tanh((0.5 * STEEPNESS * factor) * light - 0.5 * STEEPNESS * THRESHOLD)
            slope = (level - target) * (1.0 - level * level) * (0.25 * STEEPNESS * factor)
            sens = slope if sens is None else sens + slope
        for k in range(count):
            real = sens * fields[k, here, :rows].astype(FLOAT)
            imag = sens * fields[k, here, rows:].astype(FLOAT)
            cotangent[k, here, :rows] = real.astype(HALF)
            cotangent[k, here, rows:] = imag.astype(HALF)
            cotangent[k, low, :rows] = imag.astype(HALF)
            cotangent[k, low, rows:] = (-real).astype(HALF)

    waits[needed + 2].wait()
    waits[needed + 3].wait()

    def go_back(k):
        back[...] = plain(cols_v[...], cotangent[k]).astype(HALF)
        slopes = filtered_slopes(back, rows_t_v)
        for start in range(0, freqs, BLOCK):
            here = pl.ds(start, BLOCK)
            real, imag = (part.astype(FLOAT) for part in kernel_rows(k, start))
            slope_re, slope_im = slopes(start)
            total_re = real * slope_re + imag * slope_im
            total_im = real * slope_im - imag * slope_re
            if count > 2 or k > 0:
                total_re += total[here, :freqs]
                total_im += total[here, freqs:]
            total[here, :freqs] = total_re
            total[here, freqs:] = total_im

    def filtered_slopes(back, table):
        step = min(256, freqs)
        made = {}

        def at(start):
            first = start // step * step
            if first not in made:
                made.clear()
                made[first] = plain(back[first : first + step], table[...])
            part = made[first][start - first : start - first + BLOCK]
            return part[:, :freqs], part[:, freqs:]

        return at

    loop(count, go_back)

    turned[...] = plain(flip, total[:half].astype(HALF)).astype(HALF)
    half_spec[:, :freqs] = (total[half:, :freqs] + plain(turned[:, :freqs], mirror)).astype(HALF)
    half_spec[:, freqs : 2 * freqs] = (total[half:, freqs:] - plain(turned[:, freqs:], mirror)).astype(HALF)
    past_re = turned[:, :EXTRA][:, :1].astype(FLOAT)
    past_im = turned[:, freqs : freqs + EXTRA][:, :1].astype(FLOAT)
    lane = iotas(half, EXTRA)[1]
    extra = jnp.where(lane == 0, past_re, jnp.where(lane == 1, -past_im, 0.0))
    spread = spread_row(total[:1])
    lines = spread.shape[0]
    half_spec[:lines, 2 * freqs :] = (extra[:lines] + spread).astype(HALF)
    half_spec[lines:, 2 * freqs :] = extra[lines:].astype(HALF)
    write_blocks(half_spec, outs, me)


def print_kernel(index_ref, dose_ref, own_ref, other_ref, printed_ref):
    core = index_ref[2]
    cols = own_ref.shape[0]
    for focus, light_ref in ((core, own_ref), (1 - core, other_ref)):
        for start in range(0, cols, 128):
            light = light_ref[start : start + 128].astype(FLOAT).T
            for dose in range(dose_ref.shape[0]):
                level = jnp.tanh(0.5 * STEEPNESS * (dose_ref[dose] * light - THRESHOLD))
                printed_ref[focus, dose, :, start : start + 128] = 0.5 * level + 0.5


def body(kern_size, slab_size, mask_params, target_bits, kernels, weights, dose_factors):
    rows, cols = mask_params.shape
    freqs = kernels.shape[2]
    assert kernels.shape[0] == 1 and kern_size % FOCI == 0
    count = kern_size // FOCI
    wide = FOCI * cols
    sizes = {"kern": kern_size, "slab": slab_size}
    slab, kern = lax.axis_index("slab"), lax.axis_index("kern")
    rounds = plan_rounds(sizes)
    me = jnp.int32(0)
    for axis, bit in [("kern", 0)] + rounds[0]:
        me = 2 * me + (((kern if axis == "kern" else slab) >> bit) & 1)
    index = jnp.stack([slab, kern // FOCI, kern % FOCI, me]).astype(jnp.int32)
    tables = trig_tables(rows * slab_size, freqs)
    rows_all = jnp.asarray(row_blocks(tables, slab_size))
    cols_all = jnp.asarray(col_blocks(tables, count))

    smem = pl.BlockSpec(memory_space=pltpu.SMEM)
    vmem = pl.BlockSpec(memory_space=pltpu.VMEM)
    anywhere = pl.BlockSpec(memory_space=pl.ANY)
    hbm = pl.BlockSpec(memory_space=pltpu.HBM)
    compiler_params = pltpu.CompilerParams(vmem_limit_bytes=VMEM_LIMIT)
    members = 1 << len(rounds[0])
    parts_out = [jax.ShapeDtypeStruct((freqs // 4 // members, 2 * freqs + EXTRA), HALF)] * (2 * members)
    rows_n_like = ((2 * freqs + EXTRA, 2 * rows), HALF)
    rows_t_like = ((2 * rows, 2 * freqs + EXTRA), HALF)
    cols_n_like = ((freqs, 2 * wide), HALF)
    cols_t_like = ((wide, 2 * freqs), HALF)
    spec_like = ((freqs, 2 * freqs), HALF)
    half_like = ((freqs // 2, 2 * freqs + EXTRA), HALF)
    raw_rows_like = ((2, rows, freqs), FLOAT)
    dma = pltpu.SemaphoreType.DMA

    table_likes = [rows_n_like, rows_t_like, cols_n_like, cols_t_like, ((wide, rows), FLOAT)]
    rows_n, rows_t, cols_n, cols_t, target = pl.pallas_call(
        table_kernel,
        out_shape=[jax.ShapeDtypeStruct(*like) for like in table_likes],
        in_specs=[smem, hbm, hbm, anywhere],
        out_specs=[vmem] * 5,
        scratch_shapes=[
            pltpu.VMEM(*raw_rows_like),
            pltpu.VMEM((2, freqs, wide), FLOAT),
            pltpu.VMEM((rows, wide), jnp.int32),
            dma((3,)),
        ],
        compiler_params=pltpu.CompilerParams(vmem_limit_bytes=60 * 1024 * 1024),
        name="make_tables",
    )(index, rows_all, cols_all, target_bits)
    made = (rows_n, rows_t, cols_n, cols_t)

    begun = [jnp.swapaxes(kernels * jnp.sqrt(weights)[:, None, None, None], 2, 3).astype(HALF)]
    for bits in reversed(rounds[1:]):
        value = begun[0] if len(begun) == 1 else jnp.concatenate(begun, axis=0)
        begun = [value] + [partner(value, bits, p, sizes) for p in range(1, 1 << len(bits))]
    spectra = None
    order = [pair for bits in rounds for pair in bits]

    parts = pl.pallas_call(
        first_kernel,
        out_shape=parts_out,
        in_specs=[smem, vmem, hbm, hbm],
        out_specs=[vmem] * len(parts_out),
        scratch_shapes=[
            pltpu.VMEM(*raw_rows_like),
            pltpu.VMEM((2, freqs, cols), FLOAT),
            pltpu.VMEM(*rows_t_like),
            pltpu.VMEM((freqs, 2 * cols), HALF),
            pltpu.VMEM((freqs // 2, 2 * rows), HALF),
            pltpu.VMEM(*half_like),
            dma((2,)),
        ],
        compiler_params=compiler_params,
        name="first_spectrum",
    )(index, mask_params, rows_all, cols_all)

    params, printed = mask_params, None
    for step in range(STEPS):
        first, last = step == 0, step == STEPS - 1
        if first:
            def to_neighbours(pieces):
                value = jnp.concatenate(pieces, axis=0)
                return [value] + [partner(value, rounds[0], p, sizes) for p in (1, 2)], made, target

            parts, (spectra, made, target) = reduce_all(parts, rounds, sizes, begun, to_neighbours)
            cut = spectra[0].shape[0] // 2
            spectra = spectra + [
                partner(spectra[2][:cut], rounds[0], 1, sizes),
                partner(spectra[1][cut:], rounds[0], 2, sizes),
            ]
        else:
            parts, _ = reduce_all(parts, rounds, sizes)
        out_shape = list(parts_out)
        if last:
            lights = [jax.ShapeDtypeStruct((cols, rows), FLOAT), jax.ShapeDtypeStruct((cols, rows), HALF)]
            out_shape = lights + out_shape
        outs = pl.pallas_call(
            functools.partial(image_kernel, last, len(parts), order),
            out_shape=out_shape,
            in_specs=[smem, smem] + [hbm] * 5 + [anywhere] * (len(parts) + len(spectra)),
            out_specs=[vmem] * len(out_shape),
            scratch_shapes=[
                pltpu.VMEM((2 * freqs, 2 * rows), HALF),
                pltpu.VMEM((2 * rows, 2 * freqs), HALF),
                pltpu.VMEM(*cols_n_like),
                pltpu.VMEM(*cols_t_like),
                pltpu.VMEM((wide, rows), FLOAT),
                pltpu.VMEM((count * slab_size,) + kernels.shape[1:2] + (kernels.shape[3], freqs), HALF),
                pltpu.VMEM(*spec_like),
                pltpu.VMEM(*spec_like),
                pltpu.VMEM((count, 2 * freqs, 2 * rows), HALF),
                pltpu.VMEM((count, wide, 2 * rows), HALF),
                pltpu.VMEM((count, 2 * wide, 2 * rows), HALF),
                pltpu.VMEM((freqs, 2 * rows), HALF),
                pltpu.VMEM((freqs, 2 * freqs), FLOAT),
                pltpu.VMEM(*half_like),
                pltpu.VMEM((freqs // 2, 2 * freqs), HALF),
                dma((len(parts) + 5 + len(spectra),)),
            ],
            compiler_params=compiler_params,
            name="image_and_back",
        )(
            index,
            dose_factors,
            *made,
            target,
            *parts,
            *spectra,
        )
        parts = outs[-len(parts) :]
        if last:
            printed = pl.pallas_call(
                print_kernel,
                out_shape=jax.ShapeDtypeStruct((FOCI, dose_factors.shape[0], rows, cols), FLOAT),
                in_specs=[smem, smem, vmem, vmem],
                out_specs=vmem,
                compiler_params=compiler_params,
                name="print_resist",
            )(index, dose_factors, outs[0], partner(outs[1], [("kern", 0)], 1, sizes))
        shown = printed
        parts, printed = reduce_all(parts, rounds, sizes, None, (lambda _: shown) if last else None)
        tile = jax.ShapeDtypeStruct((rows, cols) if last else (cols, rows), FLOAT)
        common = [pltpu.VMEM(*rows_n_like), pltpu.VMEM((cols, 2 * freqs), HALF)]
        work = [pltpu.VMEM(*half_like), pltpu.VMEM((2 * freqs, rows), HALF)]
        if last:
            scratch = common + work + [dma((len(parts) + 2,))]
        else:
            scratch = common[:1] + [pltpu.VMEM(*rows_t_like)] + common[1:]
            scratch += [pltpu.VMEM((freqs, 2 * cols), HALF)] + work
            scratch += [pltpu.VMEM((freqs // 2, 2 * rows), HALF), dma((len(parts) + 5,))]
        outs = pl.pallas_call(
            functools.partial(update_kernel, first, last, len(parts)),
            out_shape=[tile] if last else [tile] + parts_out,
            in_specs=[smem, vmem] + [hbm] * 4 + [anywhere] * len(parts),
            out_specs=[vmem] * (1 if last else 1 + len(parts)),
            scratch_shapes=scratch,
            compiler_params=compiler_params,
            name="update",
        )(index, params, *made, *parts)
        params = outs[0]
        if not last:
            parts = outs[1:]
    return (params, printed)


def solution(mesh):
    sizes = dict(mesh.shape)
    in_specs = (P("slab", "kern"), P("slab", None), P("kern", None, None, "slab"), P("kern"), P())
    out_specs = (P("slab", "kern"), P(None, None, "slab", "kern"))
    return jax.shard_map(
        functools.partial(body, sizes["kern"], sizes["slab"]),
        mesh=mesh,
        in_specs=in_specs,
        out_specs=out_specs,
        check_vma=False,
    )
```

```python
import functools

import jax
import jax.numpy as jnp
import numpy as np
from jax import lax
from jax.experimental import pallas as pl
from jax.experimental.pallas import tpu as pltpu
from jax.sharding import PartitionSpec as P

FOCI = 2
STEPS = 2
STEEPNESS = 3.0
THRESHOLD = 1.0
STEP_RATE = 0.4
BLOCK = 16
EXTRA = 128
SPREAD = 64
VMEM_LIMIT = 50 * 1024 * 1024
FLOAT = jnp.float32
HALF = jnp.bfloat16
AXES = ("kern", "slab")


def plain(left, right):
    return jnp.dot(left, right, preferred_element_type=FLOAT)


def trig_tables(pixels, freqs):
    phases = ((np.arange(freqs) - freqs // 2)[:, None] * np.arange(pixels)[None, :]) % pixels
    angles = phases.astype(np.float32) * np.float32(2.0 * np.pi / pixels)
    scale = np.float32(1.0 / np.sqrt(pixels))
    cosine = (np.cos(angles.astype(np.float64)).astype(np.float32) * scale).astype(HALF)
    sine = (np.sin(angles.astype(np.float64)).astype(np.float32) * scale).astype(HALF)
    return np.stack([cosine.astype(np.float32), sine.astype(np.float32)])


def row_blocks(tables, parts):
    _, freqs, pixels = tables.shape
    split = tables.transpose(0, 2, 1).reshape(2, parts, pixels // parts, freqs)
    return np.ascontiguousarray(split.transpose(1, 0, 2, 3))


def col_blocks(tables, parts):
    _, freqs, pixels = tables.shape
    split = tables.reshape(2, freqs, parts, pixels // parts)
    return np.ascontiguousarray(split.transpose(2, 0, 1, 3))


def flat_index(kern, slab, sizes):
    return kern * sizes["slab"] + slab


def plan_rounds(sizes):
    kern_bits = [("kern", bit) for bit in range(1, sizes["kern"].bit_length() - 1)]
    slab_bits = [("slab", bit) for bit in range(sizes["slab"].bit_length() - 1)]
    rounds = [kern_bits[:1] + slab_bits[:1], slab_bits[1:3], kern_bits[1:3], slab_bits[3:]]
    return [bits for bits in rounds if bits]


def partner(values, bits, place, sizes):
    shift = {"kern": 0, "slab": 0}
    for i, (axis, bit) in enumerate(bits):
        if (place >> (len(bits) - 1 - i)) & 1:
            shift[axis] |= 1 << bit
    mask = flat_index(shift["kern"], shift["slab"], sizes)
    total = sizes["kern"] * sizes["slab"]
    return lax.ppermute(values, AXES, [(i, i ^ mask) for i in range(total)])


def add_all(pieces):
    total = pieces[0].astype(FLOAT)
    for piece in pieces[1:]:
        total = total + piece.astype(FLOAT)
    return total.astype(HALF)


def tied(values, others):
    return lax.optimization_barrier((values, others))


def reduce_all(parts, rounds, sizes, early=None, late=None):
    core = [("kern", 0)]
    count = len(parts) // 2
    parts = [add_all([mine, partner(other, core, 1, sizes)]) for mine, other in zip(parts[:count], parts[count:])]
    others = [partner(parts[p], rounds[0], p, sizes) for p in range(1, count)]
    if early is not None:
        others, early = tied(others, early)
    total = add_all([parts[0]] + others)
    for bits in rounds[1:]:
        others = [partner(total, bits, p, sizes) for p in range(1, 1 << len(bits))]
        if late is not None and bits is rounds[1]:
            others, late = tied(others, late(early))
        total = add_all([total] + others)
    pieces = [total] + [partner(total, rounds[0], p, sizes) for p in range(1, count)]
    return pieces + [partner(piece, core, 1, sizes) for piece in pieces], late


def start_together(copies, whole, sem):
    for source, target in copies:
        pltpu.make_async_copy(source, target, sem).start()
    return pltpu.make_async_copy(whole, whole, sem)


def start_all(copies, sems):
    started = [pltpu.make_async_copy(source, target, sems.at[i]) for i, (source, target) in enumerate(copies)]
    for copy in started:
        copy.start()
    return started


def piece_copies(pieces, spec, me):
    size = pieces[0].shape[0]
    return [
        (piece, spec.at[pl.ds(pl.multiple_of((place ^ me) * size, size), size)]) for place, piece in enumerate(pieces)
    ]


def iotas(rows, cols):
    shape = (rows, cols)
    return lax.broadcasted_iota(jnp.int32, shape, 0), lax.broadcasted_iota(jnp.int32, shape, 1)


def ones_where(condition):
    return jnp.where(condition, 1.0, 0.0).astype(HALF)


def anti_diagonal(size, total):
    row, lane = iotas(size, size)
    return ones_where(row + lane == total)


def spread_row(line):
    width = line.shape[1]
    row, lane = iotas(width // SPREAD, width)
    masked = jnp.where(lane // SPREAD == row, line, 0.0).astype(HALF)
    row, lane = iotas(width, EXTRA)
    return plain(masked, ones_where(lane == row % SPREAD + SPREAD))


def collect_rows(extra, width):
    row, lane = iotas(EXTRA, width)
    wide = plain(extra, ones_where(row == lane % SPREAD + SPREAD))
    row, lane = iotas(extra.shape[0], width)
    return jnp.where(lane // SPREAD == row, wide, 0.0)


def write_blocks(source, outs, me):
    for place, out in enumerate(outs):
        size = out.shape[0]
        out[...] = source[pl.ds(pl.multiple_of((place ^ me) * size, size), size)].astype(HALF)


def spectrum_of(mask_low, rows_t, cols_ref, col_spec, total):
    cols, rows = mask_low.shape
    half = total.shape[0]
    width = 4 * half
    col_spec[:, :rows] = plain(cols_ref[half:, :cols], mask_low).astype(HALF)
    col_spec[:, rows:] = (-plain(cols_ref[half:, cols:], mask_low)).astype(HALF)
    edge_re = plain(cols_ref[:BLOCK, :cols], mask_low).astype(HALF)
    edge_im = (-plain(cols_ref[:BLOCK, cols:], mask_low)).astype(HALF)
    edge = plain(edge_re, rows_t[:rows, :width]) + plain(edge_im, rows_t[rows:, :width])
    total[:, :width] = plain(col_spec[...], rows_t[:, :width]).astype(HALF)
    extra = plain(col_spec[...], rows_t[:, width:])
    spread = spread_row(edge[:1])
    count = spread.shape[0]
    total[:count, width:] = (extra[:count] + spread).astype(HALF)
    total[count:, width:] = extra[count:].astype(HALF)


def fill_rows_t(raw, rows_t):
    rows, freqs = raw.shape[1:]
    rows_t[:rows, :freqs] = raw[0].astype(HALF)
    rows_t[:rows, freqs : 2 * freqs] = (-raw[1]).astype(HALF)
    rows_t[rows:, :freqs] = raw[1].astype(HALF)
    rows_t[rows:, freqs : 2 * freqs] = raw[0].astype(HALF)
    lane = iotas(rows, EXTRA)[1]
    cosine, sine = raw[0, :, :1], -raw[1, :, :1]
    zero = jnp.zeros((rows, EXTRA), FLOAT)
    rows_t[:rows, 2 * freqs :] = jnp.where(lane == 0, cosine, jnp.where(lane == 1, -sine, zero)).astype(HALF)
    rows_t[rows:, 2 * freqs :] = jnp.where(lane == 0, sine, jnp.where(lane == 1, cosine, zero)).astype(HALF)


def first_kernel(index_ref, params_ref, rows_all, cols_all, *rest):
    outs, scratch = rest[:-7], rest[-7:]
    raw_rows, raw_cols, rows_t, cols_ref, col_spec, total, sems = scratch
    slab, pair, core, me = (index_ref[i] for i in range(4))
    cols = params_ref.shape[1]
    own = pl.ds(pl.multiple_of(core * cols, cols), cols)
    waits = start_all([(cols_all.at[pair, :, :, own], raw_cols), (rows_all.at[slab], raw_rows)], sems)
    mask_low = jnp.tanh(params_ref[...]).T.astype(HALF)
    waits[0].wait()
    cols_ref[:, :cols] = raw_cols[0].astype(HALF)
    cols_ref[:, cols:] = raw_cols[1].astype(HALF)
    waits[1].wait()
    fill_rows_t(raw_rows, rows_t)
    spectrum_of(mask_low, rows_t, cols_ref, col_spec, total)
    write_blocks(total, outs, me)


def table_kernel(index_ref, rows_all, cols_all, target_all, *rest):
    rows_n, rows_t, cols_n, cols_t, target_ref, raw_rows, raw_cols, raw_target, sems = rest
    slab, pair = index_ref[0], index_ref[1]
    rows, freqs = raw_rows.shape[1:]
    wide = raw_cols.shape[2]
    here = pl.ds(pl.multiple_of(pair * wide, wide), wide)
    waits = start_all(
        [(rows_all.at[slab], raw_rows), (cols_all.at[pair], raw_cols), (target_all.at[:, here], raw_target)], sems
    )
    waits[0].wait()
    fill_rows_t(raw_rows, rows_t)
    cosine, sine = raw_rows[0].T, raw_rows[1].T
    rows_n[:freqs, :rows] = cosine.astype(HALF)
    rows_n[:freqs, rows:] = sine.astype(HALF)
    rows_n[freqs : 2 * freqs, :rows] = (-sine).astype(HALF)
    rows_n[freqs : 2 * freqs, rows:] = cosine.astype(HALF)
    line = iotas(EXTRA, rows)[0]
    first, second = cosine[:1], -sine[:1]
    zero = jnp.zeros((EXTRA, rows), FLOAT)
    rows_n[2 * freqs :, :rows] = jnp.where(line == 0, first, jnp.where(line == 1, -second, zero)).astype(HALF)
    rows_n[2 * freqs :, rows:] = jnp.where(line == 0, second, jnp.where(line == 1, first, zero)).astype(HALF)
    waits[1].wait()
    for part in range(2):
        cols_n[:, part * wide : (part + 1) * wide] = raw_cols[part].astype(HALF)
        for start in range(0, wide, 128):
            some = raw_cols[part, :, start : start + 128].T
            cols_t[start : start + 128, part * freqs : (part + 1) * freqs] = some.astype(HALF)
    waits[2].wait()
    for start in range(0, wide, 128):
        target_ref[start : start + 128] = (2 * raw_target[:, start : start + 128] - 1).astype(FLOAT).T


def update_kernel(first, last, count, index_ref, params_ref, rows_n, rows_t, cols_n, cols_t, *rest):
    pieces, rest = rest[:count], rest[count:]
    if last:
        new_ref, rows_v, cols_v, spec, back, sems = rest
    else:
        new_ref, outs, scratch = rest[0], rest[1 : 1 + count], rest[1 + count :]
        rows_v, rows_t_v, cols_v, cols_n_v, spec, back, col_spec, sems = scratch
    core, me = index_ref[2], index_ref[3]
    params = params_ref[...].T if first else params_ref[...]
    cols, rows = params.shape
    half = spec.shape[0]
    freqs = 2 * half
    here = pl.ds(pl.multiple_of(core * cols, cols), cols)
    arrival = start_together(piece_copies(pieces, spec, me), spec, sems.at[0])
    copies = [(rows_n, rows_v), (cols_t.at[here], cols_v)]
    if not last:
        wide = cols_n.shape[1] // 2
        copies += [
            (rows_t, rows_t_v),
            (cols_n.at[:, here], cols_n_v.at[:, :cols]),
            (cols_n.at[:, pl.ds(pl.multiple_of(wide + core * cols, cols), cols)], cols_n_v.at[:, cols:]),
        ]
    waits = start_all(copies, sems.at[1:])
    back[...] = jnp.zeros_like(back)
    arrival.wait()
    waits[0].wait()
    result = plain(spec[...], rows_v[...])
    back[half:freqs] = result[:, :rows].astype(HALF)
    back[freqs + half :] = (-result[:, rows:]).astype(HALF)
    edge = collect_rows(spec[: 2 * freqs // SPREAD, 2 * freqs :], 2 * freqs).astype(HALF)
    edge = jnp.sum(plain(edge, rows_v[: 2 * freqs]), axis=0, keepdims=True)
    line = iotas(BLOCK, rows)[0]
    back[:BLOCK] = jnp.where(line == 0, edge[:, :rows], 0.0).astype(HALF)
    back[freqs : freqs + BLOCK] = jnp.where(line == 0, -edge[:, rows:], 0.0).astype(HALF)
    waits[1].wait()
    gradient = plain(cols_v[...], back[...])
    mask = jnp.tanh(params)
    params = params - STEP_RATE * gradient * (1.0 - mask * mask)
    if last:
        new_ref[...] = params.T
    else:
        new_ref[...] = params
        for i in range(2, len(waits)):
            waits[i].wait()
        spectrum_of(jnp.tanh(params).astype(HALF), rows_t_v, cols_n_v, col_spec, spec)
        write_blocks(spec, outs, me)


def loop(count, step):
    if count <= 2:
        for i in range(count):
            step(i)
    else:
        pl.loop(0, count)(step)


def image_kernel(last, parts, order, index_ref, dose_ref, rows_n, rows_t, cols_n, cols_t, target_all, *rest):
    spec_pieces, rest = rest[:parts], rest[parts:]
    outs = rest[-16 - parts - (2 if last else 0) : -16]
    spectra = rest[: -16 - len(outs)]
    scratch = rest[-16:]
    rows_v, rows_t_v, cols_v, cols_t_v, target_ref, kern_ref, spec = scratch[:7]
    filtered, sides, fields, cotangent, back, total, half_spec, turned, sems = scratch[7:]
    if last:
        own_light, other_light, outs = outs[0], outs[1], outs[2:]
    slab, core, me = index_ref[0], index_ref[2], index_ref[3]
    wide, rows = target_ref.shape
    count, freqs = fields.shape[0], spec.shape[0]
    width = kern_ref.shape[2]

    def kernel_rows(k, start):
        part = slab ^ (start // width)
        place = 0
        for axis, bit in order:
            place = 2 * place + (((k >> (bit - 1)) & 1) if axis == "kern" else ((part >> bit) & 1))
        here = pl.ds(start % width, BLOCK)
        return kern_ref[place, 0, here].astype(FLOAT), kern_ref[place, 1, here].astype(FLOAT)

    arrival = start_together(piece_copies(spec_pieces, half_spec, me), half_spec, sems.at[0])
    copies = []
    filled = 0
    for piece in spectra:
        copies.append((piece, kern_ref.at[filled : filled + piece.shape[0]]))
        filled += piece.shape[0]
    spectra_here = start_together(copies, kern_ref, sems.at[1])
    copies = [(rows_n.at[: 2 * freqs], rows_v), (cols_t, cols_t_v), (target_all, target_ref), (cols_n, cols_v), (rows_t.at[:, : 2 * freqs], rows_t_v)]
    waits = start_all(copies, sems.at[2:])
    if count > 2:
        total[...] = jnp.zeros_like(total)
    arrival.wait()

    half = freqs // 2
    mirror = anti_diagonal(freqs, freqs)
    flip = anti_diagonal(half, half)
    spec[half:] = half_spec[:, : 2 * freqs]
    lane = iotas(half, freqs)[1]
    past_re = half_spec[:, 2 * freqs : 2 * freqs + EXTRA][:, :1].astype(FLOAT)
    past_im = half_spec[:, 2 * freqs : 2 * freqs + EXTRA][:, 1:2].astype(FLOAT)
    turned[:, :freqs] = jnp.where(lane == 0, past_re, plain(half_spec[:, :freqs], mirror)).astype(HALF)
    turned[:, freqs:] = jnp.where(lane == 0, -past_im, -plain(half_spec[:, freqs : 2 * freqs], mirror)).astype(HALF)
    edge = collect_rows(half_spec[: 2 * freqs // SPREAD, 2 * freqs :], 2 * freqs)
    edge = jnp.sum(edge, axis=0, keepdims=True)
    line = iotas(half, 2 * freqs)[0]
    spec[:half] = jnp.where(line == 0, edge, plain(flip, turned[...])).astype(HALF)
    spectra_here.wait()
    waits[0].wait()

    def make_rows(k):
        for start in range(0, freqs, BLOCK):
            here = pl.ds(start, BLOCK)
            spec_re, spec_im = spec[here, :freqs].astype(FLOAT), spec[here, freqs:].astype(FLOAT)
            real, imag = kernel_rows(k, start)
            filtered[here, :freqs] = (real * spec_re - imag * spec_im).astype(HALF)
            filtered[here, freqs:] = (real * spec_im + imag * spec_re).astype(HALF)
        result = plain(filtered[...], rows_v[...])
        sides[k, :freqs] = result.astype(HALF)
        sides[k, freqs:, :rows] = (-result[:, rows:]).astype(HALF)
        sides[k, freqs:, rows:] = result[:, :rows].astype(HALF)

    loop(count, make_rows)

    waits[1].wait()

    def make_fields(k):
        fields[k] = plain(cols_t_v[...], sides[k])

    loop(count, make_fields)

    waits[2].wait()
    chunk = 32

    @pl.loop(0, wide // chunk, unroll=4)
    def make_sens(i):
        here = pl.ds(pl.multiple_of(i * chunk, chunk), chunk)
        low = pl.ds(pl.multiple_of(wide + i * chunk, chunk), chunk)
        target = target_ref[here]
        light = None
        for k in range(count):
            real, imag = fields[k, here, :rows], fields[k, here, rows:]
            power = real * real + imag * imag
            light = power if light is None else light + power
        if last:
            side = (i * chunk) // (wide // 2)
            place = pl.ds(pl.multiple_of(i * chunk - side * (wide // 2), chunk), chunk)

            @pl.when(side == core)
            def _():
                own_light[place] = light

            @pl.when(side != core)
            def _():
                other_light[place] = light.astype(HALF)

        sens = None
        for dose in range(dose_ref.shape[0]):
            factor = dose_ref[dose]
            level = jnp.tanh((0.5 * STEEPNESS * factor) * light - 0.5 * STEEPNESS * THRESHOLD)
            slope = (level - target) * (1.0 - level * level) * (0.25 * STEEPNESS * factor)
            sens = slope if sens is None else sens + slope
        for k in range(count):
            real = sens * fields[k, here, :rows]
            imag = sens * fields[k, here, rows:]
            cotangent[k, here, :rows] = real.astype(HALF)
            cotangent[k, here, rows:] = imag.astype(HALF)
            cotangent[k, low, :rows] = imag.astype(HALF)
            cotangent[k, low, rows:] = (-real).astype(HALF)

    waits[3].wait()
    waits[4].wait()

    def go_back(k):
        back[...] = plain(cols_v[...], cotangent[k]).astype(HALF)
        slopes = filtered_slopes(back, rows_t_v)
        for start in range(0, freqs, BLOCK):
            here = pl.ds(start, BLOCK)
            real, imag = kernel_rows(k, start)
            slope_re, slope_im = slopes(start)
            total_re = real * slope_re + imag * slope_im
            total_im = real * slope_im - imag * slope_re
            if count > 2 or k > 0:
                total_re += total[here, :freqs]
                total_im += total[here, freqs:]
            total[here, :freqs] = total_re
            total[here, freqs:] = total_im

    def filtered_slopes(back, table):
        step = min(256, freqs)
        made = {}

        def at(start):
            first = start // step * step
            if first not in made:
                made.clear()
                made[first] = plain(back[first : first + step], table[...])
            part = made[first][start - first : start - first + BLOCK]
            return part[:, :freqs], part[:, freqs:]

        return at

    loop(count, go_back)

    turned[...] = plain(flip, total[:half].astype(HALF)).astype(HALF)
    half_spec[:, :freqs] = (total[half:, :freqs] + plain(turned[:, :freqs], mirror)).astype(HALF)
    half_spec[:, freqs : 2 * freqs] = (total[half:, freqs:] - plain(turned[:, freqs:], mirror)).astype(HALF)
    past_re = turned[:, :EXTRA][:, :1].astype(FLOAT)
    past_im = turned[:, freqs : freqs + EXTRA][:, :1].astype(FLOAT)
    lane = iotas(half, EXTRA)[1]
    extra = jnp.where(lane == 0, past_re, jnp.where(lane == 1, -past_im, 0.0))
    spread = spread_row(total[:1])
    lines = spread.shape[0]
    half_spec[:lines, 2 * freqs :] = (extra[:lines] + spread).astype(HALF)
    half_spec[lines:, 2 * freqs :] = extra[lines:].astype(HALF)
    write_blocks(half_spec, outs, me)


def print_kernel(index_ref, dose_ref, own_ref, other_ref, printed_ref):
    core = index_ref[2]
    cols = own_ref.shape[0]
    for focus, light_ref in ((core, own_ref), (1 - core, other_ref)):
        for start in range(0, cols, 128):
            light = light_ref[start : start + 128].astype(FLOAT).T
            for dose in range(dose_ref.shape[0]):
                level = jnp.tanh(0.5 * STEEPNESS * (dose_ref[dose] * light - THRESHOLD))
                printed_ref[focus, dose, :, start : start + 128] = 0.5 * level + 0.5


def body(kern_size, slab_size, mask_params, target_bits, kernels, weights, dose_factors):
    rows, cols = mask_params.shape
    freqs = kernels.shape[2]
    assert kernels.shape[0] == 1 and kern_size % FOCI == 0
    count = kern_size // FOCI
    wide = FOCI * cols
    sizes = {"kern": kern_size, "slab": slab_size}
    slab, kern = lax.axis_index("slab"), lax.axis_index("kern")
    rounds = plan_rounds(sizes)
    me = jnp.int32(0)
    for axis, bit in [("kern", 0)] + rounds[0]:
        me = 2 * me + (((kern if axis == "kern" else slab) >> bit) & 1)
    index = jnp.stack([slab, kern // FOCI, kern % FOCI, me]).astype(jnp.int32)
    tables = trig_tables(rows * slab_size, freqs)
    rows_all = jnp.asarray(row_blocks(tables, slab_size))
    cols_all = jnp.asarray(col_blocks(tables, count))

    smem = pl.BlockSpec(memory_space=pltpu.SMEM)
    vmem = pl.BlockSpec(memory_space=pltpu.VMEM)
    anywhere = pl.BlockSpec(memory_space=pl.ANY)
    hbm = pl.BlockSpec(memory_space=pltpu.HBM)
    compiler_params = pltpu.CompilerParams(vmem_limit_bytes=VMEM_LIMIT)
    members = 1 << len(rounds[0])
    parts_out = [jax.ShapeDtypeStruct((freqs // 4 // members, 2 * freqs + EXTRA), HALF)] * (2 * members)
    rows_n_like = ((2 * freqs + EXTRA, 2 * rows), HALF)
    rows_t_like = ((2 * rows, 2 * freqs + EXTRA), HALF)
    cols_n_like = ((freqs, 2 * wide), HALF)
    cols_t_like = ((wide, 2 * freqs), HALF)
    spec_like = ((freqs, 2 * freqs), HALF)
    half_like = ((freqs // 2, 2 * freqs + EXTRA), HALF)
    raw_rows_like = ((2, rows, freqs), FLOAT)
    dma = pltpu.SemaphoreType.DMA

    table_likes = [rows_n_like, rows_t_like, cols_n_like, cols_t_like, ((wide, rows), FLOAT)]
    rows_n, rows_t, cols_n, cols_t, target = pl.pallas_call(
        table_kernel,
        out_shape=[jax.ShapeDtypeStruct(*like) for like in table_likes],
        in_specs=[smem, hbm, hbm, anywhere],
        out_specs=[vmem] * 5,
        scratch_shapes=[
            pltpu.VMEM(*raw_rows_like),
            pltpu.VMEM((2, freqs, wide), FLOAT),
            pltpu.VMEM((rows, wide), jnp.int32),
            dma((3,)),
        ],
        compiler_params=pltpu.CompilerParams(vmem_limit_bytes=60 * 1024 * 1024),
        name="make_tables",
    )(index, rows_all, cols_all, target_bits)
    made = (rows_n, rows_t, cols_n, cols_t)

    begun = [jnp.swapaxes(kernels * jnp.sqrt(weights)[:, None, None, None], 2, 3).astype(HALF)]
    for bits in reversed(rounds[1:]):
        value = begun[0] if len(begun) == 1 else jnp.concatenate(begun, axis=0)
        begun = [value] + [partner(value, bits, p, sizes) for p in range(1, 1 << len(bits))]
    spectra = None
    order = [pair for bits in rounds for pair in bits]

    parts = pl.pallas_call(
        first_kernel,
        out_shape=parts_out,
        in_specs=[smem, vmem, hbm, hbm],
        out_specs=[vmem] * len(parts_out),
        scratch_shapes=[
            pltpu.VMEM(*raw_rows_like),
            pltpu.VMEM((2, freqs, cols), FLOAT),
            pltpu.VMEM(*rows_t_like),
            pltpu.VMEM((freqs, 2 * cols), HALF),
            pltpu.VMEM((freqs // 2, 2 * rows), HALF),
            pltpu.VMEM(*half_like),
            dma((2,)),
        ],
        compiler_params=compiler_params,
        name="first_spectrum",
    )(index, mask_params, rows_all, cols_all)

    params, printed = mask_params, None
    for step in range(STEPS):
        first, last = step == 0, step == STEPS - 1
        if first:
            def to_neighbours(pieces):
                value = jnp.concatenate(pieces, axis=0)
                return [value] + [partner(value, rounds[0], p, sizes) for p in (1, 2)], made, target

            parts, (spectra, made, target) = reduce_all(parts, rounds, sizes, begun, to_neighbours)
            cut = spectra[0].shape[0] // 2
            spectra = spectra + [
                partner(spectra[2][:cut], rounds[0], 1, sizes),
                partner(spectra[1][cut:], rounds[0], 2, sizes),
            ]
        else:
            parts, _ = reduce_all(parts, rounds, sizes)
        out_shape = list(parts_out)
        if last:
            lights = [jax.ShapeDtypeStruct((cols, rows), FLOAT), jax.ShapeDtypeStruct((cols, rows), HALF)]
            out_shape = lights + out_shape
        outs = pl.pallas_call(
            functools.partial(image_kernel, last, len(parts), order),
            out_shape=out_shape,
            in_specs=[smem, smem] + [hbm] * 5 + [anywhere] * (len(parts) + len(spectra)),
            out_specs=[vmem] * len(out_shape),
            scratch_shapes=[
                pltpu.VMEM((2 * freqs, 2 * rows), HALF),
                pltpu.VMEM((2 * rows, 2 * freqs), HALF),
                pltpu.VMEM(*cols_n_like),
                pltpu.VMEM(*cols_t_like),
                pltpu.VMEM((wide, rows), FLOAT),
                pltpu.VMEM((count * slab_size,) + kernels.shape[1:2] + (kernels.shape[3], freqs), HALF),
                pltpu.VMEM(*spec_like),
                pltpu.VMEM(*spec_like),
                pltpu.VMEM((count, 2 * freqs, 2 * rows), HALF),
                pltpu.VMEM((count, wide, 2 * rows), FLOAT),
                pltpu.VMEM((count, 2 * wide, 2 * rows), HALF),
                pltpu.VMEM((freqs, 2 * rows), HALF),
                pltpu.VMEM((freqs, 2 * freqs), FLOAT),
                pltpu.VMEM(*half_like),
                pltpu.VMEM((freqs // 2, 2 * freqs), HALF),
                dma((7,)),
            ],
            compiler_params=compiler_params,
            name="image_and_back",
        )(
            index,
            dose_factors,
            *made,
            target,
            *parts,
            *spectra,
        )
        parts = outs[-len(parts) :]
        if last:
            printed = pl.pallas_call(
                print_kernel,
                out_shape=jax.ShapeDtypeStruct((FOCI, dose_factors.shape[0], rows, cols), FLOAT),
                in_specs=[smem, smem, vmem, vmem],
                out_specs=vmem,
                compiler_params=compiler_params,
                name="print_resist",
            )(index, dose_factors, outs[0], partner(outs[1], [("kern", 0)], 1, sizes))
        shown = printed
        parts, printed = reduce_all(parts, rounds, sizes, None, (lambda _: shown) if last else None)
        tile = jax.ShapeDtypeStruct((rows, cols) if last else (cols, rows), FLOAT)
        common = [pltpu.VMEM(*rows_n_like), pltpu.VMEM((cols, 2 * freqs), HALF)]
        work = [pltpu.VMEM(*half_like), pltpu.VMEM((2 * freqs, rows), HALF)]
        if last:
            scratch = common + work + [dma((3,))]
        else:
            scratch = common[:1] + [pltpu.VMEM(*rows_t_like)] + common[1:]
            scratch += [pltpu.VMEM((freqs, 2 * cols), HALF)] + work
            scratch += [pltpu.VMEM((freqs // 2, 2 * rows), HALF), dma((6,))]
        outs = pl.pallas_call(
            functools.partial(update_kernel, first, last, len(parts)),
            out_shape=[tile] if last else [tile] + parts_out,
            in_specs=[smem, vmem] + [hbm] * 4 + [anywhere] * len(parts),
            out_specs=[vmem] * (1 if last else 1 + len(parts)),
            scratch_shapes=scratch,
            compiler_params=compiler_params,
            name="update",
        )(index, params, *made, *parts)
        params = outs[0]
        if not last:
            parts = outs[1:]
    return (params, printed)


def solution(mesh):
    sizes = dict(mesh.shape)
    in_specs = (P("slab", "kern"), P("slab", None), P("kern", None, None, "slab"), P("kern"), P())
    out_specs = (P("slab", "kern"), P(None, None, "slab", "kern"))
    return jax.shard_map(
        functools.partial(body, sizes["kern"], sizes["slab"]),
        mesh=mesh,
        in_specs=in_specs,
        out_specs=out_specs,
        check_vma=False,
    )
```

```python
import functools

import jax
import jax.numpy as jnp
import numpy as np
from jax import lax
from jax.experimental import pallas as pl
from jax.experimental.pallas import tpu as pltpu
from jax.sharding import PartitionSpec as P

FOCI = 2
STEPS = 2
STEEPNESS = 3.0
THRESHOLD = 1.0
STEP_RATE = 0.4
BLOCK = 16
EXTRA = 128
SPREAD = 64
VMEM_LIMIT = 50 * 1024 * 1024
FLOAT = jnp.float32
HALF = jnp.bfloat16
AXES = ("kern", "slab")


def plain(left, right):
    return jnp.dot(left, right, preferred_element_type=FLOAT)


def trig_tables(pixels, freqs):
    phases = ((np.arange(freqs) - freqs // 2)[:, None] * np.arange(pixels)[None, :]) % pixels
    angles = phases.astype(np.float32) * np.float32(2.0 * np.pi / pixels)
    scale = np.float32(1.0 / np.sqrt(pixels))
    cosine = (np.cos(angles.astype(np.float64)).astype(np.float32) * scale).astype(HALF)
    sine = (np.sin(angles.astype(np.float64)).astype(np.float32) * scale).astype(HALF)
    return np.stack([cosine.astype(np.float32), sine.astype(np.float32)])


def row_blocks(tables, parts):
    _, freqs, pixels = tables.shape
    split = tables.transpose(0, 2, 1).reshape(2, parts, pixels // parts, freqs)
    return np.ascontiguousarray(split.transpose(1, 0, 2, 3))


def col_blocks(tables, parts):
    _, freqs, pixels = tables.shape
    split = tables.reshape(2, freqs, parts, pixels // parts)
    return np.ascontiguousarray(split.transpose(2, 0, 1, 3))


def flat_index(kern, slab, sizes):
    return kern * sizes["slab"] + slab


def plan_rounds(sizes):
    kern_bits = [("kern", bit) for bit in range(1, sizes["kern"].bit_length() - 1)]
    slab_bits = [("slab", bit) for bit in range(sizes["slab"].bit_length() - 1)]
    rounds = [kern_bits[:1] + slab_bits[:1], slab_bits[1:3], kern_bits[1:3], slab_bits[3:]]
    return [bits for bits in rounds if bits]


def partner(values, bits, place, sizes):
    shift = {"kern": 0, "slab": 0}
    for i, (axis, bit) in enumerate(bits):
        if (place >> (len(bits) - 1 - i)) & 1:
            shift[axis] |= 1 << bit
    mask = flat_index(shift["kern"], shift["slab"], sizes)
    total = sizes["kern"] * sizes["slab"]
    return lax.ppermute(values, AXES, [(i, i ^ mask) for i in range(total)])


def add_all(pieces):
    total = pieces[0].astype(FLOAT)
    for piece in pieces[1:]:
        total = total + piece.astype(FLOAT)
    return total.astype(HALF)


def tied(values, others):
    return lax.optimization_barrier((values, others))


def reduce_all(parts, rounds, sizes, early=None, late=None):
    core = [("kern", 0)]
    count = len(parts) // 2
    parts = [add_all([mine, partner(other, core, 1, sizes)]) for mine, other in zip(parts[:count], parts[count:])]
    others = [partner(parts[p], rounds[0], p, sizes) for p in range(1, count)]
    if early is not None:
        others, early = tied(others, early)
    total = add_all([parts[0]] + others)
    for bits in rounds[1:]:
        others = [partner(total, bits, p, sizes) for p in range(1, 1 << len(bits))]
        if late is not None and bits is rounds[1]:
            others, late = tied(others, late(early))
        total = add_all([total] + others)
    pieces = [total] + [partner(total, rounds[0], p, sizes) for p in range(1, count)]
    return pieces + [partner(piece, core, 1, sizes) for piece in pieces], late


def start_together(copies, whole, sem):
    for source, target in copies:
        pltpu.make_async_copy(source, target, sem).start()
    return pltpu.make_async_copy(whole, whole, sem)


def start_all(copies, sems):
    started = [pltpu.make_async_copy(source, target, sems.at[i]) for i, (source, target) in enumerate(copies)]
    for copy in started:
        copy.start()
    return started


def piece_copies(pieces, spec, me):
    size = pieces[0].shape[0]
    return [
        (piece, spec.at[pl.ds(pl.multiple_of((place ^ me) * size, size), size)]) for place, piece in enumerate(pieces)
    ]


def iotas(rows, cols):
    shape = (rows, cols)
    return lax.broadcasted_iota(jnp.int32, shape, 0), lax.broadcasted_iota(jnp.int32, shape, 1)


def ones_where(condition):
    return jnp.where(condition, 1.0, 0.0).astype(HALF)


def anti_diagonal(size, total):
    row, lane = iotas(size, size)
    return ones_where(row + lane == total)


def spread_row(line):
    width = line.shape[1]
    row, lane = iotas(width // SPREAD, width)
    masked = jnp.where(lane // SPREAD == row, line, 0.0).astype(HALF)
    row, lane = iotas(width, EXTRA)
    return plain(masked, ones_where(lane == row % SPREAD + SPREAD))


def collect_rows(extra, width):
    row, lane = iotas(EXTRA, width)
    wide = plain(extra, ones_where(row == lane % SPREAD + SPREAD))
    row, lane = iotas(extra.shape[0], width)
    return jnp.where(lane // SPREAD == row, wide, 0.0)


def write_blocks(source, outs, me):
    for place, out in enumerate(outs):
        size = out.shape[0]
        out[...] = source[pl.ds(pl.multiple_of((place ^ me) * size, size), size)].astype(HALF)


def spectrum_of(mask_low, rows_t, cols_ref, col_spec, total):
    cols, rows = mask_low.shape
    half = total.shape[0]
    width = 4 * half
    col_spec[:, :rows] = plain(cols_ref[half:, :cols], mask_low).astype(HALF)
    col_spec[:, rows:] = (-plain(cols_ref[half:, cols:], mask_low)).astype(HALF)
    edge_re = plain(cols_ref[:BLOCK, :cols], mask_low).astype(HALF)
    edge_im = (-plain(cols_ref[:BLOCK, cols:], mask_low)).astype(HALF)
    edge = plain(edge_re, rows_t[:rows, :width]) + plain(edge_im, rows_t[rows:, :width])
    total[:, :width] = plain(col_spec[...], rows_t[:, :width]).astype(HALF)
    extra = plain(col_spec[...], rows_t[:, width:])
    spread = spread_row(edge[:1])
    count = spread.shape[0]
    total[:count, width:] = (extra[:count] + spread).astype(HALF)
    total[count:, width:] = extra[count:].astype(HALF)


def fill_rows_t(raw, rows_t):
    rows, freqs = raw.shape[1:]
    rows_t[:rows, :freqs] = raw[0].astype(HALF)
    rows_t[:rows, freqs : 2 * freqs] = (-raw[1]).astype(HALF)
    rows_t[rows:, :freqs] = raw[1].astype(HALF)
    rows_t[rows:, freqs : 2 * freqs] = raw[0].astype(HALF)
    lane = iotas(rows, EXTRA)[1]
    cosine, sine = raw[0, :, :1], -raw[1, :, :1]
    zero = jnp.zeros((rows, EXTRA), FLOAT)
    rows_t[:rows, 2 * freqs :] = jnp.where(lane == 0, cosine, jnp.where(lane == 1, -sine, zero)).astype(HALF)
    rows_t[rows:, 2 * freqs :] = jnp.where(lane == 0, sine, jnp.where(lane == 1, cosine, zero)).astype(HALF)


def first_kernel(index_ref, params_ref, rows_all, cols_all, *rest):
    outs, scratch = rest[:-7], rest[-7:]
    raw_rows, raw_cols, rows_t, cols_ref, col_spec, total, sems = scratch
    slab, pair, core, me = (index_ref[i] for i in range(4))
    cols = params_ref.shape[1]
    own = pl.ds(pl.multiple_of(core * cols, cols), cols)
    waits = start_all([(cols_all.at[pair, :, :, own], raw_cols), (rows_all.at[slab], raw_rows)], sems)
    mask_low = jnp.tanh(params_ref[...]).T.astype(HALF)
    waits[0].wait()
    cols_ref[:, :cols] = raw_cols[0].astype(HALF)
    cols_ref[:, cols:] = raw_cols[1].astype(HALF)
    waits[1].wait()
    fill_rows_t(raw_rows, rows_t)
    spectrum_of(mask_low, rows_t, cols_ref, col_spec, total)
    write_blocks(total, outs, me)


def table_kernel(index_ref, rows_all, cols_all, target_all, *rest):
    rows_n, rows_t, cols_n, cols_t, cols_p, target_ref, raw_rows, raw_cols, raw_target, sems = rest
    slab, pair = index_ref[0], index_ref[1]
    rows, freqs = raw_rows.shape[1:]
    wide = raw_cols.shape[2]
    here = pl.ds(pl.multiple_of(pair * wide, wide), wide)
    waits = start_all(
        [(rows_all.at[slab], raw_rows), (cols_all.at[pair], raw_cols), (target_all.at[:, here], raw_target)], sems
    )
    waits[0].wait()
    fill_rows_t(raw_rows, rows_t)
    cosine, sine = raw_rows[0].T, raw_rows[1].T
    rows_n[:freqs, :rows] = cosine.astype(HALF)
    rows_n[:freqs, rows:] = sine.astype(HALF)
    rows_n[freqs : 2 * freqs, :rows] = (-sine).astype(HALF)
    rows_n[freqs : 2 * freqs, rows:] = cosine.astype(HALF)
    line = iotas(EXTRA, rows)[0]
    first, second = cosine[:1], -sine[:1]
    zero = jnp.zeros((EXTRA, rows), FLOAT)
    rows_n[2 * freqs :, :rows] = jnp.where(line == 0, first, jnp.where(line == 1, -second, zero)).astype(HALF)
    rows_n[2 * freqs :, rows:] = jnp.where(line == 0, second, jnp.where(line == 1, first, zero)).astype(HALF)
    waits[1].wait()
    half = freqs // 2
    line = iotas(BLOCK, wide)[0]
    for part, sign in ((0, 1.0), (1, -1.0)):
        start = part * (half + BLOCK)
        cols_p[start : start + half] = raw_cols[part, half:].astype(HALF)
        edge = jnp.where(line == 0, sign * raw_cols[part, :1], 0.0)
        cols_p[start + half : start + half + BLOCK] = edge.astype(HALF)
    for part in range(2):
        cols_n[:, part * wide : (part + 1) * wide] = raw_cols[part].astype(HALF)
        for start in range(0, wide, 128):
            some = raw_cols[part, :, start : start + 128].T
            cols_t[start : start + 128, part * freqs : (part + 1) * freqs] = some.astype(HALF)
    waits[2].wait()
    for start in range(0, wide, 128):
        target_ref[start : start + 128] = (2 * raw_target[:, start : start + 128] - 1).astype(FLOAT).T


def update_kernel(first, last, count, index_ref, params_ref, rows_n, rows_t, cols_n, cols_t, *rest):
    pieces, rest = rest[:count], rest[count:]
    if last:
        new_ref, rows_v, cols_v, spec, back, sems = rest
    else:
        new_ref, outs, scratch = rest[0], rest[1 : 1 + count], rest[1 + count :]
        rows_v, rows_t_v, cols_v, cols_n_v, spec, back, col_spec, sems = scratch
    core, me = index_ref[2], index_ref[3]
    params = params_ref[...].T if first else params_ref[...]
    cols, rows = params.shape
    half = spec.shape[0]
    freqs = 2 * half
    here = pl.ds(pl.multiple_of(core * cols, cols), cols)
    arrival = start_together(piece_copies(pieces, spec, me), spec, sems.at[0])
    copies = [(rows_n, rows_v), (cols_t.at[here], cols_v)]
    if not last:
        wide = cols_n.shape[1] // 2
        copies += [
            (rows_t, rows_t_v),
            (cols_n.at[:, here], cols_n_v.at[:, :cols]),
            (cols_n.at[:, pl.ds(pl.multiple_of(wide + core * cols, cols), cols)], cols_n_v.at[:, cols:]),
        ]
    waits = start_all(copies, sems.at[1:])
    back[...] = jnp.zeros_like(back)
    arrival.wait()
    waits[0].wait()
    result = plain(spec[...], rows_v[...])
    back[half:freqs] = result[:, :rows].astype(HALF)
    back[freqs + half :] = (-result[:, rows:]).astype(HALF)
    edge = collect_rows(spec[: 2 * freqs // SPREAD, 2 * freqs :], 2 * freqs).astype(HALF)
    edge = jnp.sum(plain(edge, rows_v[: 2 * freqs]), axis=0, keepdims=True)
    line = iotas(BLOCK, rows)[0]
    back[:BLOCK] = jnp.where(line == 0, edge[:, :rows], 0.0).astype(HALF)
    back[freqs : freqs + BLOCK] = jnp.where(line == 0, -edge[:, rows:], 0.0).astype(HALF)
    waits[1].wait()
    gradient = plain(cols_v[...], back[...])
    mask = jnp.tanh(params)
    params = params - STEP_RATE * gradient * (1.0 - mask * mask)
    if last:
        new_ref[...] = params.T
    else:
        new_ref[...] = params
        for i in range(2, len(waits)):
            waits[i].wait()
        spectrum_of(jnp.tanh(params).astype(HALF), rows_t_v, cols_n_v, col_spec, spec)
        write_blocks(spec, outs, me)


def loop(count, step):
    if count <= 2:
        for i in range(count):
            step(i)
    else:
        pl.loop(0, count)(step)


def image_kernel(last, parts, order, index_ref, dose_ref, rows_n, rows_t, cols_t, cols_p, target_all, *rest):
    spec_pieces, rest = rest[:parts], rest[parts:]
    outs = rest[-16 - parts - (2 if last else 0) : -16]
    spectra = rest[: -16 - len(outs)]
    scratch = rest[-16:]
    rows_v, rows_t_v, cols_v, cols_t_v, target_ref, kern_ref, spec = scratch[:7]
    filtered, sides, fields, cotangent, back, total, half_spec, turned, sems = scratch[7:]
    if last:
        own_light, other_light, outs = outs[0], outs[1], outs[2:]
    slab, core, me = index_ref[0], index_ref[2], index_ref[3]
    wide, rows = target_ref.shape
    count, freqs = fields.shape[0], spec.shape[0]
    width = kern_ref.shape[2]

    def kernel_rows(k, start):
        part = slab ^ (start // width)
        place = 0
        for axis, bit in order:
            place = 2 * place + (((k >> (bit - 1)) & 1) if axis == "kern" else ((part >> bit) & 1))
        here = pl.ds(start % width, BLOCK)
        return kern_ref[place, 0, here].astype(FLOAT), kern_ref[place, 1, here].astype(FLOAT)

    arrival = start_together(piece_copies(spec_pieces, half_spec, me), half_spec, sems.at[0])
    copies = []
    filled = 0
    for piece in spectra:
        copies.append((piece, kern_ref.at[filled : filled + piece.shape[0]]))
        filled += piece.shape[0]
    spectra_here = start_together(copies, kern_ref, sems.at[1])
    copies = [(rows_n.at[: 2 * freqs], rows_v), (cols_t, cols_t_v), (target_all, target_ref), (cols_p, cols_v), (rows_t.at[:, : 2 * freqs], rows_t_v)]
    waits = start_all(copies, sems.at[2:])
    if count > 2:
        total[...] = jnp.zeros_like(total)
    arrival.wait()

    half = freqs // 2
    mirror = anti_diagonal(freqs, freqs)
    flip = anti_diagonal(half, half)
    spec[half:] = half_spec[:, : 2 * freqs]
    lane = iotas(half, freqs)[1]
    past_re = half_spec[:, 2 * freqs : 2 * freqs + EXTRA][:, :1].astype(FLOAT)
    past_im = half_spec[:, 2 * freqs : 2 * freqs + EXTRA][:, 1:2].astype(FLOAT)
    turned[:, :freqs] = jnp.where(lane == 0, past_re, plain(half_spec[:, :freqs], mirror)).astype(HALF)
    turned[:, freqs:] = jnp.where(lane == 0, -past_im, -plain(half_spec[:, freqs : 2 * freqs], mirror)).astype(HALF)
    edge = collect_rows(half_spec[: 2 * freqs // SPREAD, 2 * freqs :], 2 * freqs)
    edge = jnp.sum(edge, axis=0, keepdims=True)
    line = iotas(half, 2 * freqs)[0]
    spec[:half] = jnp.where(line == 0, edge, plain(flip, turned[...])).astype(HALF)
    spectra_here.wait()
    waits[0].wait()

    def make_rows(k):
        for start in range(0, freqs, BLOCK):
            here = pl.ds(start, BLOCK)
            spec_re, spec_im = spec[here, :freqs].astype(FLOAT), spec[here, freqs:].astype(FLOAT)
            real, imag = kernel_rows(k, start)
            filtered[here, :freqs] = (real * spec_re - imag * spec_im).astype(HALF)
            filtered[here, freqs:] = (real * spec_im + imag * spec_re).astype(HALF)
        result = plain(filtered[...], rows_v[...])
        sides[k, :freqs] = result.astype(HALF)
        sides[k, freqs:, :rows] = (-result[:, rows:]).astype(HALF)
        sides[k, freqs:, rows:] = result[:, :rows].astype(HALF)

    loop(count, make_rows)

    waits[1].wait()

    def make_fields(k):
        fields[k] = plain(cols_t_v[...], sides[k])

    loop(count, make_fields)

    waits[2].wait()
    chunk = 32

    @pl.loop(0, wide // chunk, unroll=4)
    def make_sens(i):
        here = pl.ds(pl.multiple_of(i * chunk, chunk), chunk)
        target = target_ref[here]
        light = None
        for k in range(count):
            real, imag = fields[k, here, :rows], fields[k, here, rows:]
            power = real * real + imag * imag
            light = power if light is None else light + power
        if last:
            side = (i * chunk) // (wide // 2)
            place = pl.ds(pl.multiple_of(i * chunk - side * (wide // 2), chunk), chunk)

            @pl.when(side == core)
            def _():
                own_light[place] = light

            @pl.when(side != core)
            def _():
                other_light[place] = light.astype(HALF)

        sens = None
        for dose in range(dose_ref.shape[0]):
            factor = dose_ref[dose]
            level = jnp.tanh((0.5 * STEEPNESS * factor) * light - 0.5 * STEEPNESS * THRESHOLD)
            slope = (level - target) * (1.0 - level * level) * (0.25 * STEEPNESS * factor)
            sens = slope if sens is None else sens + slope
        for k in range(count):
            real = sens * fields[k, here, :rows]
            imag = sens * fields[k, here, rows:]
            cotangent[k, here, :rows] = real.astype(HALF)
            cotangent[k, here, rows:] = imag.astype(HALF)

    waits[3].wait()
    waits[4].wait()

    def go_back(k):
        both = plain(cols_v[...], cotangent[k])
        size = half + BLOCK
        real_c, imag_c = both[:size, :rows], both[:size, rows:]
        real_s, imag_s = both[size:, :rows], both[size:, rows:]
        back[half:, :rows] = (real_c + imag_s)[:half].astype(HALF)
        back[half:, rows:] = (imag_c - real_s)[:half].astype(HALF)
        low_re, low_im = real_c - imag_s, imag_c + real_s
        turned[:, :rows] = low_re[:half].astype(HALF)
        turned[:, rows : 2 * rows] = low_im[:half].astype(HALF)
        low = plain(flip, turned[:, : 2 * rows])
        line = iotas(half, rows)[0]
        back[:half, :rows] = jnp.where(line == 0, low_re[half : half + 1], low[:, :rows]).astype(HALF)
        back[:half, rows:] = jnp.where(line == 0, low_im[half : half + 1], low[:, rows:]).astype(HALF)
        slopes = filtered_slopes(back, rows_t_v)
        for start in range(0, freqs, BLOCK):
            here = pl.ds(start, BLOCK)
            real, imag = kernel_rows(k, start)
            slope_re, slope_im = slopes(start)
            total_re = real * slope_re + imag * slope_im
            total_im = real * slope_im - imag * slope_re
            if count > 2 or k > 0:
                total_re += total[here, :freqs]
                total_im += total[here, freqs:]
            total[here, :freqs] = total_re
            total[here, freqs:] = total_im

    def filtered_slopes(back, table):
        step = min(256, freqs)
        made = {}

        def at(start):
            first = start // step * step
            if first not in made:
                made.clear()
                made[first] = plain(back[first : first + step], table[...])
            part = made[first][start - first : start - first + BLOCK]
            return part[:, :freqs], part[:, freqs:]

        return at

    loop(count, go_back)

    turned[...] = plain(flip, total[:half].astype(HALF)).astype(HALF)
    half_spec[:, :freqs] = (total[half:, :freqs] + plain(turned[:, :freqs], mirror)).astype(HALF)
    half_spec[:, freqs : 2 * freqs] = (total[half:, freqs:] - plain(turned[:, freqs:], mirror)).astype(HALF)
    past_re = turned[:, :EXTRA][:, :1].astype(FLOAT)
    past_im = turned[:, freqs : freqs + EXTRA][:, :1].astype(FLOAT)
    lane = iotas(half, EXTRA)[1]
    extra = jnp.where(lane == 0, past_re, jnp.where(lane == 1, -past_im, 0.0))
    spread = spread_row(total[:1])
    lines = spread.shape[0]
    half_spec[:lines, 2 * freqs :] = (extra[:lines] + spread).astype(HALF)
    half_spec[lines:, 2 * freqs :] = extra[lines:].astype(HALF)
    write_blocks(half_spec, outs, me)


def print_kernel(index_ref, dose_ref, own_ref, other_ref, printed_ref):
    core = index_ref[2]
    cols = own_ref.shape[0]
    for focus, light_ref in ((core, own_ref), (1 - core, other_ref)):
        for start in range(0, cols, 128):
            light = light_ref[start : start + 128].astype(FLOAT).T
            for dose in range(dose_ref.shape[0]):
                level = jnp.tanh(0.5 * STEEPNESS * (dose_ref[dose] * light - THRESHOLD))
                printed_ref[focus, dose, :, start : start + 128] = 0.5 * level + 0.5


def body(kern_size, slab_size, mask_params, target_bits, kernels, weights, dose_factors):
    rows, cols = mask_params.shape
    freqs = kernels.shape[2]
    assert kernels.shape[0] == 1 and kern_size % FOCI == 0
    count = kern_size // FOCI
    wide = FOCI * cols
    sizes = {"kern": kern_size, "slab": slab_size}
    slab, kern = lax.axis_index("slab"), lax.axis_index("kern")
    rounds = plan_rounds(sizes)
    me = jnp.int32(0)
    for axis, bit in [("kern", 0)] + rounds[0]:
        me = 2 * me + (((kern if axis == "kern" else slab) >> bit) & 1)
    index = jnp.stack([slab, kern // FOCI, kern % FOCI, me]).astype(jnp.int32)
    tables = trig_tables(rows * slab_size, freqs)
    rows_all = jnp.asarray(row_blocks(tables, slab_size))
    cols_all = jnp.asarray(col_blocks(tables, count))

    smem = pl.BlockSpec(memory_space=pltpu.SMEM)
    vmem = pl.BlockSpec(memory_space=pltpu.VMEM)
    anywhere = pl.BlockSpec(memory_space=pl.ANY)
    hbm = pl.BlockSpec(memory_space=pltpu.HBM)
    compiler_params = pltpu.CompilerParams(vmem_limit_bytes=VMEM_LIMIT)
    members = 1 << len(rounds[0])
    parts_out = [jax.ShapeDtypeStruct((freqs // 4 // members, 2 * freqs + EXTRA), HALF)] * (2 * members)
    rows_n_like = ((2 * freqs + EXTRA, 2 * rows), HALF)
    rows_t_like = ((2 * rows, 2 * freqs + EXTRA), HALF)
    cols_n_like = ((freqs, 2 * wide), HALF)
    cols_t_like = ((wide, 2 * freqs), HALF)
    spec_like = ((freqs, 2 * freqs), HALF)
    half_like = ((freqs // 2, 2 * freqs + EXTRA), HALF)
    raw_rows_like = ((2, rows, freqs), FLOAT)
    dma = pltpu.SemaphoreType.DMA

    cols_p_like = ((freqs + 2 * BLOCK, wide), HALF)
    table_likes = [rows_n_like, rows_t_like, cols_n_like, cols_t_like, cols_p_like, ((wide, rows), FLOAT)]
    rows_n, rows_t, cols_n, cols_t, cols_p, target = pl.pallas_call(
        table_kernel,
        out_shape=[jax.ShapeDtypeStruct(*like) for like in table_likes],
        in_specs=[smem, hbm, hbm, anywhere],
        out_specs=[vmem] * 6,
        scratch_shapes=[
            pltpu.VMEM(*raw_rows_like),
            pltpu.VMEM((2, freqs, wide), FLOAT),
            pltpu.VMEM((rows, wide), jnp.int32),
            dma((3,)),
        ],
        compiler_params=pltpu.CompilerParams(vmem_limit_bytes=60 * 1024 * 1024),
        name="make_tables",
    )(index, rows_all, cols_all, target_bits)
    made = (rows_n, rows_t, cols_n, cols_t, cols_p)

    begun = [jnp.swapaxes(kernels * jnp.sqrt(weights)[:, None, None, None], 2, 3).astype(HALF)]
    for bits in reversed(rounds[1:]):
        value = begun[0] if len(begun) == 1 else jnp.concatenate(begun, axis=0)
        begun = [value] + [partner(value, bits, p, sizes) for p in range(1, 1 << len(bits))]
    spectra = None
    order = [pair for bits in rounds for pair in bits]

    parts = pl.pallas_call(
        first_kernel,
        out_shape=parts_out,
        in_specs=[smem, vmem, hbm, hbm],
        out_specs=[vmem] * len(parts_out),
        scratch_shapes=[
            pltpu.VMEM(*raw_rows_like),
            pltpu.VMEM((2, freqs, cols), FLOAT),
            pltpu.VMEM(*rows_t_like),
            pltpu.VMEM((freqs, 2 * cols), HALF),
            pltpu.VMEM((freqs // 2, 2 * rows), HALF),
            pltpu.VMEM(*half_like),
            dma((2,)),
        ],
        compiler_params=compiler_params,
        name="first_spectrum",
    )(index, mask_params, rows_all, cols_all)

    params, printed = mask_params, None
    for step in range(STEPS):
        first, last = step == 0, step == STEPS - 1
        if first:
            def to_neighbours(pieces):
                value = jnp.concatenate(pieces, axis=0)
                return [value] + [partner(value, rounds[0], p, sizes) for p in (1, 2)], made, target

            parts, (spectra, made, target) = reduce_all(parts, rounds, sizes, begun, to_neighbours)
            cut = spectra[0].shape[0] // 2
            spectra = spectra + [
                partner(spectra[2][:cut], rounds[0], 1, sizes),
                partner(spectra[1][cut:], rounds[0], 2, sizes),
            ]
        else:
            parts, _ = reduce_all(parts, rounds, sizes)
        out_shape = list(parts_out)
        if last:
            lights = [jax.ShapeDtypeStruct((cols, rows), FLOAT), jax.ShapeDtypeStruct((cols, rows), HALF)]
            out_shape = lights + out_shape
        outs = pl.pallas_call(
            functools.partial(image_kernel, last, len(parts), order),
            out_shape=out_shape,
            in_specs=[smem, smem] + [hbm] * 5 + [anywhere] * (len(parts) + len(spectra)),
            out_specs=[vmem] * len(out_shape),
            scratch_shapes=[
                pltpu.VMEM((2 * freqs, 2 * rows), HALF),
                pltpu.VMEM((2 * rows, 2 * freqs), HALF),
                pltpu.VMEM(*cols_p_like),
                pltpu.VMEM(*cols_t_like),
                pltpu.VMEM((wide, rows), FLOAT),
                pltpu.VMEM((count * slab_size,) + kernels.shape[1:2] + (kernels.shape[3], freqs), HALF),
                pltpu.VMEM(*spec_like),
                pltpu.VMEM(*spec_like),
                pltpu.VMEM((count, 2 * freqs, 2 * rows), HALF),
                pltpu.VMEM((count, wide, 2 * rows), FLOAT),
                pltpu.VMEM((count, wide, 2 * rows), HALF),
                pltpu.VMEM((freqs, 2 * rows), HALF),
                pltpu.VMEM((freqs, 2 * freqs), FLOAT),
                pltpu.VMEM(*half_like),
                pltpu.VMEM((freqs // 2, 2 * freqs), HALF),
                dma((7,)),
            ],
            compiler_params=compiler_params,
            name="image_and_back",
        )(
            index,
            dose_factors,
            made[0],
            made[1],
            *made[3:],
            target,
            *parts,
            *spectra,
        )
        parts = outs[-len(parts) :]
        if last:
            printed = pl.pallas_call(
                print_kernel,
                out_shape=jax.ShapeDtypeStruct((FOCI, dose_factors.shape[0], rows, cols), FLOAT),
                in_specs=[smem, smem, vmem, vmem],
                out_specs=vmem,
                compiler_params=compiler_params,
                name="print_resist",
            )(index, dose_factors, outs[0], partner(outs[1], [("kern", 0)], 1, sizes))
        shown = printed
        parts, printed = reduce_all(parts, rounds, sizes, None, (lambda _: shown) if last else None)
        tile = jax.ShapeDtypeStruct((rows, cols) if last else (cols, rows), FLOAT)
        common = [pltpu.VMEM(*rows_n_like), pltpu.VMEM((cols, 2 * freqs), HALF)]
        work = [pltpu.VMEM(*half_like), pltpu.VMEM((2 * freqs, rows), HALF)]
        if last:
            scratch = common + work + [dma((3,))]
        else:
            scratch = common[:1] + [pltpu.VMEM(*rows_t_like)] + common[1:]
            scratch += [pltpu.VMEM((freqs, 2 * cols), HALF)] + work
            scratch += [pltpu.VMEM((freqs // 2, 2 * rows), HALF), dma((6,))]
        outs = pl.pallas_call(
            functools.partial(update_kernel, first, last, len(parts)),
            out_shape=[tile] if last else [tile] + parts_out,
            in_specs=[smem, vmem] + [hbm] * 4 + [anywhere] * len(parts),
            out_specs=[vmem] * (1 if last else 1 + len(parts)),
            scratch_shapes=scratch,
            compiler_params=compiler_params,
            name="update",
        )(index, params, *made[:4], *parts)
        params = outs[0]
        if not last:
            parts = outs[1:]
    return (params, printed)


def solution(mesh):
    sizes = dict(mesh.shape)
    in_specs = (P("slab", "kern"), P("slab", None), P("kern", None, None, "slab"), P("kern"), P())
    out_specs = (P("slab", "kern"), P(None, None, "slab", "kern"))
    return jax.shard_map(
        functools.partial(body, sizes["kern"], sizes["slab"]),
        mesh=mesh,
        in_specs=in_specs,
        out_specs=out_specs,
        check_vma=False,
    )
```

```python
import functools

import jax
import jax.numpy as jnp
import numpy as np
from jax import lax
from jax.experimental import pallas as pl
from jax.experimental.pallas import tpu as pltpu
from jax.sharding import PartitionSpec as P

FOCI = 2
STEPS = 2
STEEPNESS = 3.0
THRESHOLD = 1.0
STEP_RATE = 0.4
BLOCK = 16
EXTRA = 128
SPREAD = 64
VMEM_LIMIT = 50 * 1024 * 1024
FLOAT = jnp.float32
HALF = jnp.bfloat16
AXES = ("kern", "slab")


def plain(left, right):
    return jnp.dot(left, right, preferred_element_type=FLOAT)


def trig_tables(pixels, freqs):
    phases = ((np.arange(freqs) - freqs // 2)[:, None] * np.arange(pixels)[None, :]) % pixels
    angles = phases.astype(np.float32) * np.float32(2.0 * np.pi / pixels)
    scale = np.float32(1.0 / np.sqrt(pixels))
    cosine = (np.cos(angles.astype(np.float64)).astype(np.float32) * scale).astype(HALF)
    sine = (np.sin(angles.astype(np.float64)).astype(np.float32) * scale).astype(HALF)
    return np.stack([cosine.astype(np.float32), sine.astype(np.float32)])


def row_blocks(tables, parts):
    _, freqs, pixels = tables.shape
    split = tables.transpose(0, 2, 1).reshape(2, parts, pixels // parts, freqs)
    return np.ascontiguousarray(split.transpose(1, 0, 2, 3))


def col_blocks(tables, parts):
    _, freqs, pixels = tables.shape
    split = tables.reshape(2, freqs, parts, pixels // parts)
    return np.ascontiguousarray(split.transpose(2, 0, 1, 3))


def flat_index(kern, slab, sizes):
    return kern * sizes["slab"] + slab


def plan_rounds(sizes):
    kern_bits = [("kern", bit) for bit in range(1, sizes["kern"].bit_length() - 1)]
    slab_bits = [("slab", bit) for bit in range(sizes["slab"].bit_length() - 1)]
    rounds = [kern_bits[:1] + slab_bits[:1], slab_bits[1:3], kern_bits[1:3], slab_bits[3:]]
    return [bits for bits in rounds if bits]


def partner(values, bits, place, sizes):
    shift = {"kern": 0, "slab": 0}
    for i, (axis, bit) in enumerate(bits):
        if (place >> (len(bits) - 1 - i)) & 1:
            shift[axis] |= 1 << bit
    mask = flat_index(shift["kern"], shift["slab"], sizes)
    total = sizes["kern"] * sizes["slab"]
    return lax.ppermute(values, AXES, [(i, i ^ mask) for i in range(total)])


def add_all(pieces):
    total = pieces[0].astype(FLOAT)
    for piece in pieces[1:]:
        total = total + piece.astype(FLOAT)
    return total.astype(HALF)


def tied(values, others):
    return lax.optimization_barrier((values, others))


def reduce_all(parts, rounds, sizes, early=None, late=None):
    core = [("kern", 0)]
    count = len(parts) // 2
    parts = [add_all([mine, partner(other, core, 1, sizes)]) for mine, other in zip(parts[:count], parts[count:])]
    others = [partner(parts[p], rounds[0], p, sizes) for p in range(1, count)]
    total = add_all([parts[0]] + others)
    for bits in rounds[1:]:
        others = [partner(total, bits, p, sizes) for p in range(1, 1 << len(bits))]
        if late is not None and bits is rounds[1]:
            others, late = tied(others, late(early))
        total = add_all([total] + others)
    pieces = [total] + [partner(total, rounds[0], p, sizes) for p in range(1, count)]
    return pieces + [partner(piece, core, 1, sizes) for piece in pieces], late


def start_together(copies, whole, sem):
    for source, target in copies:
        pltpu.make_async_copy(source, target, sem).start()
    return pltpu.make_async_copy(whole, whole, sem)


def start_all(copies, sems):
    started = [pltpu.make_async_copy(source, target, sems.at[i]) for i, (source, target) in enumerate(copies)]
    for copy in started:
        copy.start()
    return started


def piece_copies(pieces, spec, me):
    size = pieces[0].shape[0]
    return [
        (piece, spec.at[pl.ds(pl.multiple_of((place ^ me) * size, size), size)]) for place, piece in enumerate(pieces)
    ]


def iotas(rows, cols):
    shape = (rows, cols)
    return lax.broadcasted_iota(jnp.int32, shape, 0), lax.broadcasted_iota(jnp.int32, shape, 1)


def ones_where(condition):
    return jnp.where(condition, 1.0, 0.0).astype(HALF)


def anti_diagonal(size, total):
    row, lane = iotas(size, size)
    return ones_where(row + lane == total)


def spread_row(line):
    width = line.shape[1]
    row, lane = iotas(width // SPREAD, width)
    masked = jnp.where(lane // SPREAD == row, line, 0.0).astype(HALF)
    row, lane = iotas(width, EXTRA)
    return plain(masked, ones_where(lane == row % SPREAD + SPREAD))


def collect_rows(extra, width):
    row, lane = iotas(EXTRA, width)
    wide = plain(extra, ones_where(row == lane % SPREAD + SPREAD))
    row, lane = iotas(extra.shape[0], width)
    return jnp.where(lane // SPREAD == row, wide, 0.0)


def write_blocks(source, outs, me):
    for place, out in enumerate(outs):
        size = out.shape[0]
        out[...] = source[pl.ds(pl.multiple_of((place ^ me) * size, size), size)].astype(HALF)


def spectrum_of(mask_low, rows_t, cols_ref, col_spec, total):
    cols, rows = mask_low.shape
    half = total.shape[0]
    width = 4 * half
    col_spec[:, :rows] = plain(cols_ref[half:, :cols], mask_low).astype(HALF)
    col_spec[:, rows:] = (-plain(cols_ref[half:, cols:], mask_low)).astype(HALF)
    edge_re = plain(cols_ref[:BLOCK, :cols], mask_low).astype(HALF)
    edge_im = (-plain(cols_ref[:BLOCK, cols:], mask_low)).astype(HALF)
    edge = plain(edge_re, rows_t[:rows, :width]) + plain(edge_im, rows_t[rows:, :width])
    total[:, :width] = plain(col_spec[...], rows_t[:, :width]).astype(HALF)
    extra = plain(col_spec[...], rows_t[:, width:])
    spread = spread_row(edge[:1])
    count = spread.shape[0]
    total[:count, width:] = (extra[:count] + spread).astype(HALF)
    total[count:, width:] = extra[count:].astype(HALF)


def fill_rows_t(raw, rows_t):
    rows, freqs = raw.shape[1:]
    rows_t[:rows, :freqs] = raw[0].astype(HALF)
    rows_t[:rows, freqs : 2 * freqs] = (-raw[1]).astype(HALF)
    rows_t[rows:, :freqs] = raw[1].astype(HALF)
    rows_t[rows:, freqs : 2 * freqs] = raw[0].astype(HALF)
    lane = iotas(rows, EXTRA)[1]
    cosine, sine = raw[0, :, :1], -raw[1, :, :1]
    zero = jnp.zeros((rows, EXTRA), FLOAT)
    rows_t[:rows, 2 * freqs :] = jnp.where(lane == 0, cosine, jnp.where(lane == 1, -sine, zero)).astype(HALF)
    rows_t[rows:, 2 * freqs :] = jnp.where(lane == 0, sine, jnp.where(lane == 1, cosine, zero)).astype(HALF)


def first_kernel(index_ref, params_ref, rows_all, cols_all, *rest):
    outs, scratch = rest[:-7], rest[-7:]
    raw_rows, raw_cols, rows_t, cols_ref, col_spec, total, sems = scratch
    slab, pair, core, me = (index_ref[i] for i in range(4))
    cols = params_ref.shape[1]
    own = pl.ds(pl.multiple_of(core * cols, cols), cols)
    waits = start_all([(cols_all.at[pair, :, :, own], raw_cols), (rows_all.at[slab], raw_rows)], sems)
    mask_low = jnp.tanh(params_ref[...]).T.astype(HALF)
    waits[0].wait()
    cols_ref[:, :cols] = raw_cols[0].astype(HALF)
    cols_ref[:, cols:] = raw_cols[1].astype(HALF)
    waits[1].wait()
    fill_rows_t(raw_rows, rows_t)
    spectrum_of(mask_low, rows_t, cols_ref, col_spec, total)
    write_blocks(total, outs, me)


def table_kernel(index_ref, rows_all, cols_all, target_all, *rest):
    rows_n, rows_t, cols_n, cols_t, cols_p, target_ref, raw_rows, raw_cols, raw_target, sems = rest
    slab, pair = index_ref[0], index_ref[1]
    rows, freqs = raw_rows.shape[1:]
    wide = raw_cols.shape[2]
    here = pl.ds(pl.multiple_of(pair * wide, wide), wide)
    waits = start_all(
        [(rows_all.at[slab], raw_rows), (cols_all.at[pair], raw_cols), (target_all.at[:, here], raw_target)], sems
    )
    waits[0].wait()
    fill_rows_t(raw_rows, rows_t)
    cosine, sine = raw_rows[0].T, raw_rows[1].T
    rows_n[:freqs, :rows] = cosine.astype(HALF)
    rows_n[:freqs, rows:] = sine.astype(HALF)
    rows_n[freqs : 2 * freqs, :rows] = (-sine).astype(HALF)
    rows_n[freqs : 2 * freqs, rows:] = cosine.astype(HALF)
    line = iotas(EXTRA, rows)[0]
    first, second = cosine[:1], -sine[:1]
    zero = jnp.zeros((EXTRA, rows), FLOAT)
    rows_n[2 * freqs :, :rows] = jnp.where(line == 0, first, jnp.where(line == 1, -second, zero)).astype(HALF)
    rows_n[2 * freqs :, rows:] = jnp.where(line == 0, second, jnp.where(line == 1, first, zero)).astype(HALF)
    waits[1].wait()
    half = freqs // 2
    line = iotas(BLOCK, wide)[0]
    for part, sign in ((0, 1.0), (1, -1.0)):
        start = part * (half + BLOCK)
        cols_p[start : start + half] = raw_cols[part, half:].astype(HALF)
        edge = jnp.where(line == 0, sign * raw_cols[part, :1], 0.0)
        cols_p[start + half : start + half + BLOCK] = edge.astype(HALF)
    for part in range(2):
        cols_n[:, part * wide : (part + 1) * wide] = raw_cols[part].astype(HALF)
        for start in range(0, wide, 128):
            some = raw_cols[part, :, start : start + 128].T
            cols_t[start : start + 128, part * freqs : (part + 1) * freqs] = some.astype(HALF)
    waits[2].wait()
    for start in range(0, wide, 128):
        target_ref[start : start + 128] = (2 * raw_target[:, start : start + 128] - 1).astype(FLOAT).T


def update_kernel(first, last, count, index_ref, params_ref, rows_n, rows_t, cols_n, cols_t, *rest):
    pieces, rest = rest[:count], rest[count:]
    if last:
        new_ref, rows_v, cols_v, spec, back, sems = rest
    else:
        new_ref, outs, scratch = rest[0], rest[1 : 1 + count], rest[1 + count :]
        rows_v, rows_t_v, cols_v, cols_n_v, spec, back, col_spec, sems = scratch
    core, me = index_ref[2], index_ref[3]
    params = params_ref[...].T if first else params_ref[...]
    cols, rows = params.shape
    half = spec.shape[0]
    freqs = 2 * half
    here = pl.ds(pl.multiple_of(core * cols, cols), cols)
    arrival = start_together(piece_copies(pieces, spec, me), spec, sems.at[0])
    copies = [(rows_n, rows_v), (cols_t.at[here], cols_v)]
    if not last:
        wide = cols_n.shape[1] // 2
        copies += [
            (rows_t, rows_t_v),
            (cols_n.at[:, here], cols_n_v.at[:, :cols]),
            (cols_n.at[:, pl.ds(pl.multiple_of(wide + core * cols, cols), cols)], cols_n_v.at[:, cols:]),
        ]
    waits = start_all(copies, sems.at[1:])
    back[...] = jnp.zeros_like(back)
    arrival.wait()
    waits[0].wait()
    result = plain(spec[...], rows_v[...])
    back[half:freqs] = result[:, :rows].astype(HALF)
    back[freqs + half :] = (-result[:, rows:]).astype(HALF)
    edge = collect_rows(spec[: 2 * freqs // SPREAD, 2 * freqs :], 2 * freqs).astype(HALF)
    edge = jnp.sum(plain(edge, rows_v[: 2 * freqs]), axis=0, keepdims=True)
    line = iotas(BLOCK, rows)[0]
    back[:BLOCK] = jnp.where(line == 0, edge[:, :rows], 0.0).astype(HALF)
    back[freqs : freqs + BLOCK] = jnp.where(line == 0, -edge[:, rows:], 0.0).astype(HALF)
    waits[1].wait()
    gradient = plain(cols_v[...], back[...])
    mask = jnp.tanh(params)
    params = params - STEP_RATE * gradient * (1.0 - mask * mask)
    if last:
        new_ref[...] = params.T
    else:
        new_ref[...] = params
        for i in range(2, len(waits)):
            waits[i].wait()
        spectrum_of(jnp.tanh(params).astype(HALF), rows_t_v, cols_n_v, col_spec, spec)
        write_blocks(spec, outs, me)


def loop(count, step):
    if count <= 2:
        for i in range(count):
            step(i)
    else:
        pl.loop(0, count)(step)


def image_kernel(last, parts, order, index_ref, dose_ref, rows_n, rows_t, cols_t, cols_p, target_all, *rest):
    spec_pieces, rest = rest[:parts], rest[parts:]
    outs = rest[-16 - parts - (2 if last else 0) : -16]
    spectra = rest[: -16 - len(outs)]
    scratch = rest[-16:]
    rows_v, rows_t_v, cols_v, cols_t_v, target_ref, kern_ref, spec = scratch[:7]
    filtered, sides, fields, cotangent, back, total, half_spec, turned, sems = scratch[7:]
    if last:
        own_light, other_light, outs = outs[0], outs[1], outs[2:]
    slab, core, me = index_ref[0], index_ref[2], index_ref[3]
    wide, rows = target_ref.shape
    count, freqs = fields.shape[0], spec.shape[0]
    width = kern_ref.shape[2]

    def kernel_rows(k, start):
        part = slab ^ (start // width)
        place = 0
        for axis, bit in order:
            place = 2 * place + (((k >> (bit - 1)) & 1) if axis == "kern" else ((part >> bit) & 1))
        here = pl.ds(start % width, BLOCK)
        return kern_ref[place, 0, here].astype(FLOAT), kern_ref[place, 1, here].astype(FLOAT)

    arrival = start_together(piece_copies(spec_pieces, half_spec, me), half_spec, sems.at[0])
    copies = []
    filled = 0
    for piece in spectra:
        copies.append((piece, kern_ref.at[filled : filled + piece.shape[0]]))
        filled += piece.shape[0]
    spectra_here = start_together(copies, kern_ref, sems.at[1])
    copies = [(rows_n.at[: 2 * freqs], rows_v), (cols_t, cols_t_v), (target_all, target_ref), (cols_p, cols_v), (rows_t.at[:, : 2 * freqs], rows_t_v)]
    waits = start_all(copies, sems.at[2:])
    if count > 2:
        total[...] = jnp.zeros_like(total)
    arrival.wait()

    half = freqs // 2
    mirror = anti_diagonal(freqs, freqs)
    flip = anti_diagonal(half, half)
    spec[half:] = half_spec[:, : 2 * freqs]
    lane = iotas(half, freqs)[1]
    past_re = half_spec[:, 2 * freqs : 2 * freqs + EXTRA][:, :1].astype(FLOAT)
    past_im = half_spec[:, 2 * freqs : 2 * freqs + EXTRA][:, 1:2].astype(FLOAT)
    turned[:, :freqs] = jnp.where(lane == 0, past_re, plain(half_spec[:, :freqs], mirror)).astype(HALF)
    turned[:, freqs:] = jnp.where(lane == 0, -past_im, -plain(half_spec[:, freqs : 2 * freqs], mirror)).astype(HALF)
    edge = collect_rows(half_spec[: 2 * freqs // SPREAD, 2 * freqs :], 2 * freqs)
    edge = jnp.sum(edge, axis=0, keepdims=True)
    line = iotas(half, 2 * freqs)[0]
    spec[:half] = jnp.where(line == 0, edge, plain(flip, turned[...])).astype(HALF)
    spectra_here.wait()
    waits[0].wait()

    def make_rows(k):
        for start in range(0, freqs, BLOCK):
            here = pl.ds(start, BLOCK)
            spec_re, spec_im = spec[here, :freqs].astype(FLOAT), spec[here, freqs:].astype(FLOAT)
            real, imag = kernel_rows(k, start)
            filtered[here, :freqs] = (real * spec_re - imag * spec_im).astype(HALF)
            filtered[here, freqs:] = (real * spec_im + imag * spec_re).astype(HALF)
        result = plain(filtered[...], rows_v[...])
        sides[k, :freqs] = result.astype(HALF)
        sides[k, freqs:, :rows] = (-result[:, rows:]).astype(HALF)
        sides[k, freqs:, rows:] = result[:, :rows].astype(HALF)

    loop(count, make_rows)

    waits[1].wait()

    def make_fields(k):
        fields[k] = plain(cols_t_v[...], sides[k])

    loop(count, make_fields)

    waits[2].wait()
    chunk = 32

    @pl.loop(0, wide // chunk, unroll=4)
    def make_sens(i):
        here = pl.ds(pl.multiple_of(i * chunk, chunk), chunk)
        target = target_ref[here]
        light = None
        for k in range(count):
            real, imag = fields[k, here, :rows], fields[k, here, rows:]
            power = real * real + imag * imag
            light = power if light is None else light + power
        if last:
            side = (i * chunk) // (wide // 2)
            place = pl.ds(pl.multiple_of(i * chunk - side * (wide // 2), chunk), chunk)

            @pl.when(side == core)
            def _():
                own_light[place] = light

            @pl.when(side != core)
            def _():
                other_light[place] = light.astype(HALF)

        sens = None
        for dose in range(dose_ref.shape[0]):
            factor = dose_ref[dose]
            level = jnp.tanh((0.5 * STEEPNESS * factor) * light - 0.5 * STEEPNESS * THRESHOLD)
            slope = (level - target) * (1.0 - level * level) * (0.25 * STEEPNESS * factor)
            sens = slope if sens is None else sens + slope
        for k in range(count):
            real = sens * fields[k, here, :rows]
            imag = sens * fields[k, here, rows:]
            cotangent[k, here, :rows] = real.astype(HALF)
            cotangent[k, here, rows:] = imag.astype(HALF)

    waits[3].wait()
    waits[4].wait()

    def go_back(k):
        both = plain(cols_v[...], cotangent[k])
        size = half + BLOCK
        real_c, imag_c = both[:size, :rows], both[:size, rows:]
        real_s, imag_s = both[size:, :rows], both[size:, rows:]
        back[half:, :rows] = (real_c + imag_s)[:half].astype(HALF)
        back[half:, rows:] = (imag_c - real_s)[:half].astype(HALF)
        low_re, low_im = real_c - imag_s, imag_c + real_s
        turned[:, :rows] = low_re[:half].astype(HALF)
        turned[:, rows : 2 * rows] = low_im[:half].astype(HALF)
        low = plain(flip, turned[:, : 2 * rows])
        line = iotas(half, rows)[0]
        back[:half, :rows] = jnp.where(line == 0, low_re[half : half + 1], low[:, :rows]).astype(HALF)
        back[:half, rows:] = jnp.where(line == 0, low_im[half : half + 1], low[:, rows:]).astype(HALF)
        slopes = filtered_slopes(back, rows_t_v)
        for start in range(0, freqs, BLOCK):
            here = pl.ds(start, BLOCK)
            real, imag = kernel_rows(k, start)
            slope_re, slope_im = slopes(start)
            total_re = real * slope_re + imag * slope_im
            total_im = real * slope_im - imag * slope_re
            if count > 2 or k > 0:
                total_re += total[here, :freqs]
                total_im += total[here, freqs:]
            total[here, :freqs] = total_re
            total[here, freqs:] = total_im

    def filtered_slopes(back, table):
        step = min(256, freqs)
        made = {}

        def at(start):
            first = start // step * step
            if first not in made:
                made.clear()
                made[first] = plain(back[first : first + step], table[...])
            part = made[first][start - first : start - first + BLOCK]
            return part[:, :freqs], part[:, freqs:]

        return at

    loop(count, go_back)

    turned[...] = plain(flip, total[:half].astype(HALF)).astype(HALF)
    half_spec[:, :freqs] = (total[half:, :freqs] + plain(turned[:, :freqs], mirror)).astype(HALF)
    half_spec[:, freqs : 2 * freqs] = (total[half:, freqs:] - plain(turned[:, freqs:], mirror)).astype(HALF)
    past_re = turned[:, :EXTRA][:, :1].astype(FLOAT)
    past_im = turned[:, freqs : freqs + EXTRA][:, :1].astype(FLOAT)
    lane = iotas(half, EXTRA)[1]
    extra = jnp.where(lane == 0, past_re, jnp.where(lane == 1, -past_im, 0.0))
    spread = spread_row(total[:1])
    lines = spread.shape[0]
    half_spec[:lines, 2 * freqs :] = (extra[:lines] + spread).astype(HALF)
    half_spec[lines:, 2 * freqs :] = extra[lines:].astype(HALF)
    write_blocks(half_spec, outs, me)


def print_kernel(index_ref, dose_ref, own_ref, other_ref, printed_ref):
    core = index_ref[2]
    cols = own_ref.shape[0]
    for focus, light_ref in ((core, own_ref), (1 - core, other_ref)):
        for start in range(0, cols, 128):
            light = light_ref[start : start + 128].astype(FLOAT).T
            for dose in range(dose_ref.shape[0]):
                level = jnp.tanh(0.5 * STEEPNESS * (dose_ref[dose] * light - THRESHOLD))
                printed_ref[focus, dose, :, start : start + 128] = 0.5 * level + 0.5


def body(kern_size, slab_size, mask_params, target_bits, kernels, weights, dose_factors):
    rows, cols = mask_params.shape
    freqs = kernels.shape[2]
    assert kernels.shape[0] == 1 and kern_size % FOCI == 0
    count = kern_size // FOCI
    wide = FOCI * cols
    sizes = {"kern": kern_size, "slab": slab_size}
    slab, kern = lax.axis_index("slab"), lax.axis_index("kern")
    rounds = plan_rounds(sizes)
    me = jnp.int32(0)
    for axis, bit in [("kern", 0)] + rounds[0]:
        me = 2 * me + (((kern if axis == "kern" else slab) >> bit) & 1)
    index = jnp.stack([slab, kern // FOCI, kern % FOCI, me]).astype(jnp.int32)
    tables = trig_tables(rows * slab_size, freqs)
    rows_all = jnp.asarray(row_blocks(tables, slab_size))
    cols_all = jnp.asarray(col_blocks(tables, count))

    smem = pl.BlockSpec(memory_space=pltpu.SMEM)
    vmem = pl.BlockSpec(memory_space=pltpu.VMEM)
    anywhere = pl.BlockSpec(memory_space=pl.ANY)
    hbm = pl.BlockSpec(memory_space=pltpu.HBM)
    compiler_params = pltpu.CompilerParams(vmem_limit_bytes=VMEM_LIMIT)
    members = 1 << len(rounds[0])
    parts_out = [jax.ShapeDtypeStruct((freqs // 4 // members, 2 * freqs + EXTRA), HALF)] * (2 * members)
    rows_n_like = ((2 * freqs + EXTRA, 2 * rows), HALF)
    rows_t_like = ((2 * rows, 2 * freqs + EXTRA), HALF)
    cols_n_like = ((freqs, 2 * wide), HALF)
    cols_t_like = ((wide, 2 * freqs), HALF)
    spec_like = ((freqs, 2 * freqs), HALF)
    half_like = ((freqs // 2, 2 * freqs + EXTRA), HALF)
    raw_rows_like = ((2, rows, freqs), FLOAT)
    dma = pltpu.SemaphoreType.DMA

    cols_p_like = ((freqs + 2 * BLOCK, wide), HALF)
    table_likes = [rows_n_like, rows_t_like, cols_n_like, cols_t_like, cols_p_like, ((wide, rows), FLOAT)]
    rows_n, rows_t, cols_n, cols_t, cols_p, target = pl.pallas_call(
        table_kernel,
        out_shape=[jax.ShapeDtypeStruct(*like) for like in table_likes],
        in_specs=[smem, hbm, hbm, anywhere],
        out_specs=[vmem] * 6,
        scratch_shapes=[
            pltpu.VMEM(*raw_rows_like),
            pltpu.VMEM((2, freqs, wide), FLOAT),
            pltpu.VMEM((rows, wide), jnp.int32),
            dma((3,)),
        ],
        compiler_params=pltpu.CompilerParams(vmem_limit_bytes=60 * 1024 * 1024),
        name="make_tables",
    )(index, rows_all, cols_all, target_bits)
    made = (rows_n, rows_t, cols_n, cols_t, cols_p)

    scaled = jnp.swapaxes(kernels * jnp.sqrt(weights)[:, None, None, None], 2, 3).astype(HALF)
    params, scaled = tied(mask_params, scaled)
    begun = [scaled]
    for bits in reversed(rounds[1:]):
        value = begun[0] if len(begun) == 1 else jnp.concatenate(begun, axis=0)
        begun = [value] + [partner(value, bits, p, sizes) for p in range(1, 1 << len(bits))]
    spectra = None
    order = [pair for bits in rounds for pair in bits]

    parts = pl.pallas_call(
        first_kernel,
        out_shape=parts_out,
        in_specs=[smem, vmem, hbm, hbm],
        out_specs=[vmem] * len(parts_out),
        scratch_shapes=[
            pltpu.VMEM(*raw_rows_like),
            pltpu.VMEM((2, freqs, cols), FLOAT),
            pltpu.VMEM(*rows_t_like),
            pltpu.VMEM((freqs, 2 * cols), HALF),
            pltpu.VMEM((freqs // 2, 2 * rows), HALF),
            pltpu.VMEM(*half_like),
            dma((2,)),
        ],
        compiler_params=compiler_params,
        name="first_spectrum",
    )(index, params, rows_all, cols_all)

    printed = None
    for step in range(STEPS):
        first, last = step == 0, step == STEPS - 1
        if first:
            def to_neighbours(pieces):
                value = jnp.concatenate(pieces, axis=0)
                return [value] + [partner(value, rounds[0], p, sizes) for p in (1, 2)], made, target

            parts, (spectra, made, target) = reduce_all(parts, rounds, sizes, begun, to_neighbours)
            cut = spectra[0].shape[0] // 2
            spectra = spectra + [
                partner(spectra[2][:cut], rounds[0], 1, sizes),
                partner(spectra[1][cut:], rounds[0], 2, sizes),
            ]
        else:
            parts, _ = reduce_all(parts, rounds, sizes)
        out_shape = list(parts_out)
        if last:
            lights = [jax.ShapeDtypeStruct((cols, rows), FLOAT), jax.ShapeDtypeStruct((cols, rows), HALF)]
            out_shape = lights + out_shape
        outs = pl.pallas_call(
            functools.partial(image_kernel, last, len(parts), order),
            out_shape=out_shape,
            in_specs=[smem, smem] + [hbm] * 5 + [anywhere] * (len(parts) + len(spectra)),
            out_specs=[vmem] * len(out_shape),
            scratch_shapes=[
                pltpu.VMEM((2 * freqs, 2 * rows), HALF),
                pltpu.VMEM((2 * rows, 2 * freqs), HALF),
                pltpu.VMEM(*cols_p_like),
                pltpu.VMEM(*cols_t_like),
                pltpu.VMEM((wide, rows), FLOAT),
                pltpu.VMEM((count * slab_size,) + kernels.shape[1:2] + (kernels.shape[3], freqs), HALF),
                pltpu.VMEM(*spec_like),
                pltpu.VMEM(*spec_like),
                pltpu.VMEM((count, 2 * freqs, 2 * rows), HALF),
                pltpu.VMEM((count, wide, 2 * rows), FLOAT),
                pltpu.VMEM((count, wide, 2 * rows), HALF),
                pltpu.VMEM((freqs, 2 * rows), HALF),
                pltpu.VMEM((freqs, 2 * freqs), FLOAT),
                pltpu.VMEM(*half_like),
                pltpu.VMEM((freqs // 2, 2 * freqs), HALF),
                dma((7,)),
            ],
            compiler_params=compiler_params,
            name="image_and_back",
        )(
            index,
            dose_factors,
            made[0],
            made[1],
            *made[3:],
            target,
            *parts,
            *spectra,
        )
        parts = outs[-len(parts) :]
        if last:
            printed = pl.pallas_call(
                print_kernel,
                out_shape=jax.ShapeDtypeStruct((FOCI, dose_factors.shape[0], rows, cols), FLOAT),
                in_specs=[smem, smem, vmem, vmem],
                out_specs=vmem,
                compiler_params=compiler_params,
                name="print_resist",
            )(index, dose_factors, outs[0], partner(outs[1], [("kern", 0)], 1, sizes))
        shown = printed
        parts, printed = reduce_all(parts, rounds, sizes, None, (lambda _: shown) if last else None)
        tile = jax.ShapeDtypeStruct((rows, cols) if last else (cols, rows), FLOAT)
        common = [pltpu.VMEM(*rows_n_like), pltpu.VMEM((cols, 2 * freqs), HALF)]
        work = [pltpu.VMEM(*half_like), pltpu.VMEM((2 * freqs, rows), HALF)]
        if last:
            scratch = common + work + [dma((3,))]
        else:
            scratch = common[:1] + [pltpu.VMEM(*rows_t_like)] + common[1:]
            scratch += [pltpu.VMEM((freqs, 2 * cols), HALF)] + work
            scratch += [pltpu.VMEM((freqs // 2, 2 * rows), HALF), dma((6,))]
        outs = pl.pallas_call(
            functools.partial(update_kernel, first, last, len(parts)),
            out_shape=[tile] if last else [tile] + parts_out,
            in_specs=[smem, vmem] + [hbm] * 4 + [anywhere] * len(parts),
            out_specs=[vmem] * (1 if last else 1 + len(parts)),
            scratch_shapes=scratch,
            compiler_params=compiler_params,
            name="update",
        )(index, params, *made[:4], *parts)
        params = outs[0]
        if not last:
            parts = outs[1:]
    return (params, printed)


def solution(mesh):
    sizes = dict(mesh.shape)
    in_specs = (P("slab", "kern"), P("slab", None), P("kern", None, None, "slab"), P("kern"), P())
    out_specs = (P("slab", "kern"), P(None, None, "slab", "kern"))
    return jax.shard_map(
        functools.partial(body, sizes["kern"], sizes["slab"]),
        mesh=mesh,
        in_specs=in_specs,
        out_specs=out_specs,
        check_vma=False,
    )
```

```python
import functools

import jax
import jax.numpy as jnp
import numpy as np
from jax import lax
from jax.experimental import pallas as pl
from jax.experimental.pallas import tpu as pltpu
from jax.sharding import PartitionSpec as P

FOCI = 2
STEPS = 2
STEEPNESS = 3.0
THRESHOLD = 1.0
STEP_RATE = 0.4
BLOCK = 16
EXTRA = 128
SPREAD = 64
VMEM_LIMIT = 50 * 1024 * 1024
FLOAT = jnp.float32
HALF = jnp.bfloat16
AXES = ("kern", "slab")


def plain(left, right):
    return jnp.dot(left, right, preferred_element_type=FLOAT)


def trig_tables(pixels, freqs):
    phases = ((np.arange(freqs) - freqs // 2)[:, None] * np.arange(pixels)[None, :]) % pixels
    angles = phases.astype(np.float32) * np.float32(2.0 * np.pi / pixels)
    scale = np.float32(1.0 / np.sqrt(pixels))
    cosine = (np.cos(angles.astype(np.float64)).astype(np.float32) * scale).astype(HALF)
    sine = (np.sin(angles.astype(np.float64)).astype(np.float32) * scale).astype(HALF)
    return np.stack([cosine.astype(np.float32), sine.astype(np.float32)])


def row_blocks(tables, parts):
    _, freqs, pixels = tables.shape
    split = tables.transpose(0, 2, 1).reshape(2, parts, pixels // parts, freqs)
    return np.ascontiguousarray(split.transpose(1, 0, 2, 3))


def col_blocks(tables, parts):
    _, freqs, pixels = tables.shape
    split = tables.reshape(2, freqs, parts, pixels // parts)
    return np.ascontiguousarray(split.transpose(2, 0, 1, 3))


def flat_index(kern, slab, sizes):
    return kern * sizes["slab"] + slab


def plan_rounds(sizes):
    kern_bits = [("kern", bit) for bit in range(1, sizes["kern"].bit_length() - 1)]
    slab_bits = [("slab", bit) for bit in range(sizes["slab"].bit_length() - 1)]
    rounds = [kern_bits[:1] + slab_bits[:1], slab_bits[1:3], kern_bits[1:3], slab_bits[3:]]
    return [bits for bits in rounds if bits]


def partner(values, bits, place, sizes):
    shift = {"kern": 0, "slab": 0}
    for i, (axis, bit) in enumerate(bits):
        if (place >> (len(bits) - 1 - i)) & 1:
            shift[axis] |= 1 << bit
    mask = flat_index(shift["kern"], shift["slab"], sizes)
    total = sizes["kern"] * sizes["slab"]
    return lax.ppermute(values, AXES, [(i, i ^ mask) for i in range(total)])


def add_all(pieces):
    total = pieces[0].astype(FLOAT)
    for piece in pieces[1:]:
        total = total + piece.astype(FLOAT)
    return total.astype(HALF)


def tied(values, others):
    return lax.optimization_barrier((values, others))


def reduce_all(parts, rounds, sizes, early=None, late=None, middle=None):
    core = [("kern", 0)]
    count = len(parts) // 2
    parts = [add_all([mine, partner(other, core, 1, sizes)]) for mine, other in zip(parts[:count], parts[count:])]
    others = [partner(parts[p], rounds[0], p, sizes) for p in range(1, count)]
    if middle is not None:
        others, middle = tied(others, middle)
    total = add_all([parts[0]] + others)
    for bits in rounds[1:]:
        others = [partner(total, bits, p, sizes) for p in range(1, 1 << len(bits))]
        if late is not None and bits is rounds[1]:
            others, late = tied(others, late(early))
        total = add_all([total] + others)
    pieces = [total] + [partner(total, rounds[0], p, sizes) for p in range(1, count)]
    return pieces + [partner(piece, core, 1, sizes) for piece in pieces], late, middle


def start_together(copies, whole, sem):
    for source, target in copies:
        pltpu.make_async_copy(source, target, sem).start()
    return pltpu.make_async_copy(whole, whole, sem)


def start_all(copies, sems):
    started = [pltpu.make_async_copy(source, target, sems.at[i]) for i, (source, target) in enumerate(copies)]
    for copy in started:
        copy.start()
    return started


def piece_copies(pieces, spec, me):
    size = pieces[0].shape[0]
    return [
        (piece, spec.at[pl.ds(pl.multiple_of((place ^ me) * size, size), size)]) for place, piece in enumerate(pieces)
    ]


def iotas(rows, cols):
    shape = (rows, cols)
    return lax.broadcasted_iota(jnp.int32, shape, 0), lax.broadcasted_iota(jnp.int32, shape, 1)


def ones_where(condition):
    return jnp.where(condition, 1.0, 0.0).astype(HALF)


def anti_diagonal(size, total):
    row, lane = iotas(size, size)
    return ones_where(row + lane == total)


def spread_row(line):
    width = line.shape[1]
    row, lane = iotas(width // SPREAD, width)
    masked = jnp.where(lane // SPREAD == row, line, 0.0).astype(HALF)
    row, lane = iotas(width, EXTRA)
    return plain(masked, ones_where(lane == row % SPREAD + SPREAD))


def collect_rows(extra, width):
    row, lane = iotas(EXTRA, width)
    wide = plain(extra, ones_where(row == lane % SPREAD + SPREAD))
    row, lane = iotas(extra.shape[0], width)
    return jnp.where(lane // SPREAD == row, wide, 0.0)


def write_blocks(source, outs, me):
    for place, out in enumerate(outs):
        size = out.shape[0]
        out[...] = source[pl.ds(pl.multiple_of((place ^ me) * size, size), size)].astype(HALF)


def spectrum_of(mask_low, rows_t, cols_ref, col_spec, total):
    cols, rows = mask_low.shape
    half = total.shape[0]
    width = 4 * half
    col_spec[:, :rows] = plain(cols_ref[half:, :cols], mask_low).astype(HALF)
    col_spec[:, rows:] = (-plain(cols_ref[half:, cols:], mask_low)).astype(HALF)
    edge_re = plain(cols_ref[:BLOCK, :cols], mask_low).astype(HALF)
    edge_im = (-plain(cols_ref[:BLOCK, cols:], mask_low)).astype(HALF)
    edge = plain(edge_re, rows_t[:rows, :width]) + plain(edge_im, rows_t[rows:, :width])
    total[:, :width] = plain(col_spec[...], rows_t[:, :width]).astype(HALF)
    extra = plain(col_spec[...], rows_t[:, width:])
    spread = spread_row(edge[:1])
    count = spread.shape[0]
    total[:count, width:] = (extra[:count] + spread).astype(HALF)
    total[count:, width:] = extra[count:].astype(HALF)


def fill_rows_t(raw, rows_t):
    rows, freqs = raw.shape[1:]
    rows_t[:rows, :freqs] = raw[0].astype(HALF)
    rows_t[:rows, freqs : 2 * freqs] = (-raw[1]).astype(HALF)
    rows_t[rows:, :freqs] = raw[1].astype(HALF)
    rows_t[rows:, freqs : 2 * freqs] = raw[0].astype(HALF)
    lane = iotas(rows, EXTRA)[1]
    cosine, sine = raw[0, :, :1], -raw[1, :, :1]
    zero = jnp.zeros((rows, EXTRA), FLOAT)
    rows_t[:rows, 2 * freqs :] = jnp.where(lane == 0, cosine, jnp.where(lane == 1, -sine, zero)).astype(HALF)
    rows_t[rows:, 2 * freqs :] = jnp.where(lane == 0, sine, jnp.where(lane == 1, cosine, zero)).astype(HALF)


def first_kernel(index_ref, params_ref, rows_all, cols_all, *rest):
    outs, scratch = rest[:-7], rest[-7:]
    raw_rows, raw_cols, rows_t, cols_ref, col_spec, total, sems = scratch
    slab, pair, core, me = (index_ref[i] for i in range(4))
    cols = params_ref.shape[1]
    own = pl.ds(pl.multiple_of(core * cols, cols), cols)
    waits = start_all([(cols_all.at[pair, :, :, own], raw_cols), (rows_all.at[slab], raw_rows)], sems)
    mask_low = jnp.tanh(params_ref[...]).T.astype(HALF)
    waits[0].wait()
    cols_ref[:, :cols] = raw_cols[0].astype(HALF)
    cols_ref[:, cols:] = raw_cols[1].astype(HALF)
    waits[1].wait()
    fill_rows_t(raw_rows, rows_t)
    spectrum_of(mask_low, rows_t, cols_ref, col_spec, total)
    write_blocks(total, outs, me)


def table_kernel(index_ref, rows_all, cols_all, target_all, *rest):
    rows_n, rows_t, cols_n, cols_t, cols_p, target_ref, raw_rows, raw_cols, raw_target, sems = rest
    slab, pair = index_ref[0], index_ref[1]
    rows, freqs = raw_rows.shape[1:]
    wide = raw_cols.shape[2]
    here = pl.ds(pl.multiple_of(pair * wide, wide), wide)
    waits = start_all(
        [(rows_all.at[slab], raw_rows), (cols_all.at[pair], raw_cols), (target_all.at[:, here], raw_target)], sems
    )
    waits[0].wait()
    fill_rows_t(raw_rows, rows_t)
    cosine, sine = raw_rows[0].T, raw_rows[1].T
    rows_n[:freqs, :rows] = cosine.astype(HALF)
    rows_n[:freqs, rows:] = sine.astype(HALF)
    rows_n[freqs : 2 * freqs, :rows] = (-sine).astype(HALF)
    rows_n[freqs : 2 * freqs, rows:] = cosine.astype(HALF)
    line = iotas(EXTRA, rows)[0]
    first, second = cosine[:1], -sine[:1]
    zero = jnp.zeros((EXTRA, rows), FLOAT)
    rows_n[2 * freqs :, :rows] = jnp.where(line == 0, first, jnp.where(line == 1, -second, zero)).astype(HALF)
    rows_n[2 * freqs :, rows:] = jnp.where(line == 0, second, jnp.where(line == 1, first, zero)).astype(HALF)
    waits[1].wait()
    half = freqs // 2
    line = iotas(BLOCK, wide)[0]
    for part, sign in ((0, 1.0), (1, -1.0)):
        start = part * (half + BLOCK)
        cols_p[start : start + half] = raw_cols[part, half:].astype(HALF)
        edge = jnp.where(line == 0, sign * raw_cols[part, :1], 0.0)
        cols_p[start + half : start + half + BLOCK] = edge.astype(HALF)
    for part in range(2):
        cols_n[:, part * wide : (part + 1) * wide] = raw_cols[part].astype(HALF)
        for start in range(0, wide, 128):
            some = raw_cols[part, :, start : start + 128].T
            cols_t[start : start + 128, part * freqs : (part + 1) * freqs] = some.astype(HALF)
    waits[2].wait()
    for start in range(0, wide, 128):
        target_ref[start : start + 128] = (2 * raw_target[:, start : start + 128] - 1).astype(FLOAT).T


def update_kernel(first, last, count, index_ref, params_ref, rows_n, rows_t, cols_n, cols_t, *rest):
    pieces, rest = rest[:count], rest[count:]
    if last:
        new_ref, rows_v, cols_v, spec, back, sems = rest
    else:
        new_ref, outs, scratch = rest[0], rest[1 : 1 + count], rest[1 + count :]
        rows_v, rows_t_v, cols_v, cols_n_v, spec, back, col_spec, sems = scratch
    core, me = index_ref[2], index_ref[3]
    params = params_ref[...].T if first else params_ref[...]
    cols, rows = params.shape
    half = spec.shape[0]
    freqs = 2 * half
    here = pl.ds(pl.multiple_of(core * cols, cols), cols)
    arrival = start_together(piece_copies(pieces, spec, me), spec, sems.at[0])
    copies = [(rows_n, rows_v), (cols_t.at[here], cols_v)]
    if not last:
        wide = cols_n.shape[1] // 2
        copies += [
            (rows_t, rows_t_v),
            (cols_n.at[:, here], cols_n_v.at[:, :cols]),
            (cols_n.at[:, pl.ds(pl.multiple_of(wide + core * cols, cols), cols)], cols_n_v.at[:, cols:]),
        ]
    waits = start_all(copies, sems.at[1:])
    back[...] = jnp.zeros_like(back)
    arrival.wait()
    waits[0].wait()
    result = plain(spec[...], rows_v[...])
    back[half:freqs] = result[:, :rows].astype(HALF)
    back[freqs + half :] = (-result[:, rows:]).astype(HALF)
    edge = collect_rows(spec[: 2 * freqs // SPREAD, 2 * freqs :], 2 * freqs).astype(HALF)
    edge = jnp.sum(plain(edge, rows_v[: 2 * freqs]), axis=0, keepdims=True)
    line = iotas(BLOCK, rows)[0]
    back[:BLOCK] = jnp.where(line == 0, edge[:, :rows], 0.0).astype(HALF)
    back[freqs : freqs + BLOCK] = jnp.where(line == 0, -edge[:, rows:], 0.0).astype(HALF)
    waits[1].wait()
    gradient = plain(cols_v[...], back[...])
    mask = jnp.tanh(params)
    params = params - STEP_RATE * gradient * (1.0 - mask * mask)
    if last:
        new_ref[...] = params.T
    else:
        new_ref[...] = params
        for i in range(2, len(waits)):
            waits[i].wait()
        spectrum_of(jnp.tanh(params).astype(HALF), rows_t_v, cols_n_v, col_spec, spec)
        write_blocks(spec, outs, me)


def loop(count, step):
    if count <= 2:
        for i in range(count):
            step(i)
    else:
        pl.loop(0, count)(step)


def image_kernel(last, parts, order, index_ref, dose_ref, rows_n, rows_t, cols_t, cols_p, target_all, *rest):
    spec_pieces, rest = rest[:parts], rest[parts:]
    outs = rest[-16 - parts - (2 if last else 0) : -16]
    spectra = rest[: -16 - len(outs)]
    scratch = rest[-16:]
    rows_v, rows_t_v, cols_v, cols_t_v, target_ref, kern_ref, spec = scratch[:7]
    filtered, sides, fields, cotangent, back, total, half_spec, turned, sems = scratch[7:]
    if last:
        own_light, other_light, outs = outs[0], outs[1], outs[2:]
    slab, core, me = index_ref[0], index_ref[2], index_ref[3]
    wide, rows = target_ref.shape
    count, freqs = fields.shape[0], spec.shape[0]
    width = kern_ref.shape[2]

    def kernel_rows(k, start):
        part = slab ^ (start // width)
        place = 0
        for axis, bit in order:
            place = 2 * place + (((k >> (bit - 1)) & 1) if axis == "kern" else ((part >> bit) & 1))
        here = pl.ds(start % width, BLOCK)
        return kern_ref[place, 0, here].astype(FLOAT), kern_ref[place, 1, here].astype(FLOAT)

    arrival = start_together(piece_copies(spec_pieces, half_spec, me), half_spec, sems.at[0])
    copies = []
    filled = 0
    for piece in spectra:
        copies.append((piece, kern_ref.at[filled : filled + piece.shape[0]]))
        filled += piece.shape[0]
    spectra_here = start_together(copies, kern_ref, sems.at[1])
    copies = [(rows_n.at[: 2 * freqs], rows_v), (cols_t, cols_t_v), (target_all, target_ref), (cols_p, cols_v), (rows_t.at[:, : 2 * freqs], rows_t_v)]
    waits = start_all(copies, sems.at[2:])
    if count > 2:
        total[...] = jnp.zeros_like(total)
    arrival.wait()

    half = freqs // 2
    mirror = anti_diagonal(freqs, freqs)
    flip = anti_diagonal(half, half)
    spec[half:] = half_spec[:, : 2 * freqs]
    lane = iotas(half, freqs)[1]
    past_re = half_spec[:, 2 * freqs : 2 * freqs + EXTRA][:, :1].astype(FLOAT)
    past_im = half_spec[:, 2 * freqs : 2 * freqs + EXTRA][:, 1:2].astype(FLOAT)
    turned[:, :freqs] = jnp.where(lane == 0, past_re, plain(half_spec[:, :freqs], mirror)).astype(HALF)
    turned[:, freqs:] = jnp.where(lane == 0, -past_im, -plain(half_spec[:, freqs : 2 * freqs], mirror)).astype(HALF)
    edge = collect_rows(half_spec[: 2 * freqs // SPREAD, 2 * freqs :], 2 * freqs)
    edge = jnp.sum(edge, axis=0, keepdims=True)
    line = iotas(half, 2 * freqs)[0]
    spec[:half] = jnp.where(line == 0, edge, plain(flip, turned[...])).astype(HALF)
    spectra_here.wait()
    waits[0].wait()

    def make_rows(k):
        for start in range(0, freqs, BLOCK):
            here = pl.ds(start, BLOCK)
            spec_re, spec_im = spec[here, :freqs].astype(FLOAT), spec[here, freqs:].astype(FLOAT)
            real, imag = kernel_rows(k, start)
            filtered[here, :freqs] = (real * spec_re - imag * spec_im).astype(HALF)
            filtered[here, freqs:] = (real * spec_im + imag * spec_re).astype(HALF)
        result = plain(filtered[...], rows_v[...])
        sides[k, :freqs] = result.astype(HALF)
        sides[k, freqs:, :rows] = (-result[:, rows:]).astype(HALF)
        sides[k, freqs:, rows:] = result[:, :rows].astype(HALF)

    loop(count, make_rows)

    waits[1].wait()

    def make_fields(k):
        fields[k] = plain(cols_t_v[...], sides[k])

    loop(count, make_fields)

    waits[2].wait()
    chunk = 32

    @pl.loop(0, wide // chunk, unroll=4)
    def make_sens(i):
        here = pl.ds(pl.multiple_of(i * chunk, chunk), chunk)
        target = target_ref[here]
        light = None
        for k in range(count):
            real, imag = fields[k, here, :rows], fields[k, here, rows:]
            power = real * real + imag * imag
            light = power if light is None else light + power
        if last:
            side = (i * chunk) // (wide // 2)
            place = pl.ds(pl.multiple_of(i * chunk - side * (wide // 2), chunk), chunk)

            @pl.when(side == core)
            def _():
                own_light[place] = light

            @pl.when(side != core)
            def _():
                other_light[place] = light.astype(HALF)

        sens = None
        for dose in range(dose_ref.shape[0]):
            factor = dose_ref[dose]
            level = jnp.tanh((0.5 * STEEPNESS * factor) * light - 0.5 * STEEPNESS * THRESHOLD)
            slope = (level - target) * (1.0 - level * level) * (0.25 * STEEPNESS * factor)
            sens = slope if sens is None else sens + slope
        for k in range(count):
            real = sens * fields[k, here, :rows]
            imag = sens * fields[k, here, rows:]
            cotangent[k, here, :rows] = real.astype(HALF)
            cotangent[k, here, rows:] = imag.astype(HALF)

    waits[3].wait()
    waits[4].wait()

    def go_back(k):
        both = plain(cols_v[...], cotangent[k])
        size = half + BLOCK
        real_c, imag_c = both[:size, :rows], both[:size, rows:]
        real_s, imag_s = both[size:, :rows], both[size:, rows:]
        back[half:, :rows] = (real_c + imag_s)[:half].astype(HALF)
        back[half:, rows:] = (imag_c - real_s)[:half].astype(HALF)
        low_re, low_im = real_c - imag_s, imag_c + real_s
        turned[:, :rows] = low_re[:half].astype(HALF)
        turned[:, rows : 2 * rows] = low_im[:half].astype(HALF)
        low = plain(flip, turned[:, : 2 * rows])
        line = iotas(half, rows)[0]
        back[:half, :rows] = jnp.where(line == 0, low_re[half : half + 1], low[:, :rows]).astype(HALF)
        back[:half, rows:] = jnp.where(line == 0, low_im[half : half + 1], low[:, rows:]).astype(HALF)
        slopes = filtered_slopes(back, rows_t_v)
        for start in range(0, freqs, BLOCK):
            here = pl.ds(start, BLOCK)
            real, imag = kernel_rows(k, start)
            slope_re, slope_im = slopes(start)
            total_re = real * slope_re + imag * slope_im
            total_im = real * slope_im - imag * slope_re
            if count > 2 or k > 0:
                total_re += total[here, :freqs]
                total_im += total[here, freqs:]
            total[here, :freqs] = total_re
            total[here, freqs:] = total_im

    def filtered_slopes(back, table):
        step = min(256, freqs)
        made = {}

        def at(start):
            first = start // step * step
            if first not in made:
                made.clear()
                made[first] = plain(back[first : first + step], table[...])
            part = made[first][start - first : start - first + BLOCK]
            return part[:, :freqs], part[:, freqs:]

        return at

    loop(count, go_back)

    turned[...] = plain(flip, total[:half].astype(HALF)).astype(HALF)
    half_spec[:, :freqs] = (total[half:, :freqs] + plain(turned[:, :freqs], mirror)).astype(HALF)
    half_spec[:, freqs : 2 * freqs] = (total[half:, freqs:] - plain(turned[:, freqs:], mirror)).astype(HALF)
    past_re = turned[:, :EXTRA][:, :1].astype(FLOAT)
    past_im = turned[:, freqs : freqs + EXTRA][:, :1].astype(FLOAT)
    lane = iotas(half, EXTRA)[1]
    extra = jnp.where(lane == 0, past_re, jnp.where(lane == 1, -past_im, 0.0))
    spread = spread_row(total[:1])
    lines = spread.shape[0]
    half_spec[:lines, 2 * freqs :] = (extra[:lines] + spread).astype(HALF)
    half_spec[lines:, 2 * freqs :] = extra[lines:].astype(HALF)
    write_blocks(half_spec, outs, me)


def print_kernel(index_ref, dose_ref, own_ref, other_ref, printed_ref):
    core = index_ref[2]
    cols = own_ref.shape[0]
    for focus, light_ref in ((core, own_ref), (1 - core, other_ref)):
        for start in range(0, cols, 128):
            light = light_ref[start : start + 128].astype(FLOAT).T
            for dose in range(dose_ref.shape[0]):
                level = jnp.tanh(0.5 * STEEPNESS * (dose_ref[dose] * light - THRESHOLD))
                printed_ref[focus, dose, :, start : start + 128] = 0.5 * level + 0.5


def body(kern_size, slab_size, mask_params, target_bits, kernels, weights, dose_factors):
    rows, cols = mask_params.shape
    freqs = kernels.shape[2]
    assert kernels.shape[0] == 1 and kern_size % FOCI == 0
    count = kern_size // FOCI
    wide = FOCI * cols
    sizes = {"kern": kern_size, "slab": slab_size}
    slab, kern = lax.axis_index("slab"), lax.axis_index("kern")
    rounds = plan_rounds(sizes)
    me = jnp.int32(0)
    for axis, bit in [("kern", 0)] + rounds[0]:
        me = 2 * me + (((kern if axis == "kern" else slab) >> bit) & 1)
    index = jnp.stack([slab, kern // FOCI, kern % FOCI, me]).astype(jnp.int32)
    tables = trig_tables(rows * slab_size, freqs)
    rows_all = jnp.asarray(row_blocks(tables, slab_size))
    cols_all = jnp.asarray(col_blocks(tables, count))

    smem = pl.BlockSpec(memory_space=pltpu.SMEM)
    vmem = pl.BlockSpec(memory_space=pltpu.VMEM)
    anywhere = pl.BlockSpec(memory_space=pl.ANY)
    hbm = pl.BlockSpec(memory_space=pltpu.HBM)
    compiler_params = pltpu.CompilerParams(vmem_limit_bytes=VMEM_LIMIT)
    members = 1 << len(rounds[0])
    parts_out = [jax.ShapeDtypeStruct((freqs // 4 // members, 2 * freqs + EXTRA), HALF)] * (2 * members)
    rows_n_like = ((2 * freqs + EXTRA, 2 * rows), HALF)
    rows_t_like = ((2 * rows, 2 * freqs + EXTRA), HALF)
    cols_n_like = ((freqs, 2 * wide), HALF)
    cols_t_like = ((wide, 2 * freqs), HALF)
    spec_like = ((freqs, 2 * freqs), HALF)
    half_like = ((freqs // 2, 2 * freqs + EXTRA), HALF)
    raw_rows_like = ((2, rows, freqs), FLOAT)
    dma = pltpu.SemaphoreType.DMA

    cols_p_like = ((freqs + 2 * BLOCK, wide), HALF)
    table_likes = [rows_n_like, rows_t_like, cols_n_like, cols_t_like, cols_p_like, ((wide, rows), FLOAT)]
    rows_n, rows_t, cols_n, cols_t, cols_p, target = pl.pallas_call(
        table_kernel,
        out_shape=[jax.ShapeDtypeStruct(*like) for like in table_likes],
        in_specs=[smem, hbm, hbm, anywhere],
        out_specs=[vmem] * 6,
        scratch_shapes=[
            pltpu.VMEM(*raw_rows_like),
            pltpu.VMEM((2, freqs, wide), FLOAT),
            pltpu.VMEM((rows, wide), jnp.int32),
            dma((3,)),
        ],
        compiler_params=pltpu.CompilerParams(vmem_limit_bytes=60 * 1024 * 1024),
        name="make_tables",
    )(index, rows_all, cols_all, target_bits)
    made = (rows_n, rows_t, cols_n, cols_t, cols_p)

    scaled = jnp.swapaxes(kernels * jnp.sqrt(weights)[:, None, None, None], 2, 3).astype(HALF)
    params, scaled = tied(mask_params, scaled)
    begun = [scaled]
    for bits in reversed(rounds[1:]):
        value = begun[0] if len(begun) == 1 else jnp.concatenate(begun, axis=0)
        begun = [value] + [partner(value, bits, p, sizes) for p in range(1, 1 << len(bits))]
    spectra = None
    order = [pair for bits in rounds for pair in bits]

    parts = pl.pallas_call(
        first_kernel,
        out_shape=parts_out,
        in_specs=[smem, vmem, hbm, hbm],
        out_specs=[vmem] * len(parts_out),
        scratch_shapes=[
            pltpu.VMEM(*raw_rows_like),
            pltpu.VMEM((2, freqs, cols), FLOAT),
            pltpu.VMEM(*rows_t_like),
            pltpu.VMEM((freqs, 2 * cols), HALF),
            pltpu.VMEM((freqs // 2, 2 * rows), HALF),
            pltpu.VMEM(*half_like),
            dma((2,)),
        ],
        compiler_params=compiler_params,
        name="first_spectrum",
    )(index, params, rows_all, cols_all)

    printed = None
    for step in range(STEPS):
        first, last = step == 0, step == STEPS - 1
        if first:
            def to_neighbours(pieces):
                value = jnp.concatenate(pieces, axis=0)
                return [value] + [partner(value, rounds[0], p, sizes) for p in (1, 2)]

            parts, spectra, (made, target) = reduce_all(
                parts, rounds, sizes, begun, to_neighbours, (made, target)
            )
            cut = spectra[0].shape[0] // 2
            spectra = spectra + [
                partner(spectra[2][:cut], rounds[0], 1, sizes),
                partner(spectra[1][cut:], rounds[0], 2, sizes),
            ]
        else:
            parts, _, _ = reduce_all(parts, rounds, sizes)
        out_shape = list(parts_out)
        if last:
            lights = [jax.ShapeDtypeStruct((cols, rows), FLOAT), jax.ShapeDtypeStruct((cols, rows), HALF)]
            out_shape = lights + out_shape
        outs = pl.pallas_call(
            functools.partial(image_kernel, last, len(parts), order),
            out_shape=out_shape,
            in_specs=[smem, smem] + [hbm] * 5 + [anywhere] * (len(parts) + len(spectra)),
            out_specs=[vmem] * len(out_shape),
            scratch_shapes=[
                pltpu.VMEM((2 * freqs, 2 * rows), HALF),
                pltpu.VMEM((2 * rows, 2 * freqs), HALF),
                pltpu.VMEM(*cols_p_like),
                pltpu.VMEM(*cols_t_like),
                pltpu.VMEM((wide, rows), FLOAT),
                pltpu.VMEM((count * slab_size,) + kernels.shape[1:2] + (kernels.shape[3], freqs), HALF),
                pltpu.VMEM(*spec_like),
                pltpu.VMEM(*spec_like),
                pltpu.VMEM((count, 2 * freqs, 2 * rows), HALF),
                pltpu.VMEM((count, wide, 2 * rows), FLOAT),
                pltpu.VMEM((count, wide, 2 * rows), HALF),
                pltpu.VMEM((freqs, 2 * rows), HALF),
                pltpu.VMEM((freqs, 2 * freqs), FLOAT),
                pltpu.VMEM(*half_like),
                pltpu.VMEM((freqs // 2, 2 * freqs), HALF),
                dma((7,)),
            ],
            compiler_params=compiler_params,
            name="image_and_back",
        )(
            index,
            dose_factors,
            made[0],
            made[1],
            *made[3:],
            target,
            *parts,
            *spectra,
        )
        parts = outs[-len(parts) :]
        if last:
            printed = pl.pallas_call(
                print_kernel,
                out_shape=jax.ShapeDtypeStruct((FOCI, dose_factors.shape[0], rows, cols), FLOAT),
                in_specs=[smem, smem, vmem, vmem],
                out_specs=vmem,
                compiler_params=compiler_params,
                name="print_resist",
            )(index, dose_factors, outs[0], partner(outs[1], [("kern", 0)], 1, sizes))
        shown = printed
        parts, printed, _ = reduce_all(parts, rounds, sizes, None, (lambda _: shown) if last else None)
        tile = jax.ShapeDtypeStruct((rows, cols) if last else (cols, rows), FLOAT)
        common = [pltpu.VMEM(*rows_n_like), pltpu.VMEM((cols, 2 * freqs), HALF)]
        work = [pltpu.VMEM(*half_like), pltpu.VMEM((2 * freqs, rows), HALF)]
        if last:
            scratch = common + work + [dma((3,))]
        else:
            scratch = common[:1] + [pltpu.VMEM(*rows_t_like)] + common[1:]
            scratch += [pltpu.VMEM((freqs, 2 * cols), HALF)] + work
            scratch += [pltpu.VMEM((freqs // 2, 2 * rows), HALF), dma((6,))]
        outs = pl.pallas_call(
            functools.partial(update_kernel, first, last, len(parts)),
            out_shape=[tile] if last else [tile] + parts_out,
            in_specs=[smem, vmem] + [hbm] * 4 + [anywhere] * len(parts),
            out_specs=[vmem] * (1 if last else 1 + len(parts)),
            scratch_shapes=scratch,
            compiler_params=compiler_params,
            name="update",
        )(index, params, *made[:4], *parts)
        params = outs[0]
        if not last:
            parts = outs[1:]
    return (params, printed)


def solution(mesh):
    sizes = dict(mesh.shape)
    in_specs = (P("slab", "kern"), P("slab", None), P("kern", None, None, "slab"), P("kern"), P())
    out_specs = (P("slab", "kern"), P(None, None, "slab", "kern"))
    return jax.shard_map(
        functools.partial(body, sizes["kern"], sizes["slab"]),
        mesh=mesh,
        in_specs=in_specs,
        out_specs=out_specs,
        check_vma=False,
    )
```
